32 devices in a mesh: dp: 4 (over y, x), ctx: 8 (over z, core).
Axes of the slice: x: 2, y: 2, z: 4, core: 2. Of those that a mesh axis runs over, the one named last changes fastest.
Arguments:
- tokens: bfloat16 [4, 1024, 2048], P('dp', 'ctx'), may hold values from -6 to 6
- cotangent: bfloat16 [4, 1024, 2048], P('dp', 'ctx'), may hold values from -6 to 6
- group_ids: int32 [4], P('dp'), may hold values from 0 to 3, as said below
- group_scale: float32 [4], replicated, may hold values from 0.5 to 2
- attn_gain: bfloat16 [2048], P(('dp', 'ctx')), may hold values from 0.099609375 to 1.8984375
- w_qkv: bfloat16 [2048, 6144], P(('dp', 'ctx')), may hold values from -0.125 to 0.125
- conv_weight: bfloat16 [4, 6144], P(None, ('dp', 'ctx')), may hold values from -3 to 3
- w_beta: bfloat16 [2048, 16], P(('dp', 'ctx')), may hold values from -0.25 to 0.25
- w_gate_o: bfloat16 [2048, 2048], P(('dp', 'ctx')), may hold values from -0.125 to 0.125
- norm_gain_o: bfloat16 [128], P(('dp', 'ctx')), may hold values from 0.099609375 to 1.8984375
- w_out: bfloat16 [2048, 2048], P(('dp', 'ctx')), may hold values from -0.125 to 0.125
- ffn_gain: bfloat16 [2048], P(('dp', 'ctx')), may hold values from 0.099609375 to 1.8984375
- w_gate_up: bfloat16 [2048, 11264], P(('dp', 'ctx')), may hold values from -0.125 to 0.125
- w_down: bfloat16 [5632, 2048], P(('dp', 'ctx')), may hold values from -0.078125 to 0.078125
Outputs:
- block_out: bfloat16 [4, 1024, 2048], P('dp', 'ctx')
- d_tokens: float32 [4, 1024, 2048], P('dp', 'ctx')
- g_attn_gain: float32 [2048], P(('dp', 'ctx'))
- g_w_qkv: float32 [2048, 6144], P(('dp', 'ctx'))
- g_conv_weight: float32 [4, 6144], P(None, ('dp', 'ctx'))
- g_w_beta: float32 [2048, 16], P(('dp', 'ctx'))
- g_w_gate_o: float32 [2048, 2048], P(('dp', 'ctx'))
- g_norm_gain_o: float32 [128], P(('dp', 'ctx'))
- g_w_out: float32 [2048, 2048], P(('dp', 'ctx'))
- g_ffn_gain: float32 [2048], P(('dp', 'ctx'))
- g_w_gate_up: float32 [2048, 11264], P(('dp', 'ctx'))
- g_w_down: float32 [5632, 2048], P(('dp', 'ctx'))
The draws below stay inside these ranges and needn't reach their ends.
Inputs may be any that keep to these rules, and one draw needn't show every extreme that they name: `group_ids`: every group is named by exactly 1 sequence.
All inputs are finite; a program needn't handle non-finite values.
Results may differ from the reference program's by a relative error of at most 0.019.
The reference program's roundings to bfloat16 on the way count: a program that leaves them out, or rounds other values in their place, can miss the bound.
Values may be sent and summed in bfloat16 or wider, within the bound.
No kernel may reach another device: no remote copies, remote signals or barrier semaphores. Data moves between devices by JAX's collectives and lax.ppermute only.
A program may use at most 576 MiB of HBM per device.

```python
import math
import jax
import jax.numpy as jnp
from jax import lax

D = 2048
H = 16
HD = 128
FF = 5632
CONV = 4
SPAN = 64
GROUPS = 4
SEQUENCES = 4
LENGTH = 1024


def draw_group_ids(key, part):
    key = jax.random.fold_in(key, 5)
    order = jax.random.permutation(key, SEQUENCES)
    return (order % GROUPS).astype(jnp.int32)


def shard_levels(key, shape, cuts, smallest, high):
    def one(position, blocks):
        draws = jax.random.uniform(jax.random.fold_in(jax.random.fold_in(key, 6), position), (blocks,), jnp.float32, smallest / len(cuts), high / len(cuts))
        return jnp.repeat(jnp.exp(draws), shape[position] // blocks).reshape((-1,) + (1,) * (len(shape) - position - 1))

    gain = one(*cuts[0])
    for cut in cuts[1:]:
        gain = gain * one(*cut)
    return gain


def noise(stream_key, shape, scale, reach, cuts=(), kind=jnp.bfloat16):
    loudness = shard_levels(stream_key, shape, cuts, -0.22, 0.18) if cuts else 1.0
    array = jax.random.normal(stream_key, shape, jnp.float32) * scale * loudness
    return jnp.minimum(jnp.maximum(array, -reach), reach).astype(kind)


def setup_inputs(seed: int = 0) -> dict:
    seeds = jax.random.split(jax.random.key(seed), 15)
    tokens = noise(seeds[0], (SEQUENCES, LENGTH, D), 1.0, 6.0, ((0, 4), (1, 8)))
    cotangent = noise(seeds[1], (SEQUENCES, LENGTH, D), 1.0, 6.0, ((0, 4), (1, 8)))
    group_ids = draw_group_ids(jax.random.fold_in(seeds[14], 71), 0)
    group_scale = jnp.clip(jnp.exp(jax.random.uniform(seeds[3], (GROUPS,), jnp.float32, math.log(0.5), math.log(2.0))), 0.5, 2.0)
    attn_gain = jnp.clip(1.0 + 0.18 * jax.random.normal(seeds[4], (D,), jnp.float32), 0.099609375, 1.8984375).astype(jnp.bfloat16)
    w_qkv = noise(seeds[5], (D, 3 * D), D ** -0.5, 0.125, ((0, 32),))
    conv_weight = noise(seeds[6], (CONV, 3 * D), CONV ** -0.5, 3.0, ((1, 32),))
    w_beta = noise(seeds[7], (D, H), (D // 4) ** -0.5, 0.25, ((0, 32),))
    w_gate_o = noise(seeds[8], (D, D), D ** -0.5, 0.125, ((0, 32),))
    norm_gain_o = jnp.clip(1.0 + 0.18 * jax.random.normal(seeds[9], (HD,), jnp.float32), 0.099609375, 1.8984375).astype(jnp.bfloat16)
    w_out = noise(seeds[10], (D, D), D ** -0.5, 0.125, ((0, 32),))
    ffn_gain = jnp.clip(1.0 + 0.18 * jax.random.normal(seeds[11], (D,), jnp.float32), 0.099609375, 1.8984375).astype(jnp.bfloat16)
    w_gate_up = noise(seeds[12], (D, 2 * FF), D ** -0.5, 0.125, ((0, 32),))
    w_down = noise(seeds[13], (FF, D), FF ** -0.5, 0.078125, ((0, 32),))
    return dict(tokens=tokens, cotangent=cotangent, group_ids=group_ids, group_scale=group_scale, attn_gain=attn_gain, w_qkv=w_qkv, conv_weight=conv_weight, w_beta=w_beta, w_gate_o=w_gate_o, norm_gain_o=norm_gain_o, w_out=w_out, ffn_gain=ffn_gain, w_gate_up=w_gate_up, w_down=w_down)


EPS = 1e-05
HIGH = lax.Precision.HIGHEST

@jax.custom_vjp
def low(v):
    return lax.optimization_barrier(v.astype(jnp.bfloat16)).astype(jnp.float32)

@jax.custom_vjp
def low_back(v):
    return v

def low_keep(v):
    return (low(v), None)

def low_pass(kept, grad):
    return (grad,)

def back_keep(v):
    return (v, None)

def back_low(kept, grad):
    return (low(grad),)
low.defvjp(low_keep, low_pass)
low_back.defvjp(back_keep, back_low)

def matmul_hi(left_op, right_op):
    return jnp.einsum('...ij,...jk->...ik', left_op, right_op, precision=HIGH, preferred_element_type=jnp.float32)

def flip(matrix):
    return jnp.swapaxes(matrix, -1, -2)

def norm_rows(values, gain_vec):
    inv_rms = lax.rsqrt(lax.optimization_barrier(jnp.mean(values * values, axis=-1, keepdims=True)) + EPS)
    return values * inv_rms * gain_vec

def mixer_inputs(extended, conv_w, beta_logit):
    extent = extended.shape[1] - CONV + 1
    summed = conv_w[0] * extended[:, 0:extent]
    for offset in range(1, CONV):
        summed = summed + conv_w[offset] * extended[:, offset:offset + extent]
    mixture = jax.nn.silu(summed)
    batches = mixture.shape[0]
    head_count = beta_logit.shape[-1]
    head_size = mixture.shape[-1] // (3 * head_count)
    pieces = jnp.transpose(mixture.reshape(batches, extent, 3, head_count, head_size), (2, 0, 3, 1, 4))
    k_raw = pieces[1]
    k_rows = k_raw * lax.rsqrt(lax.optimization_barrier(jnp.sum(k_raw * k_raw, axis=-1, keepdims=True)) + 1e-06)
    beta_rows = jnp.transpose(jax.nn.sigmoid(beta_logit), (0, 2, 1))
    return (pieces[0], k_rows, pieces[2], beta_rows)

def lower_inverse(strict_part):
    extent = strict_part.shape[-1]
    negated = -strict_part
    result = jnp.eye(extent, dtype=jnp.float32) + negated
    powered = negated
    for _ in range((extent - 1).bit_length() - 1):
        powered = matmul_hi(powered, powered)
        result = result + matmul_hi(result, powered)
    return result

def span_masks(extent):
    row_ids = lax.broadcasted_iota(jnp.int32, (extent, extent), 0)
    col_ids = lax.broadcasted_iota(jnp.int32, (extent, extent), 1)
    return (row_ids > col_ids, row_ids >= col_ids)

def span_update(state_now, k_rows, v_rows, beta_rows):
    strict, _ = span_masks(k_rows.shape[-2])
    k_gram = matmul_hi(k_rows, flip(k_rows))
    strict_part = jnp.where(strict, beta_rows[..., :, None] * k_gram, 0.0)
    inverse = lower_inverse(strict_part)
    weighted_k = matmul_hi(inverse, beta_rows[..., None] * k_rows)
    return matmul_hi(inverse, beta_rows[..., None] * v_rows) - matmul_hi(weighted_k, state_now)

def span_step(state_now, block_in):
    q_rows, k_rows, v_rows, beta_rows = block_in
    update = span_update(state_now, k_rows, v_rows, beta_rows)
    _, causal = span_masks(k_rows.shape[-2])
    scores = jnp.where(causal, matmul_hi(q_rows, flip(k_rows)), 0.0)
    output = matmul_hi(q_rows, state_now) + matmul_hi(scores, update)
    return (state_now + matmul_hi(flip(k_rows), update), output)

def to_blocks(rows_in):
    leading = rows_in.shape[:-2]
    extent, trailing = rows_in.shape[-2:]
    pieces = rows_in.reshape(leading + (extent // SPAN, SPAN, trailing))
    return jnp.moveaxis(pieces, -3, 0)

def from_blocks(blocks):
    moved = jnp.moveaxis(blocks, 0, -3)
    leading = moved.shape[:-3]
    return moved.reshape(leading + (moved.shape[-3] * moved.shape[-2], moved.shape[-1]))

def run_core(q_rows, k_rows, v_rows, beta_rows, state_in, stepper):
    blocks = (to_blocks(q_rows), to_blocks(k_rows), to_blocks(v_rows), to_blocks(beta_rows[..., None])[..., 0])
    final, outputs = lax.scan(stepper, state_in, blocks)
    return (from_blocks(outputs), final)

def out_gate(core_out, gate_raw, gain_vec):
    batches, head_count, extent, head_size = core_out.shape
    normed = norm_rows(core_out, gain_vec)
    normed = jnp.transpose(normed, (0, 2, 1, 3)).reshape(batches * extent, head_count * head_size)
    return normed * jax.nn.silu(gate_raw)

def swiglu(gate_up):
    midpoint = gate_up.shape[-1] // 2
    return jax.nn.silu(gate_up[:, :midpoint]) * gate_up[:, midpoint:]

def block_forward(x_rows, attn_gain, w_qkv, conv_w, w_beta, w_gate_o, gain_o, w_out, ffn_gain, w_gate_up, w_down):
    extent, model_width = x_rows.shape
    head_count = w_beta.shape[1]
    head_size = model_width // head_count
    h1_rows = low_back(low(norm_rows(x_rows, attn_gain)))
    pre_rows = low_back(low(matmul_hi(h1_rows, w_qkv)))
    beta_logit = low_back(matmul_hi(h1_rows, w_beta))
    gate_raw = low_back(matmul_hi(h1_rows, w_gate_o))
    extended = jnp.concatenate([jnp.zeros((CONV - 1, pre_rows.shape[1]), jnp.float32), pre_rows], axis=0)[None]
    q_rows, k_rows, v_rows, beta_rows = mixer_inputs(extended, conv_w, beta_logit.reshape(1, extent, head_count))
    start_state = jnp.zeros((1, head_count, head_size, head_size), jnp.float32)
    core_out, _ = run_core(q_rows, k_rows, v_rows, beta_rows, start_state, jax.checkpoint(span_step))
    y_rows = low_back(low(out_gate(core_out, gate_raw, gain_o)))
    resid = x_rows + low_back(matmul_hi(y_rows, w_out))
    h2_rows = low_back(low(norm_rows(resid, ffn_gain)))
    gate_up = low_back(matmul_hi(h2_rows, w_gate_up))
    hidden = low_back(low(swiglu(gate_up)))
    return resid + low_back(matmul_hi(hidden, w_down))

def reference(tokens, cotangent, group_ids, group_scale, attn_gain, w_qkv, conv_weight, w_beta, w_gate_o, norm_gain_o, w_out, ffn_gain, w_gate_up, w_down):
    weights = tuple((w.astype(jnp.float32) for w in (attn_gain, w_qkv, conv_weight, w_beta, w_gate_o, norm_gain_o, w_out, ffn_gain, w_gate_up, w_down)))
    matches = group_ids[:, None] == jnp.arange(GROUPS, dtype=jnp.int32)[None, :]
    seq_scale = lax.optimization_barrier(jnp.sum(jnp.where(matches, group_scale[None, :], 0.0), axis=1))

    def one_sequence(totals, inputs):
        x_seq, ct_seq, scale_seq = inputs
        out_seq, pullback = jax.vjp(block_forward, x_seq.astype(jnp.float32), *weights)
        grads = pullback(ct_seq.astype(jnp.float32) * scale_seq)
        totals = jax.tree.map(jnp.add, totals, tuple(grads[1:]))
        return (totals, (out_seq.astype(jnp.bfloat16), grads[0]))
    start = tuple((jnp.zeros_like(w) for w in weights))
    totals, (outputs, d_inputs) = lax.scan(one_sequence, start, (tokens, cotangent, seq_scale))
    return (outputs, d_inputs, totals[0], totals[1], totals[2], totals[3], totals[4], totals[5], totals[6], totals[7], totals[8], totals[9])
```

```python
import functools

import jax
import jax.numpy as jnp
from jax import lax
from jax.experimental import pallas as pl
from jax.experimental.pallas import tpu as pltpu
from jax.sharding import PartitionSpec as P

CONV = 4
HD = 128
CHUNK = 128
STEP = 256
EPS = 1e-05
KEY_EPS = 1e-06
BF = jnp.bfloat16
F32 = jnp.float32
NN = ((1,), (0,))
NT = ((1,), (1,))
TN = ((0,), (0,))


def mm(left, right, dims):
    return lax.dot_general(
        left.astype(BF), right.astype(BF), (dims, ((), ())), preferred_element_type=F32
    )


def halves(values):
    high = values.astype(BF)
    return high, (values - high.astype(F32)).astype(BF)


def mm_fine(left, right, dims):
    left_hi, left_lo = halves(left)
    right_hi, right_lo = halves(right)

    def product(a, b):
        return lax.dot_general(a, b, (dims, ((), ())), preferred_element_type=F32)

    return product(left_hi, right_hi) + (product(left_hi, right_lo) + product(left_lo, right_hi))


def sigmoid(values):
    return 1.0 / (1.0 + jnp.exp(-values))


def chunk_ids():
    row_ids = lax.broadcasted_iota(jnp.int32, (CHUNK, CHUNK), 0)
    col_ids = lax.broadcasted_iota(jnp.int32, (CHUNK, CHUNK), 1)
    return row_ids, col_ids


def lower_inverses(strict_parts):
    row_ids, col_ids = chunk_ids()
    results = None
    size = 1
    while size < CHUNK:
        pair_mask = (row_ids // (2 * size) == col_ids // (2 * size)) & (
            (row_ids // size) != (col_ids // size)
        )
        corners = [jnp.where(pair_mask, part, 0.0) for part in strict_parts]
        if results is None:
            ident = jnp.where(row_ids == col_ids, 1.0, 0.0)
            results = [ident - corner for corner in corners]
        else:
            moved = [mm_fine(corner, result, NN) for corner, result in zip(corners, results)]
            results = [result - mm_fine(result, part, NN) for result, part in zip(results, moved)]
        size *= 2
    return results


def conv_taps(extended, taps, extent):
    total = taps[0:1] * extended[5 : 5 + extent]
    for offset in range(1, CONV):
        total = total + taps[offset : offset + 1] * extended[5 + offset : 5 + offset + extent]
    return total


def unit_keys(raw):
    scale = lax.rsqrt(jnp.sum(raw * raw, axis=-1, keepdims=True) + KEY_EPS)
    return raw * scale, scale


def mix_forward_kernel(
    pre_ref, gate_ref, beta_ref, taps_ref, gain_ref, y_ref, core_ref, state_ref, inverse_ref,
    state_now, rim, *, heads
):
    width = heads * HD
    step = pre_ref.shape[0]
    chunks = step // CHUNK

    @pl.when(pl.program_id(0) == 0)
    def _():
        state_now[...] = jnp.zeros_like(state_now)
        rim[...] = jnp.zeros_like(rim)

    pre = pre_ref[...].astype(F32)
    extended = jnp.concatenate([rim[...], pre], axis=0)
    rim[...] = pre[step - 8 :]
    conv = conv_taps(extended, taps_ref[...], step)
    mixture = conv * sigmoid(conv)
    beta = sigmoid(beta_ref[...])
    row_ids, col_ids = chunk_ids()
    tiles = [(chunk, head) for chunk in range(chunks) for head in range(heads)]
    q_t, k_t, v_t, b_t, score_t, strict_t = [], [], [], [], [], []
    for chunk, head in tiles:
        rows = slice(chunk * CHUNK, (chunk + 1) * CHUNK)
        q_rows = mixture[rows, head * HD : (head + 1) * HD]
        k_rows, _ = unit_keys(mixture[rows, width + head * HD : width + (head + 1) * HD])
        v_rows = mixture[rows, 2 * width + head * HD : 2 * width + (head + 1) * HD]
        b_rows = beta[rows, head : head + 1]
        q_t.append(q_rows)
        k_t.append(k_rows)
        v_t.append(v_rows)
        b_t.append(b_rows)
        score_t.append(jnp.where(row_ids >= col_ids, mm(q_rows, k_rows, NT), 0.0))
        strict_t.append(jnp.where(row_ids > col_ids, b_rows * mm_fine(k_rows, k_rows, NT), 0.0))
    inverse_t = lower_inverses(strict_t)
    w_t = [mm(t, b * k, NN) for t, b, k in zip(inverse_t, b_t, k_t)]
    u_t = [mm(t, b * v, NN) for t, b, v in zip(inverse_t, b_t, v_t)]
    for index, (chunk, head) in enumerate(tiles):
        rows = slice(chunk * CHUNK, (chunk + 1) * CHUNK)
        cols = slice(head * HD, (head + 1) * HD)
        state = state_now[head]
        state_ref[chunk, head] = state
        inverse_ref[chunk, head] = inverse_t[index]
        update = u_t[index] - mm(w_t[index], state, NN)
        core = mm(q_t[index], state, NN) + mm(score_t[index], update, NN)
        state_now[head] = state + mm(k_t[index], update, TN)
        core_ref[rows, cols] = core
        scale = lax.rsqrt(jnp.mean(core * core, axis=-1, keepdims=True) + EPS)
        gate = gate_ref[rows, cols]
        y_ref[rows, cols] = (
            core * scale * gain_ref[...] * (gate * sigmoid(gate))
        ).astype(y_ref.dtype)


def mix_backward_kernel(
    pre_ref, before_ref, gate_ref, beta_ref, dy_ref, core_ref, state_ref, inverse_ref, taps_ref,
    gain_ref, dpre_ref, dgate_ref, dbeta_ref, gtaps_ref, ggain_ref, adjoint, rim, *, heads, blocks
):
    width = heads * HD
    step = pre_ref.shape[0]
    chunks = step // CHUNK
    block = blocks - 1 - pl.program_id(0)

    @pl.when(pl.program_id(0) == 0)
    def _():
        adjoint[...] = jnp.zeros_like(adjoint)
        rim[...] = jnp.zeros_like(rim)
        gtaps_ref[...] = jnp.zeros_like(gtaps_ref)
        ggain_ref[...] = jnp.zeros_like(ggain_ref)

    before = before_ref[...].astype(F32)
    before = jnp.where(block > 0, before[before.shape[0] - 8 :], 0.0)
    extended = jnp.concatenate([before, pre_ref[...].astype(F32)], axis=0)
    taps = taps_ref[...]
    conv = conv_taps(extended, taps, step)
    conv_sig = sigmoid(conv)
    mixture = conv * conv_sig
    beta = sigmoid(beta_ref[...])
    gain = gain_ref[...]
    row_ids, col_ids = chunk_ids()
    causal, strict = row_ids >= col_ids, row_ids > col_ids
    tiles = [(chunk, head) for chunk in range(chunks) for head in range(heads)]
    held = {}
    ggain = jnp.zeros((1, HD), F32)
    for chunk, head in tiles:
        rows = slice(chunk * CHUNK, (chunk + 1) * CHUNK)
        cols = slice(head * HD, (head + 1) * HD)
        q_rows = mixture[rows, head * HD : (head + 1) * HD]
        k_rows, k_scale = unit_keys(mixture[rows, width + head * HD : width + (head + 1) * HD])
        v_rows = mixture[rows, 2 * width + head * HD : 2 * width + (head + 1) * HD]
        b_rows = beta[rows, head : head + 1]
        core = core_ref[rows, cols]
        scale = lax.rsqrt(jnp.mean(core * core, axis=-1, keepdims=True) + EPS)
        gate = gate_ref[rows, cols]
        gate_sig = sigmoid(gate)
        dy = dy_ref[rows, cols].astype(F32)
        normed = core * scale
        ggain += jnp.sum(dy * (gate * gate_sig) * normed, axis=0, keepdims=True)
        dgate_ref[rows, cols] = (
            dy * normed * gain * (gate_sig * (1.0 + gate * (1.0 - gate_sig)))
        ).astype(dgate_ref.dtype)
        dnorm = dy * (gate * gate_sig) * gain
        dcore = scale * (dnorm - normed * jnp.mean(dnorm * normed, axis=-1, keepdims=True))
        state = state_ref[chunk, head]
        inverse = inverse_ref[chunk, head]
        scores = jnp.where(causal, mm(q_rows, k_rows, NT), 0.0)
        weighted = mm(inverse, b_rows * k_rows, NN)
        resid = v_rows - mm(k_rows, state, NN)
        update = mm(inverse, b_rows * resid, NN)
        dupdate = mm(scores, dcore, TN)
        dstate = mm(q_rows, dcore, TN)
        held[chunk, head] = [
            q_rows, k_rows, k_scale, b_rows, dcore, state, inverse, weighted, resid, update, dupdate,
            dstate
        ]
    later = {}
    for chunk in reversed(range(chunks)):
        for head in range(heads):
            entry = held[chunk, head]
            after = adjoint[head]
            later[chunk, head] = after
            entry[10] = entry[10] + mm(entry[1], after, NN)
            adjoint[head] = after + entry[11] - mm(entry[7], entry[10], TN)
    pieces = {}
    for chunk, head in tiles:
        (
            q_rows, k_rows, k_scale, b_rows, dcore, state, inverse, _, resid, update, dupdate, _
        ) = held[chunk, head]
        after = later[chunk, head]
        rows = slice(chunk * CHUNK, (chunk + 1) * CHUNK)
        dr = mm(inverse, dupdate, TN)
        dv = b_rows * dr
        dstrict = jnp.where(strict, -mm(dr, update, NT), 0.0)
        gram = mm(k_rows, k_rows, NT)
        dbeta = jnp.sum(dr * resid, axis=-1, keepdims=True) + jnp.sum(
            dstrict * gram, axis=-1, keepdims=True
        )
        dgram = b_rows * dstrict
        dscores = jnp.where(causal, mm(dcore, update, NT), 0.0)
        dq = mm(dcore, state, NT) + mm(dscores, k_rows, NN)
        dk = (
            mm(dscores, q_rows, TN)
            + mm(update, after, NT)
            - mm(dv, state, NT)
            + mm(dgram, k_rows, NN)
            + mm(dgram, k_rows, TN)
        )
        dkraw = k_scale * (dk - k_rows * jnp.sum(dk * k_rows, axis=-1, keepdims=True))
        pieces[0, head, chunk] = dq
        pieces[1, head, chunk] = dkraw
        pieces[2, head, chunk] = dv
        dbeta_ref[rows, head : head + 1] = dbeta * b_rows * (1.0 - b_rows)
    dmixture = jnp.concatenate(
        [
            jnp.concatenate([pieces[part, head, chunk] for chunk in range(chunks)], axis=0)
            for part in range(3)
            for head in range(heads)
        ],
        axis=1,
    )
    dconv = dmixture * (conv_sig * (1.0 + conv * (1.0 - conv_sig)))
    followed = jnp.concatenate([dconv, rim[...]], axis=0)
    rim[...] = dconv[:8]
    dpre = taps[CONV - 1 : CONV] * followed[0:step]
    for offset in range(CONV - 1):
        shift = CONV - 1 - offset
        dpre = dpre + taps[offset : offset + 1] * followed[shift : shift + step]
    dpre_ref[...] = dpre.astype(dpre_ref.dtype)
    for offset in range(CONV):
        gtaps_ref[offset : offset + 1] += jnp.sum(
            dconv * extended[5 + offset : 5 + offset + step], axis=0, keepdims=True
        )
    ggain_ref[0:1] += ggain


def mix_forward(pre, gate, beta, taps, gain):
    extent, width3 = pre.shape
    width = width3 // 3
    heads = width // HD
    step = min(STEP, extent)
    blocks, chunks = extent // step, step // CHUNK
    return pl.pallas_call(
        functools.partial(mix_forward_kernel, heads=heads),
        grid=(blocks,),
        in_specs=[
            pl.BlockSpec((step, width3), lambda i: (i, 0)),
            pl.BlockSpec((step, width), lambda i: (i, 0)),
            pl.BlockSpec((step, heads), lambda i: (i, 0)),
            pl.BlockSpec((8, width3), lambda i: (0, 0)),
            pl.BlockSpec((1, HD), lambda i: (0, 0)),
        ],
        out_specs=[
            pl.BlockSpec((step, width), lambda i: (i, 0)),
            pl.BlockSpec((step, width), lambda i: (i, 0)),
            pl.BlockSpec((chunks, heads, HD, HD), lambda i: (i, 0, 0, 0)),
            pl.BlockSpec((chunks, heads, CHUNK, CHUNK), lambda i: (i, 0, 0, 0)),
        ],
        out_shape=[
            jax.ShapeDtypeStruct((extent, width), BF),
            jax.ShapeDtypeStruct((extent, width), F32),
            jax.ShapeDtypeStruct((extent // CHUNK, heads, HD, HD), F32),
            jax.ShapeDtypeStruct((extent // CHUNK, heads, CHUNK, CHUNK), F32),
        ],
        scratch_shapes=[pltpu.VMEM((heads, HD, HD), F32), pltpu.VMEM((8, width3), F32)],
        compiler_params=pltpu.CompilerParams(
            dimension_semantics=("arbitrary",), vmem_limit_bytes=48 * 1024 * 1024
        ),
        name="mix_forward",
    )(pre, gate, beta, taps, gain)


def mix_backward(pre, gate, beta, dy, core, states, inverses, taps, gain):
    extent, width3 = pre.shape
    width = width3 // 3
    heads = width // HD
    step = min(STEP, extent)
    blocks, chunks = extent // step, step // CHUNK
    rows_before = 16

    def at(i):
        return (blocks - 1 - i, 0)

    def at_tiles(i):
        return (blocks - 1 - i, 0, 0, 0)

    def just_before(i):
        return (jnp.maximum((blocks - 1 - i) * (step // rows_before) - 1, 0), 0)

    return pl.pallas_call(
        functools.partial(mix_backward_kernel, heads=heads, blocks=blocks),
        grid=(blocks,),
        in_specs=[
            pl.BlockSpec((step, width3), at),
            pl.BlockSpec((rows_before, width3), just_before),
            pl.BlockSpec((step, width), at),
            pl.BlockSpec((step, heads), at),
            pl.BlockSpec((step, width), at),
            pl.BlockSpec((step, width), at),
            pl.BlockSpec((chunks, heads, HD, HD), at_tiles),
            pl.BlockSpec((chunks, heads, CHUNK, CHUNK), at_tiles),
            pl.BlockSpec((8, width3), lambda i: (0, 0)),
            pl.BlockSpec((1, HD), lambda i: (0, 0)),
        ],
        out_specs=[
            pl.BlockSpec((step, width3), at),
            pl.BlockSpec((step, width), at),
            pl.BlockSpec((step, heads), at),
            pl.BlockSpec((8, width3), lambda i: (0, 0)),
            pl.BlockSpec((8, HD), lambda i: (0, 0)),
        ],
        out_shape=[
            jax.ShapeDtypeStruct((extent, width3), BF),
            jax.ShapeDtypeStruct((extent, width), BF),
            jax.ShapeDtypeStruct((extent, heads), F32),
            jax.ShapeDtypeStruct((8, width3), F32),
            jax.ShapeDtypeStruct((8, HD), F32),
        ],
        scratch_shapes=[pltpu.VMEM((heads, HD, HD), F32), pltpu.VMEM((8, width3), F32)],
        compiler_params=pltpu.CompilerParams(
            dimension_semantics=("arbitrary",), vmem_limit_bytes=48 * 1024 * 1024
        ),
        name="mix_backward",
    )(pre, pre, gate, beta, dy, core, states, inverses, taps, gain)


def dot(left, right, dims=NN):
    return lax.dot_general(left, right, (dims, ((), ())), preferred_element_type=F32)


def swapped(value, axis, distance):
    count = lax.axis_size(axis)
    return lax.ppermute(value, axis, [(i, i ^ distance) for i in range(count)])


def gathered(shard, axis):
    count, place = lax.axis_size(axis), lax.axis_index(axis)
    whole = jnp.zeros((count,) + shard.shape, shard.dtype)
    for distance in range(count):
        part = swapped(shard, axis, distance) if distance else shard
        whole = lax.dynamic_update_index_in_dim(whole, part, place ^ distance, 0)
    return whole


def summed_shard(parts, axis):
    count, place = lax.axis_size(axis), lax.axis_index(axis)
    total = lax.dynamic_index_in_dim(parts, place, 0, False)
    low = parts.astype(BF)
    for distance in range(1, count):
        piece = lax.dynamic_index_in_dim(low, place ^ distance, 0, False)
        total = total + swapped(piece, axis, distance).astype(F32)
    return total


def spread(value, axis):
    return lax.all_to_all(value, axis, 0, 0, tiled=True)


def rms_scale(values):
    return lax.rsqrt(jnp.mean(values * values, axis=-1, keepdims=True) + EPS)


def norm_pull(values, scale, gain, grad):
    weighted = grad * gain
    return scale * weighted - values * (
        scale * scale * scale * jnp.mean(weighted * values, axis=-1, keepdims=True)
    )


def per_device(
    tokens,
    cotangent,
    group_ids,
    group_scale,
    attn_gain,
    w_qkv,
    conv_weight,
    w_beta,
    w_gate_o,
    norm_gain_o,
    w_out,
    ffn_gain,
    w_gate_up,
    w_down,
):
    seg_len, width = tokens.shape[1:]
    dps, ctxs = lax.axis_size("dp"), lax.axis_size("ctx")
    devices = dps * ctxs
    ctx_place = lax.axis_index("ctx")
    extent = seg_len * ctxs
    head_count = w_beta.shape[1]
    heads = head_count // ctxs
    mix_width = heads * HD
    row_part = w_qkv.shape[0]
    ff_part = w_down.shape[0]
    ff_local = dps * ff_part
    taps_part = conv_weight.shape[1]
    taps_cols = CONV * taps_part // row_part
    gain_part = norm_gain_o.shape[0]
    own_rows = ctx_place * seg_len

    small = jnp.concatenate(
        [
            w_beta,
            attn_gain[:, None],
            ffn_gain[:, None],
            jnp.pad(norm_gain_o, (0, row_part - gain_part))[:, None],
            conv_weight.reshape(row_part, taps_cols),
        ],
        axis=1,
    )
    small = jnp.pad(small, ((0, 0), (0, 128 - small.shape[1])))
    mix_rows = jnp.concatenate(
        [
            w_qkv.reshape(row_part, 3, ctxs, mix_width).transpose(2, 0, 1, 3).reshape(
                ctxs, row_part, 3 * mix_width
            ),
            w_gate_o.reshape(row_part, ctxs, mix_width).transpose(1, 0, 2),
            jnp.broadcast_to(small[None], (ctxs,) + small.shape),
        ],
        axis=2,
    )
    mix_cols = mix_rows.shape[2]
    x_full = lax.all_gather(tokens[0], "ctx", axis=0, tiled=True)
    mix_half = spread(mix_rows, "ctx").reshape(ctxs * row_part, mix_cols)
    w_mix = gathered(mix_half, "dp").reshape(width, mix_cols)
    gate_up_rows = (
        w_gate_up.reshape(row_part, 2, dps, ctxs, ff_part)
        .transpose(3, 0, 1, 2, 4)
        .reshape(ctxs, row_part, 2 * ff_local)
    )
    gate_up_half = spread(gate_up_rows, "ctx").reshape(ctxs * row_part, 2 * ff_local)
    w_gu = gathered(gate_up_half, "dp").reshape(width, 2 * ff_local)
    w_dn = gathered(w_down, "dp").reshape(ff_local, width)
    w_out_full = lax.all_gather(w_out, ("dp", "ctx"), axis=0, tiled=True)

    w_proj = w_mix[:, : 4 * mix_width]
    w_small = w_mix[:, 4 * mix_width :]
    place = head_count
    attn_full = w_small[:, place].astype(F32)
    ffn_full = w_small[:, place + 1].astype(F32)
    norm_o_full = w_small[:, place + 2].reshape(devices, row_part)[:, :gain_part]
    norm_o_full = norm_o_full.reshape(1, HD).astype(F32)
    conv_full = (
        w_small[:, place + 3 : place + 3 + taps_cols]
        .reshape(devices, CONV, taps_part)
        .transpose(1, 0, 2)
        .reshape(CONV, 3, ctxs, mix_width)
    )
    taps = lax.dynamic_index_in_dim(conv_full, ctx_place, 2, False).reshape(CONV, 3 * mix_width)
    taps = jnp.pad(taps.astype(F32), ((0, 8 - CONV), (0, 0)))

    x_rows = x_full.astype(F32)
    x_scale = rms_scale(x_rows)
    h1_low = (x_rows * x_scale * attn_full).astype(BF)
    proj = dot(h1_low, w_mix)
    pre_low = proj[:, : 3 * mix_width].astype(BF)
    gate_raw = proj[:, 3 * mix_width : 4 * mix_width]
    beta_logit = lax.dynamic_slice_in_dim(
        proj[:, 4 * mix_width : 4 * mix_width + head_count], ctx_place * heads, heads, 1
    )
    y_local, core, states, inverses = mix_forward(pre_low, gate_raw, beta_logit, taps, norm_o_full)
    y_full = lax.all_gather(y_local, "ctx", axis=1, tiled=True)
    resid = x_rows + dot(y_full, w_out_full)
    resid_scale = rms_scale(resid)
    h2_low = (resid * resid_scale * ffn_full).astype(BF)
    resid_own = lax.dynamic_slice_in_dim(resid, own_rows, seg_len, 0)

    matches = group_ids[:, None] == lax.broadcasted_iota(
        jnp.int32, (group_ids.shape[0], group_scale.shape[0]), 1
    )
    seq_scale = jnp.sum(jnp.where(matches, group_scale[None, :], 0.0), axis=1)
    d_out = cotangent[0].astype(F32) * seq_scale[0]
    d_out_full = lax.all_gather(d_out.astype(BF), "ctx", axis=0, tiled=True)
    gate_up = dot(h2_low, w_gu)
    gate, up = gate_up[:, :ff_local], gate_up[:, ff_local:]
    gate_sig = jax.nn.sigmoid(gate)
    hidden_low = (gate * gate_sig * up).astype(BF)
    out_part = dot(hidden_low, w_dn).astype(BF)
    d_hidden = dot(d_out_full, w_dn, NT).astype(BF).astype(F32)
    d_gate_up = jnp.concatenate(
        [
            (d_hidden * up * (gate_sig * (1.0 + gate * (1.0 - gate_sig)))).astype(BF),
            (d_hidden * (gate * gate_sig)).astype(BF),
        ],
        axis=1,
    )
    d_h2_part = dot(d_gate_up, w_gu, NT).astype(BF)
    d_h2 = lax.psum_scatter(d_h2_part, "ctx", scatter_dimension=0, tiled=True).astype(F32)
    g_down = dot(hidden_low, d_out_full, TN)
    g_gate_up = dot(h2_low, d_gate_up, TN)
    out_sum = lax.psum_scatter(out_part, "ctx", scatter_dimension=0, tiled=True)
    block_out = (resid_own + out_sum.astype(F32)).astype(BF)[None]
    g_w_down = summed_shard(g_down.reshape(dps, ff_part, width), "dp")
    g_gate_up = summed_shard(g_gate_up.reshape(dps, ctxs * row_part, 2 * ff_local), "dp")
    g_gate_up = spread(g_gate_up.astype(BF).reshape(ctxs, row_part, 2 * ff_local), "ctx")
    g_w_gate_up = (
        g_gate_up.reshape(ctxs, row_part, 2, dps, ff_part)
        .transpose(1, 2, 3, 0, 4)
        .reshape(row_part, 2 * ff_local * ctxs)
        .astype(F32)
    )
    g_ffn_gain = jnp.sum(g_w_gate_up * w_gate_up.astype(F32), axis=1) / ffn_gain.astype(F32)

    d_resid = d_out + norm_pull(resid_own, rms_scale(resid_own), ffn_full, d_h2)
    d_attn = d_resid.astype(BF)
    d_y_own = dot(d_attn, w_out_full, NT).astype(BF)
    d_y = spread(d_y_own.reshape(seg_len, ctxs, mix_width).transpose(1, 0, 2), "ctx")
    d_y = d_y.reshape(extent, mix_width)
    col_part = width // ctxs
    d_attn_cols = spread(d_attn.reshape(seg_len, ctxs, col_part).transpose(1, 0, 2), "ctx")
    d_attn_cols = d_attn_cols.reshape(extent, col_part)
    g_out = dot(y_full, d_attn_cols, TN)

    d_pre, d_gate_low, d_beta, g_taps, g_gain_o = mix_backward(
        pre_low, gate_raw, beta_logit, d_y, core, states, inverses, taps, norm_o_full
    )
    d_beta_low = d_beta.astype(BF)
    d_proj = jnp.concatenate([d_pre, d_gate_low], axis=1)
    w_beta_own = lax.dynamic_slice_in_dim(w_small[:, :head_count], ctx_place * heads, heads, 1)
    d_h1_part = (dot(d_proj, w_proj, NT) + dot(d_beta_low, w_beta_own, NT)).astype(BF)
    d_h1 = lax.psum_scatter(d_h1_part, "ctx", scatter_dimension=0, tiled=True).astype(F32)
    x_own = tokens[0].astype(F32)
    d_tokens = (d_resid + norm_pull(x_own, rms_scale(x_own), attn_full, d_h1))[None]

    g_proj = dot(h1_low, d_proj, TN)
    g_beta = dot(h1_low, d_beta_low, TN)
    taps_grad = jnp.zeros((CONV, 3, ctxs, mix_width), F32)
    taps_grad = lax.dynamic_update_index_in_dim(
        taps_grad, g_taps[:CONV].reshape(CONV, 3, mix_width), ctx_place, 2
    )
    taps_grad = (
        taps_grad.reshape(CONV, devices, taps_part)
        .transpose(1, 0, 2)
        .reshape(width, taps_cols)
    )
    gain_grad = jnp.pad(g_gain_o[0].reshape(devices, gain_part), ((0, 0), (0, row_part - gain_part)))
    small_grad = jnp.concatenate([g_beta, gain_grad.reshape(width, 1), taps_grad], axis=1)
    small_grad = jnp.pad(small_grad, ((0, 0), (0, 128 - small_grad.shape[1])))
    g_mix = jnp.concatenate([g_proj, g_out, small_grad], axis=1)
    g_cols = g_mix.shape[1]
    g_mix = summed_shard(g_mix.reshape(dps, ctxs * row_part, g_cols), "dp")
    g_mix = spread(g_mix.astype(BF).reshape(ctxs, row_part, g_cols), "ctx").astype(F32)

    def own_cols(start, size):
        return g_mix[:, :, start : start + size].transpose(1, 0, 2).reshape(row_part, ctxs * size)

    g_w_qkv = (
        g_mix[:, :, : 3 * mix_width]
        .reshape(ctxs, row_part, 3, mix_width)
        .transpose(1, 2, 0, 3)
        .reshape(row_part, 3 * width)
    )
    g_w_gate_o = own_cols(3 * mix_width, mix_width)
    g_w_out = own_cols(4 * mix_width, col_part)
    place = 4 * mix_width + col_part
    g_w_beta = own_cols(place, heads)
    g_norm_gain_o = jnp.sum(g_mix[:, :gain_part, place + heads], axis=0)
    g_conv = jnp.sum(g_mix[:, :, place + heads + 1 : place + heads + 1 + taps_cols], axis=0)
    g_conv = g_conv.reshape(CONV, taps_part)
    g_attn_gain = (
        jnp.sum(g_w_qkv * w_qkv.astype(F32), axis=1)
        + jnp.sum(g_w_beta * w_beta.astype(F32), axis=1)
        + jnp.sum(g_w_gate_o * w_gate_o.astype(F32), axis=1)
    ) / attn_gain.astype(F32)
    return (
        block_out,
        d_tokens,
        g_attn_gain,
        g_w_qkv,
        g_conv,
        g_w_beta,
        g_w_gate_o,
        g_norm_gain_o,
        g_w_out,
        g_ffn_gain,
        g_w_gate_up,
        g_w_down,
    )


def solution(mesh):
    rows = P(("dp", "ctx"), None)
    flat = P(("dp", "ctx"))
    taps = P(None, ("dp", "ctx"))
    acts = P("dp", "ctx", None)
    return jax.shard_map(
        per_device,
        mesh=mesh,
        in_specs=(
            acts, acts, P("dp"), P(), flat, rows, taps, rows, rows, flat, rows, flat, rows, rows
        ),
        out_specs=(acts, acts, flat, rows, taps, rows, rows, flat, rows, flat, rows, rows),
        check_vma=False,
    )
```

```python
import functools

import jax
import jax.numpy as jnp
from jax import lax
from jax.experimental import pallas as pl
from jax.experimental.layout import Layout, with_layout_constraint
from jax.experimental.pallas import tpu as pltpu
from jax.sharding import PartitionSpec as P

CONV = 4
HD = 128
CHUNK = 128
STEP = 256
EPS = 1e-05
KEY_EPS = 1e-06
BF = jnp.bfloat16
F32 = jnp.float32
NN = ((1,), (0,))
NT = ((1,), (1,))
TN = ((0,), (0,))


def mm(left, right, dims):
    return lax.dot_general(
        left.astype(BF), right.astype(BF), (dims, ((), ())), preferred_element_type=F32
    )


def halves(values):
    high = values.astype(BF)
    return high, (values - high.astype(F32)).astype(BF)


def mm_fine(left, right, dims):
    left_hi, left_lo = halves(left)
    right_hi, right_lo = halves(right)

    def product(a, b):
        return lax.dot_general(a, b, (dims, ((), ())), preferred_element_type=F32)

    return product(left_hi, right_hi) + (product(left_hi, right_lo) + product(left_lo, right_hi))


def sigmoid(values):
    return 1.0 / (1.0 + jnp.exp(-values))


def chunk_ids():
    row_ids = lax.broadcasted_iota(jnp.int32, (CHUNK, CHUNK), 0)
    col_ids = lax.broadcasted_iota(jnp.int32, (CHUNK, CHUNK), 1)
    return row_ids, col_ids


def lower_inverses(strict_parts):
    row_ids, col_ids = chunk_ids()
    results = None
    size = 1
    while size < CHUNK:
        pair_mask = (row_ids // (2 * size) == col_ids // (2 * size)) & (
            (row_ids // size) != (col_ids // size)
        )
        corners = [jnp.where(pair_mask, part, 0.0) for part in strict_parts]
        if results is None:
            ident = jnp.where(row_ids == col_ids, 1.0, 0.0)
            results = [ident - corner for corner in corners]
        else:
            moved = [mm_fine(corner, result, NN) for corner, result in zip(corners, results)]
            results = [result - mm_fine(result, part, NN) for result, part in zip(results, moved)]
        size *= 2
    return results


def conv_taps(extended, taps, extent):
    total = taps[0:1] * extended[5 : 5 + extent]
    for offset in range(1, CONV):
        total = total + taps[offset : offset + 1] * extended[5 + offset : 5 + offset + extent]
    return total


def unit_keys(raw):
    scale = lax.rsqrt(jnp.sum(raw * raw, axis=-1, keepdims=True) + KEY_EPS)
    return raw * scale, scale


def mix_forward_kernel(
    pre_ref, gate_ref, beta_ref, taps_ref, gain_ref, y_ref, core_ref, state_ref, inverse_ref,
    state_now, rim, *, heads
):
    width = heads * HD
    step = pre_ref.shape[0]
    chunks = step // CHUNK

    @pl.when(pl.program_id(0) == 0)
    def _():
        state_now[...] = jnp.zeros_like(state_now)
        rim[...] = jnp.zeros_like(rim)

    pre = pre_ref[...].astype(F32)
    extended = jnp.concatenate([rim[...], pre], axis=0)
    rim[...] = pre[step - 8 :]
    conv = conv_taps(extended, taps_ref[...], step)
    mixture = conv * sigmoid(conv)
    beta = sigmoid(beta_ref[...])
    row_ids, col_ids = chunk_ids()
    tiles = [(chunk, head) for chunk in range(chunks) for head in range(heads)]
    q_t, k_t, v_t, b_t, score_t, strict_t = [], [], [], [], [], []
    for chunk, head in tiles:
        rows = slice(chunk * CHUNK, (chunk + 1) * CHUNK)
        q_rows = mixture[rows, head * HD : (head + 1) * HD]
        k_rows, _ = unit_keys(mixture[rows, width + head * HD : width + (head + 1) * HD])
        v_rows = mixture[rows, 2 * width + head * HD : 2 * width + (head + 1) * HD]
        b_rows = beta[rows, head : head + 1]
        q_t.append(q_rows)
        k_t.append(k_rows)
        v_t.append(v_rows)
        b_t.append(b_rows)
        score_t.append(jnp.where(row_ids >= col_ids, mm(q_rows, k_rows, NT), 0.0))
        strict_t.append(jnp.where(row_ids > col_ids, b_rows * mm_fine(k_rows, k_rows, NT), 0.0))
    inverse_t = lower_inverses(strict_t)
    w_t = [mm(t, b * k, NN) for t, b, k in zip(inverse_t, b_t, k_t)]
    u_t = [mm(t, b * v, NN) for t, b, v in zip(inverse_t, b_t, v_t)]
    for index, (chunk, head) in enumerate(tiles):
        rows = slice(chunk * CHUNK, (chunk + 1) * CHUNK)
        cols = slice(head * HD, (head + 1) * HD)
        state = state_now[head]
        state_ref[chunk, head] = state
        inverse_ref[chunk, head] = inverse_t[index]
        update = u_t[index] - mm(w_t[index], state, NN)
        core = mm(q_t[index], state, NN) + mm(score_t[index], update, NN)
        state_now[head] = state + mm(k_t[index], update, TN)
        core_ref[rows, cols] = core
        scale = lax.rsqrt(jnp.mean(core * core, axis=-1, keepdims=True) + EPS)
        gate = gate_ref[rows, cols]
        y_ref[rows, cols] = (
            core * scale * gain_ref[...] * (gate * sigmoid(gate))
        ).astype(y_ref.dtype)


def mix_backward_kernel(
    pre_ref, before_ref, gate_ref, beta_ref, dy_ref, core_ref, state_ref, inverse_ref, taps_ref,
    gain_ref, dproj_ref, dbeta_ref, gtaps_ref, ggain_ref, adjoint, rim, *, heads, blocks
):
    width = heads * HD
    step = pre_ref.shape[0]
    chunks = step // CHUNK
    block = blocks - 1 - pl.program_id(0)

    @pl.when(pl.program_id(0) == 0)
    def _():
        adjoint[...] = jnp.zeros_like(adjoint)
        rim[...] = jnp.zeros_like(rim)
        gtaps_ref[...] = jnp.zeros_like(gtaps_ref)
        ggain_ref[...] = jnp.zeros_like(ggain_ref)

    before = before_ref[...].astype(F32)
    before = jnp.where(block > 0, before[before.shape[0] - 8 :], 0.0)
    extended = jnp.concatenate([before, pre_ref[...].astype(F32)], axis=0)
    taps = taps_ref[...]
    conv = conv_taps(extended, taps, step)
    conv_sig = sigmoid(conv)
    mixture = conv * conv_sig
    beta = sigmoid(beta_ref[...])
    gain = gain_ref[...]
    row_ids, col_ids = chunk_ids()
    causal, strict = row_ids >= col_ids, row_ids > col_ids
    tiles = [(chunk, head) for chunk in range(chunks) for head in range(heads)]
    held = {}
    ggain = jnp.zeros((1, HD), F32)
    for chunk, head in tiles:
        rows = slice(chunk * CHUNK, (chunk + 1) * CHUNK)
        cols = slice(head * HD, (head + 1) * HD)
        q_rows = mixture[rows, head * HD : (head + 1) * HD]
        k_rows, k_scale = unit_keys(mixture[rows, width + head * HD : width + (head + 1) * HD])
        v_rows = mixture[rows, 2 * width + head * HD : 2 * width + (head + 1) * HD]
        b_rows = beta[rows, head : head + 1]
        core = core_ref[rows, cols]
        scale = lax.rsqrt(jnp.mean(core * core, axis=-1, keepdims=True) + EPS)
        gate = gate_ref[rows, cols]
        gate_sig = sigmoid(gate)
        dy = dy_ref[rows, cols].astype(F32)
        normed = core * scale
        ggain += jnp.sum(dy * (gate * gate_sig) * normed, axis=0, keepdims=True)
        dproj_ref[rows, 3 * width + head * HD : 3 * width + (head + 1) * HD] = (
            dy * normed * gain * (gate_sig * (1.0 + gate * (1.0 - gate_sig)))
        ).astype(dproj_ref.dtype)
        dnorm = dy * (gate * gate_sig) * gain
        dcore = scale * (dnorm - normed * jnp.mean(dnorm * normed, axis=-1, keepdims=True))
        state = state_ref[chunk, head]
        inverse = inverse_ref[chunk, head]
        scores = jnp.where(causal, mm(q_rows, k_rows, NT), 0.0)
        weighted = mm(inverse, b_rows * k_rows, NN)
        resid = v_rows - mm(k_rows, state, NN)
        update = mm(inverse, b_rows * resid, NN)
        dupdate = mm(scores, dcore, TN)
        dstate = mm(q_rows, dcore, TN)
        held[chunk, head] = [
            q_rows, k_rows, k_scale, b_rows, dcore, state, inverse, weighted, resid, update, dupdate,
            dstate
        ]
    later = {}
    for chunk in reversed(range(chunks)):
        for head in range(heads):
            entry = held[chunk, head]
            after = adjoint[head]
            later[chunk, head] = after
            entry[10] = entry[10] + mm(entry[1], after, NN)
            adjoint[head] = after + entry[11] - mm(entry[7], entry[10], TN)
    pieces = {}
    for chunk, head in tiles:
        (
            q_rows, k_rows, k_scale, b_rows, dcore, state, inverse, _, resid, update, dupdate, _
        ) = held[chunk, head]
        after = later[chunk, head]
        rows = slice(chunk * CHUNK, (chunk + 1) * CHUNK)
        dr = mm(inverse, dupdate, TN)
        dv = b_rows * dr
        dstrict = jnp.where(strict, -mm(dr, update, NT), 0.0)
        gram = mm(k_rows, k_rows, NT)
        dbeta = jnp.sum(dr * resid, axis=-1, keepdims=True) + jnp.sum(
            dstrict * gram, axis=-1, keepdims=True
        )
        dgram = b_rows * dstrict
        dscores = jnp.where(causal, mm(dcore, update, NT), 0.0)
        dq = mm(dcore, state, NT) + mm(dscores, k_rows, NN)
        dk = (
            mm(dscores, q_rows, TN)
            + mm(update, after, NT)
            - mm(dv, state, NT)
            + mm(dgram, k_rows, NN)
            + mm(dgram, k_rows, TN)
        )
        dkraw = k_scale * (dk - k_rows * jnp.sum(dk * k_rows, axis=-1, keepdims=True))
        pieces[0, head, chunk] = dq
        pieces[1, head, chunk] = dkraw
        pieces[2, head, chunk] = dv
        dbeta_ref[rows, head : head + 1] = dbeta * b_rows * (1.0 - b_rows)
    dmixture = jnp.concatenate(
        [
            jnp.concatenate([pieces[part, head, chunk] for chunk in range(chunks)], axis=0)
            for part in range(3)
            for head in range(heads)
        ],
        axis=1,
    )
    dconv = dmixture * (conv_sig * (1.0 + conv * (1.0 - conv_sig)))
    followed = jnp.concatenate([dconv, rim[...]], axis=0)
    rim[...] = dconv[:8]
    dpre = taps[CONV - 1 : CONV] * followed[0:step]
    for offset in range(CONV - 1):
        shift = CONV - 1 - offset
        dpre = dpre + taps[offset : offset + 1] * followed[shift : shift + step]
    dproj_ref[:, : 3 * width] = dpre.astype(dproj_ref.dtype)
    for offset in range(CONV):
        gtaps_ref[offset : offset + 1] += jnp.sum(
            dconv * extended[5 + offset : 5 + offset + step], axis=0, keepdims=True
        )
    ggain_ref[0:1] += ggain


def mix_forward(pre, gate, beta, taps, gain):
    extent, width3 = pre.shape
    width = width3 // 3
    heads = width // HD
    step = min(STEP, extent)
    blocks, chunks = extent // step, step // CHUNK
    return pl.pallas_call(
        functools.partial(mix_forward_kernel, heads=heads),
        grid=(blocks,),
        in_specs=[
            pl.BlockSpec((step, width3), lambda i: (i, 0)),
            pl.BlockSpec((step, width), lambda i: (i, 0)),
            pl.BlockSpec((step, heads), lambda i: (i, 0)),
            pl.BlockSpec((8, width3), lambda i: (0, 0)),
            pl.BlockSpec((1, HD), lambda i: (0, 0)),
        ],
        out_specs=[
            pl.BlockSpec((step, width), lambda i: (i, 0)),
            pl.BlockSpec((step, width), lambda i: (i, 0)),
            pl.BlockSpec((chunks, heads, HD, HD), lambda i: (i, 0, 0, 0)),
            pl.BlockSpec((chunks, heads, CHUNK, CHUNK), lambda i: (i, 0, 0, 0)),
        ],
        out_shape=[
            jax.ShapeDtypeStruct((extent, width), BF),
            jax.ShapeDtypeStruct((extent, width), F32),
            jax.ShapeDtypeStruct((extent // CHUNK, heads, HD, HD), F32),
            jax.ShapeDtypeStruct((extent // CHUNK, heads, CHUNK, CHUNK), F32),
        ],
        scratch_shapes=[pltpu.VMEM((heads, HD, HD), F32), pltpu.VMEM((8, width3), F32)],
        compiler_params=pltpu.CompilerParams(
            dimension_semantics=("arbitrary",), vmem_limit_bytes=48 * 1024 * 1024
        ),
        cost_estimate=pl.CostEstimate(
            flops=90 * extent * width * CHUNK, bytes_accessed=40 * extent * width, transcendentals=0
        ),
        name="mix_forward",
    )(pre, gate, beta, taps, gain)


def mix_backward(pre, gate, beta, dy, core, states, inverses, taps, gain):
    extent, width3 = pre.shape
    width = width3 // 3
    heads = width // HD
    step = min(STEP, extent)
    blocks, chunks = extent // step, step // CHUNK
    rows_before = 16

    def at(i):
        return (blocks - 1 - i, 0)

    def at_tiles(i):
        return (blocks - 1 - i, 0, 0, 0)

    def just_before(i):
        return (jnp.maximum((blocks - 1 - i) * (step // rows_before) - 1, 0), 0)

    return pl.pallas_call(
        functools.partial(mix_backward_kernel, heads=heads, blocks=blocks),
        grid=(blocks,),
        in_specs=[
            pl.BlockSpec((step, width3), at),
            pl.BlockSpec((rows_before, width3), just_before),
            pl.BlockSpec((step, width), at),
            pl.BlockSpec((step, heads), at),
            pl.BlockSpec((step, width), at),
            pl.BlockSpec((step, width), at),
            pl.BlockSpec((chunks, heads, HD, HD), at_tiles),
            pl.BlockSpec((chunks, heads, CHUNK, CHUNK), at_tiles),
            pl.BlockSpec((8, width3), lambda i: (0, 0)),
            pl.BlockSpec((1, HD), lambda i: (0, 0)),
        ],
        out_specs=[
            pl.BlockSpec((step, width3 + width), at),
            pl.BlockSpec((step, heads), at),
            pl.BlockSpec((8, width3), lambda i: (0, 0)),
            pl.BlockSpec((8, HD), lambda i: (0, 0)),
        ],
        out_shape=[
            jax.ShapeDtypeStruct((extent, width3 + width), BF),
            jax.ShapeDtypeStruct((extent, heads), F32),
            jax.ShapeDtypeStruct((8, width3), F32),
            jax.ShapeDtypeStruct((8, HD), F32),
        ],
        scratch_shapes=[pltpu.VMEM((heads, HD, HD), F32), pltpu.VMEM((8, width3), F32)],
        compiler_params=pltpu.CompilerParams(
            dimension_semantics=("arbitrary",), vmem_limit_bytes=48 * 1024 * 1024
        ),
        cost_estimate=pl.CostEstimate(
            flops=90 * extent * width * CHUNK, bytes_accessed=40 * extent * width, transcendentals=0
        ),
        name="mix_backward",
    )(pre, pre, gate, beta, dy, core, states, inverses, taps, gain)


def heads_of(ctx, ctxs, heads, row_part):
    blocks = HD // row_part
    groups = ctxs // blocks
    return [((ctx % blocks) * heads + slot) * groups + ctx // blocks for slot in range(heads)]


def pack_mix_kernel(qkv_ref, gate_ref, beta_ref, small_ref, out_ref):
    ctxs = out_ref.shape[0]
    rows, total = gate_ref.shape
    width = total // ctxs
    heads = beta_ref.shape[1] // ctxs
    small = small_ref[...]
    for ctx in range(ctxs):
        betas = []
        for slot, head in enumerate(heads_of(ctx, ctxs, heads, rows)):
            to, cols = slot * HD, slice(head * HD, (head + 1) * HD)
            for part in range(3):
                out_ref[ctx, :, part * width + to : part * width + to + HD] = qkv_ref[
                    :, part * total + head * HD : part * total + (head + 1) * HD
                ]
            out_ref[ctx, :, 3 * width + to : 3 * width + to + HD] = gate_ref[:, cols]
            betas.append(beta_ref[:, head : head + 1])
        out_ref[ctx, :, 4 * width :] = jnp.concatenate(betas + [small], axis=1)


def pack_mix(w_qkv, w_gate_o, w_beta, small, ctxs):
    rows, total = w_gate_o.shape
    cols = 4 * (total // ctxs) + 128
    return pl.pallas_call(
        pack_mix_kernel,
        out_shape=jax.ShapeDtypeStruct((ctxs, rows, cols), w_qkv.dtype),
        name="pack_mix",
    )(w_qkv, w_gate_o, w_beta, small)


def unpack_mix_kernel(
    in_ref, small_in_ref, qkv_ref, gate_ref, beta_ref, gqkv_ref, ggate_ref, gbeta_ref, small_ref,
    rows_ref
):
    ctxs = in_ref.shape[0]
    rows, total = gate_ref.shape
    width = total // ctxs
    heads = gbeta_ref.shape[1] // ctxs
    row_sum = jnp.zeros(rows_ref.shape, F32)
    small_sum = jnp.zeros(small_ref.shape, F32)
    betas = [None] * (heads * ctxs)
    for ctx in range(ctxs):
        small = small_in_ref[ctx].astype(F32)
        small_sum += small
        for slot, head in enumerate(heads_of(ctx, ctxs, heads, rows)):
            betas[head] = small[:, slot : slot + 1]
            for part in range(4):
                start = part * width + slot * HD
                grad = in_ref[ctx, :, start : start + HD].astype(F32)
                if part == 3:
                    cols = slice(head * HD, (head + 1) * HD)
                    ggate_ref[:, cols] = grad
                    weight = gate_ref[:, cols].astype(F32)
                else:
                    cols = slice(part * total + head * HD, part * total + (head + 1) * HD)
                    gqkv_ref[:, cols] = grad
                    weight = qkv_ref[:, cols].astype(F32)
                row_sum += jnp.sum(grad * weight, axis=1, keepdims=True)
    grad = jnp.concatenate(betas, axis=1)
    gbeta_ref[...] = grad
    small_ref[...] = small_sum
    rows_ref[...] = row_sum + jnp.sum(grad * beta_ref[...].astype(F32), axis=1, keepdims=True)


def unpack_mix(received, small, w_qkv, w_gate_o, w_beta):
    rows = w_qkv.shape[0]
    return pl.pallas_call(
        unpack_mix_kernel,
        out_shape=[
            jax.ShapeDtypeStruct(w_qkv.shape, F32),
            jax.ShapeDtypeStruct(w_gate_o.shape, F32),
            jax.ShapeDtypeStruct(w_beta.shape, F32),
            jax.ShapeDtypeStruct((rows, 128), F32),
            jax.ShapeDtypeStruct((rows, 1), F32),
        ],
        compiler_params=pltpu.CompilerParams(vmem_limit_bytes=48 * 1024 * 1024),
        name="unpack_mix",
    )(received, small, w_qkv, w_gate_o, w_beta)


def pack_ff_kernel(in_ref, out_ref, *, dps):
    ctxs = out_ref.shape[0]
    part = out_ref.shape[2] // (2 * dps)
    hidden = in_ref.shape[1] // 2
    for ctx in range(ctxs):
        starts = [
            side * hidden + (place * ctxs + ctx) * part for side in range(2) for place in range(dps)
        ]
        out_ref[ctx] = jnp.concatenate([in_ref[:, s : s + part] for s in starts], axis=1)


def pack_ff(w_gate_up, ctxs, dps):
    rows, total = w_gate_up.shape
    return pl.pallas_call(
        functools.partial(pack_ff_kernel, dps=dps),
        out_shape=jax.ShapeDtypeStruct((ctxs, rows, total // ctxs), w_gate_up.dtype),
        compiler_params=pltpu.CompilerParams(vmem_limit_bytes=48 * 1024 * 1024),
        name="pack_ff",
    )(w_gate_up)


def unpack_ff_kernel(in_ref, w_ref, out_ref, rows_ref, *, dps):
    ctxs = in_ref.shape[0]
    part = in_ref.shape[2] // (2 * dps)
    hidden = out_ref.shape[1] // 2
    row_sum = jnp.zeros(rows_ref.shape, F32)
    for side in range(2):
        pieces = []
        for place in range(dps):
            start = (side * dps + place) * part
            pieces.extend(in_ref[ctx, :, start : start + part] for ctx in range(ctxs))
        grad = jnp.concatenate(pieces, axis=1).astype(F32)
        cols = slice(side * hidden, (side + 1) * hidden)
        out_ref[:, cols] = grad
        row_sum += jnp.sum(grad * w_ref[:, cols].astype(F32), axis=1, keepdims=True)
    rows_ref[...] = row_sum


def unpack_ff(received, w_gate_up, dps):
    return pl.pallas_call(
        functools.partial(unpack_ff_kernel, dps=dps),
        out_shape=[
            jax.ShapeDtypeStruct(w_gate_up.shape, F32),
            jax.ShapeDtypeStruct((w_gate_up.shape[0], 1), F32),
        ],
        compiler_params=pltpu.CompilerParams(vmem_limit_bytes=48 * 1024 * 1024),
        name="unpack_ff",
    )(received, w_gate_up)


def dot(left, right, dims=NN):
    return lax.dot_general(left, right, (dims, ((), ())), preferred_element_type=F32)


def after(value, *others):
    return lax.optimization_barrier((value,) + others)[0]


def swapped(value, axis, distance):
    count = lax.axis_size(axis)
    return lax.ppermute(value, axis, [(i, i ^ distance) for i in range(count)])


def row_major(value):
    return with_layout_constraint(value, Layout(major_to_minor=tuple(range(value.ndim))))


def placed(parts, order):
    whole = row_major(jnp.zeros((len(parts),) + parts[0].shape, parts[0].dtype))
    for part, place in zip(parts, order):
        whole = lax.dynamic_update_index_in_dim(whole, part, place, 0)
    return row_major(lax.optimization_barrier(whole))


def shards_of(shard, axis):
    count = lax.axis_size(axis)
    return [shard] + [swapped(shard, axis, distance) for distance in range(1, count)]


def placed_shards(parts, axis):
    place = lax.axis_index(axis)
    return placed(parts, [place ^ distance for distance in range(len(parts))])


def shard_parts(part_of, axis):
    count, place = lax.axis_size(axis), lax.axis_index(axis)
    sent = [part_of(place ^ distance) for distance in range(1, count)]
    return sent + [part_of(place)]


def swapped_parts(parts, axis):
    return [swapped(part, axis, index + 1) for index, part in enumerate(parts[:-1])] + parts[-1:]


def total_of(parts):
    total = parts[-1].astype(F32)
    for part in parts[:-1]:
        total = total + part.astype(F32)
    return total


def head_routes(row_part, turn):
    dps, ctxs = lax.axis_size("dp"), lax.axis_size("ctx")
    blocks = HD // row_part
    heads = dps // blocks
    routes = []
    for dp in range(dps):
        for ctx in range(ctxs):
            place = (dp % heads) * blocks + ctx % blocks
            user = (ctx // blocks) * blocks + dp // heads
            routes.append((dp * ctxs + ctx, (place ^ turn) * ctxs + user))
    return routes


def head_owner_parts(rows):
    turns = range(lax.axis_size("dp"))
    return [lax.ppermute(rows, ("dp", "ctx"), head_routes(rows.shape[0], turn)) for turn in turns]


def row_owner_parts(blocks):
    place = lax.axis_index("dp")
    parts = []
    for turn in range(lax.axis_size("dp")):
        routes = [(user, owner) for owner, user in head_routes(blocks.shape[1], turn)]
        block = lax.dynamic_index_in_dim(blocks, place ^ turn, 0, False)
        parts.append(lax.ppermute(block, ("dp", "ctx"), routes))
    return parts


def spread(value, axis):
    return lax.all_to_all(value, axis, 0, 0, tiled=True)


def rms_scale(values):
    return lax.rsqrt(jnp.mean(values * values, axis=-1, keepdims=True) + EPS)


def norm_pull(values, scale, gain, grad):
    weighted = grad * gain
    return scale * weighted - values * (
        scale * scale * scale * jnp.mean(weighted * values, axis=-1, keepdims=True)
    )


def per_device(
    tokens,
    cotangent,
    group_ids,
    group_scale,
    attn_gain,
    w_qkv,
    conv_weight,
    w_beta,
    w_gate_o,
    norm_gain_o,
    w_out,
    ffn_gain,
    w_gate_up,
    w_down,
):
    seg_len, width = tokens.shape[1:]
    dps, ctxs = lax.axis_size("dp"), lax.axis_size("ctx")
    devices = dps * ctxs
    ctx_place = lax.axis_index("ctx")
    head_count = w_beta.shape[1]
    heads = head_count // ctxs
    mix_width = heads * HD
    row_part = w_qkv.shape[0]
    dp_rows = ctxs * row_part
    ff_part = w_down.shape[0]
    ff_local = dps * ff_part
    taps_part = conv_weight.shape[1]
    taps_cols = CONV * taps_part // row_part
    gain_part = norm_gain_o.shape[0]
    head_dims = (HD // row_part, heads, ctxs * row_part // HD)

    small = jnp.concatenate(
        [
            attn_gain[:, None],
            ffn_gain[:, None],
            jnp.pad(norm_gain_o, (0, row_part - gain_part))[:, None],
            conv_weight.reshape(row_part, taps_cols),
        ],
        axis=1,
    )
    small = jnp.pad(small, ((0, 0), (0, 128 - heads - small.shape[1])))
    mix_rows = pack_mix(w_qkv, w_gate_o, w_beta, small, ctxs)
    mix_half = spread(mix_rows, "ctx").reshape(dp_rows, mix_rows.shape[2])
    down_parts = shards_of(w_down, "dp")
    mix_half, *down_parts = lax.optimization_barrier((mix_half, *down_parts))
    mix_parts = shards_of(mix_half, "dp")
    x_full = lax.all_gather(after(tokens[0], mix_half), "ctx", axis=0, tiled=True)
    gate_up_rows = pack_ff(w_gate_up, ctxs, dps)
    gate_up_half = spread(after(gate_up_rows, mix_half), "ctx").reshape(dp_rows, 2 * ff_local)
    x_full, gate_up_half, *mix_parts[1:3] = lax.optimization_barrier(
        (x_full, gate_up_half, *mix_parts[1:3])
    )
    out_parts = head_owner_parts(after(w_out, mix_half))
    w_mix = placed_shards(mix_parts, "dp").reshape(width, mix_rows.shape[2])

    matches = group_ids[:, None] == lax.broadcasted_iota(
        jnp.int32, (group_ids.shape[0], group_scale.shape[0]), 1
    )
    seq_scale = jnp.sum(jnp.where(matches, group_scale[None, :], 0.0), axis=1)
    d_out = cotangent[0].astype(F32) * seq_scale[0]
    d_out_full = lax.all_gather(after(d_out.astype(BF), x_full), "ctx", axis=0, tiled=True)

    w_small = lax.optimization_barrier(w_mix[:, 4 * mix_width :].T)
    place = heads
    attn_full = w_small[place].astype(F32)
    ffn_full = w_small[place + 1].astype(F32)
    norm_o_full = w_small[place + 2].reshape(devices, row_part)[:, :gain_part]
    norm_o_full = norm_o_full.reshape(1, HD).astype(F32)
    conv_full = (
        w_small[place + 3 : place + 3 + taps_cols]
        .reshape(taps_cols, devices, row_part)
        .transpose(1, 2, 0)
        .reshape(devices, CONV, taps_part)
        .transpose(1, 0, 2)
        .reshape(CONV, 3, *head_dims, HD)
        .transpose(4, 2, 0, 1, 3, 5)
        .reshape(ctxs, CONV, 3 * mix_width)
    )
    taps = lax.dynamic_index_in_dim(conv_full, ctx_place, 0, False)
    taps = jnp.pad(taps.astype(F32), ((0, 8 - CONV), (0, 0)))

    x_rows = x_full.astype(F32)
    h1_low = (x_rows * rms_scale(x_rows) * attn_full).astype(BF)
    proj = dot(h1_low, w_mix)
    pre_low = proj[:, : 3 * mix_width].astype(BF)
    gate_raw = proj[:, 3 * mix_width : 4 * mix_width]
    beta_logit = proj[:, 4 * mix_width : 4 * mix_width + heads]
    pre_low, *out_parts = lax.optimization_barrier((pre_low, *out_parts))
    w_out_own = placed_shards(out_parts, "dp").reshape(mix_width, width)
    y_local, core, states, inverses = mix_forward(pre_low, gate_raw, beta_logit, taps, norm_o_full)
    gate_up_parts = shards_of(gate_up_half, "dp")
    attn_part = dot(y_local, w_out_own).astype(BF)
    attn_part, d_out_full = lax.optimization_barrier((attn_part, d_out_full))
    attn_sum = lax.psum_scatter(attn_part, "ctx", scatter_dimension=0, tiled=True)

    x_own = tokens[0].astype(F32)
    attn_sum, *gate_up_parts[1:3] = lax.optimization_barrier((attn_sum, *gate_up_parts[1:3]))
    resid = x_own + attn_sum.astype(F32)
    resid_scale = rms_scale(resid)
    h2_own = (resid * resid_scale * ffn_full).astype(BF)
    h2_low = lax.all_gather(h2_own, "ctx", axis=0, tiled=True)

    w_dn = placed_shards(down_parts, "dp").reshape(ff_local, width)
    w_gu = placed_shards(gate_up_parts, "dp").reshape(width, 2 * ff_local)
    gate_up = dot(h2_low, w_gu)
    gate, up = gate_up[:, :ff_local], gate_up[:, ff_local:]
    gate_sig = jax.nn.sigmoid(gate)
    hidden_low = (gate * gate_sig * up).astype(BF)
    d_hidden = dot(d_out_full, w_dn, NT).astype(BF).astype(F32)
    d_gate_up = jnp.concatenate(
        [
            (d_hidden * up * (gate_sig * (1.0 + gate * (1.0 - gate_sig)))).astype(BF),
            (d_hidden * (gate * gate_sig)).astype(BF),
        ],
        axis=1,
    )
    d_h2_part = dot(d_gate_up, w_gu, NT).astype(BF)
    d_h2 = lax.psum_scatter(d_h2_part, "ctx", scatter_dimension=0, tiled=True)
    hidden_later, d_gate_up_later = lax.optimization_barrier((hidden_low, d_gate_up, d_h2_part))[:2]
    out_part = dot(hidden_later, w_dn).astype(BF)

    def down_part(place):
        hidden_cols = lax.dynamic_slice_in_dim(hidden_later, place * ff_part, ff_part, 1)
        return dot(hidden_cols, d_out_full, TN).astype(BF)

    def gate_up_part(place):
        h2_cols = lax.dynamic_slice_in_dim(h2_low, place * dp_rows, dp_rows, 1)
        return dot(h2_cols, d_gate_up_later, TN).astype(BF)

    g_gate_up_parts = shard_parts(gate_up_part, "dp")
    g_down_parts = shard_parts(down_part, "dp")
    g_gate_up_parts = swapped_parts(g_gate_up_parts, "dp")
    d_h2, out_part, *parts = lax.optimization_barrier(
        (d_h2, out_part, *g_gate_up_parts[:2], *g_down_parts)
    )
    g_gate_up_parts[:2] = parts[:2]
    g_down_parts = swapped_parts(parts[2:], "dp")

    d_resid = d_out + norm_pull(resid, resid_scale, ffn_full, d_h2.astype(F32))
    d_attn = lax.all_gather(d_resid.astype(BF), "ctx", axis=0, tiled=True)
    d_attn, *g_gate_up_parts = lax.optimization_barrier((d_attn, *g_gate_up_parts))
    out_sum = lax.psum_scatter(after(out_part, d_attn), "ctx", scatter_dimension=0, tiled=True)
    d_y = dot(d_attn, w_out_own, NT).astype(BF)
    g_gate_up = total_of(g_gate_up_parts).astype(BF)
    g_gate_up = spread(g_gate_up.reshape(ctxs, row_part, 2 * ff_local), "ctx")

    d_proj, d_beta, g_taps, g_gain_o = mix_backward(
        pre_low, gate_raw, beta_logit, d_y, core, states, inverses, taps, norm_o_full
    )

    def mix_part(place):
        h1_cols = lax.dynamic_slice_in_dim(h1_low, place * dp_rows, dp_rows, 1)
        return dot(h1_cols, d_proj, TN).astype(BF)

    g_mix_parts = shard_parts(mix_part, "dp")
    d_proj_later, *parts = lax.optimization_barrier(
        (d_proj, *g_mix_parts[:-1], *g_down_parts)
    )
    g_mix_parts = swapped_parts(parts[: dps - 1] + g_mix_parts[-1:], "dp")
    g_down_parts = parts[dps - 1 :]
    d_beta_low = jnp.pad(d_beta.astype(BF), ((0, 0), (0, 128 - heads)))
    d_h1_part = dot(jnp.concatenate([d_proj_later, d_beta_low], axis=1), w_mix, NT).astype(BF)
    d_h1_part, out_sum, g_gate_up, *g_mix_parts[:2] = lax.optimization_barrier(
        (d_h1_part, out_sum, g_gate_up, *g_mix_parts[:2])
    )
    block_out = (resid + out_sum.astype(F32)).astype(BF)[None]
    d_h1 = lax.psum_scatter(d_h1_part, "ctx", scatter_dimension=0, tiled=True).astype(F32)
    d_tokens = (d_resid + norm_pull(x_own, rms_scale(x_own), attn_full, d_h1))[None]

    taps_grad = jnp.zeros((ctxs, CONV, 3 * mix_width), F32)
    taps_grad = lax.dynamic_update_index_in_dim(taps_grad, g_taps[:CONV], ctx_place, 0)
    taps_grad = (
        taps_grad.reshape(head_dims[2], head_dims[0], CONV, 3, heads, HD)
        .transpose(2, 3, 1, 4, 0, 5)
        .reshape(CONV, devices, taps_part)
        .transpose(1, 0, 2)
        .reshape(width, taps_cols)
    )
    gain_grad = jnp.pad(g_gain_o[0].reshape(devices, gain_part), ((0, 0), (0, row_part - gain_part)))
    small_grad = jnp.concatenate(
        [jnp.zeros((width, heads), F32), gain_grad.reshape(width, 1), taps_grad], axis=1
    )
    small_grad = jnp.pad(small_grad, ((0, 0), (0, 128 - small_grad.shape[1])))
    small_grad = (small_grad + dot(h1_low, d_beta_low, TN)).astype(BF)
    small_grad = small_grad.reshape(dps, dp_rows, 128)

    def small_part(place):
        return lax.dynamic_index_in_dim(small_grad, place, 0, False)

    g_small = total_of(swapped_parts(shard_parts(small_part, "dp"), "dp")).astype(BF)
    g_small = spread(g_small.reshape(ctxs, row_part, 128), "ctx")
    g_out = dot(y_local, after(d_attn, *g_mix_parts[:2]), TN).astype(BF)
    g_w_out = total_of(row_owner_parts(g_out.reshape(dps, row_part, width)))
    g_w_down = total_of(g_down_parts)

    g_w_gate_up, ffn_sum = unpack_ff(g_gate_up, w_gate_up, dps)
    g_ffn_gain = ffn_sum[:, 0] / ffn_gain.astype(F32)
    g_mix = total_of(g_mix_parts).astype(BF)
    g_mix = spread(g_mix.reshape(ctxs, row_part, g_mix.shape[1]), "ctx")
    g_w_qkv, g_w_gate_o, g_w_beta, small_sum, attn_row_sum = unpack_mix(
        g_mix, g_small, w_qkv, w_gate_o, w_beta
    )
    g_attn_gain = attn_row_sum[:, 0] / attn_gain.astype(F32)
    g_norm_gain_o = small_sum[:gain_part, heads]
    g_conv = small_sum[:, heads + 1 : heads + 1 + taps_cols].reshape(CONV, taps_part)
    return (
        block_out,
        d_tokens,
        g_attn_gain,
        g_w_qkv,
        g_conv,
        g_w_beta,
        g_w_gate_o,
        g_norm_gain_o,
        g_w_out,
        g_ffn_gain,
        g_w_gate_up,
        g_w_down,
    )


def solution(mesh):
    rows = P(("dp", "ctx"), None)
    flat = P(("dp", "ctx"))
    taps = P(None, ("dp", "ctx"))
    acts = P("dp", "ctx", None)
    return jax.shard_map(
        per_device,
        mesh=mesh,
        in_specs=(
            acts, acts, P("dp"), P(), flat, rows, taps, rows, rows, flat, rows, flat, rows, rows
        ),
        out_specs=(acts, acts, flat, rows, taps, rows, rows, flat, rows, flat, rows, rows),
        check_vma=False,
    )
```

```python
import functools

import jax
import jax.numpy as jnp
from jax import lax
from jax.experimental import pallas as pl
from jax.experimental.layout import Layout, with_layout_constraint
from jax.experimental.pallas import tpu as pltpu
from jax.sharding import PartitionSpec as P

CONV = 4
HD = 128
CHUNK = 128
STEP = 512
SMALL = 64
EPS = 1e-05
KEY_EPS = 1e-06
BF = jnp.bfloat16
F32 = jnp.float32
NN = ((1,), (0,))
NT = ((1,), (1,))
TN = ((0,), (0,))


def mm(left, right, dims):
    return lax.dot_general(
        left.astype(BF), right.astype(BF), (dims, ((), ())), preferred_element_type=F32
    )


def halves(values):
    high = values.astype(BF)
    return high, (values - high.astype(F32)).astype(BF)


def mm_fine(left, right, dims):
    left_hi, left_lo = halves(left)
    right_hi, right_lo = halves(right)

    def product(a, b):
        return lax.dot_general(a, b, (dims, ((), ())), preferred_element_type=F32)

    return product(left_hi, right_hi) + (product(left_hi, right_lo) + product(left_lo, right_hi))


def sigmoid(values):
    return 1.0 / (1.0 + jnp.exp(-values))


def chunk_ids():
    row_ids = lax.broadcasted_iota(jnp.int32, (CHUNK, CHUNK), 0)
    col_ids = lax.broadcasted_iota(jnp.int32, (CHUNK, CHUNK), 1)
    return row_ids, col_ids


def lower_inverses(strict_parts):
    row_ids, col_ids = chunk_ids()
    results = None
    size = 1
    while size < CHUNK:
        pair_mask = (row_ids // (2 * size) == col_ids // (2 * size)) & (
            (row_ids // size) != (col_ids // size)
        )
        corners = [jnp.where(pair_mask, part, 0.0) for part in strict_parts]
        if results is None:
            ident = jnp.where(row_ids == col_ids, 1.0, 0.0)
            results = [ident - corner for corner in corners]
        else:
            moved = [mm_fine(corner, result, NN) for corner, result in zip(corners, results)]
            results = [result - mm_fine(result, part, NN) for result, part in zip(results, moved)]
        size *= 2
    return results


def conv_taps(extended, taps, extent):
    total = taps[0:1] * extended[5 : 5 + extent]
    for offset in range(1, CONV):
        total = total + taps[offset : offset + 1] * extended[5 + offset : 5 + offset + extent]
    return total


def unit_keys(raw):
    scale = lax.rsqrt(jnp.sum(raw * raw, axis=-1, keepdims=True) + KEY_EPS)
    return raw * scale, scale


def conv_inputs(first, second, width):
    pre = jnp.concatenate([first[:, : 2 * width], second[:, :width]], axis=1)
    return pre.astype(BF).astype(F32)


def mix_forward_kernel(
    first_ref, second_ref, taps_ref, gain_ref, y_ref, core_ref, state_ref, inverse_ref, state_now,
    rim, *, heads
):
    width = heads * HD
    step = first_ref.shape[0]
    chunks = step // CHUNK

    @pl.when(pl.program_id(0) == 0)
    def _():
        state_now[...] = jnp.zeros_like(state_now)
        rim[...] = jnp.zeros_like(rim)

    pre = conv_inputs(first_ref[...], second_ref[...], width)
    extended = jnp.concatenate([rim[...], pre], axis=0)
    rim[...] = pre[step - 8 :]
    conv = conv_taps(extended, taps_ref[...], step)
    mixture = conv * sigmoid(conv)
    beta = sigmoid(first_ref[:, 2 * width : 2 * width + heads])
    row_ids, col_ids = chunk_ids()
    tiles = [(chunk, head) for chunk in range(chunks) for head in range(heads)]
    q_t, k_t, v_t, b_t, score_t, strict_t = [], [], [], [], [], []
    for chunk, head in tiles:
        rows = slice(chunk * CHUNK, (chunk + 1) * CHUNK)
        q_rows = mixture[rows, head * HD : (head + 1) * HD]
        k_rows, _ = unit_keys(mixture[rows, width + head * HD : width + (head + 1) * HD])
        v_rows = mixture[rows, 2 * width + head * HD : 2 * width + (head + 1) * HD]
        b_rows = beta[rows, head : head + 1]
        q_t.append(q_rows)
        k_t.append(k_rows)
        v_t.append(v_rows)
        b_t.append(b_rows)
        score_t.append(jnp.where(row_ids >= col_ids, mm(q_rows, k_rows, NT), 0.0))
        strict_t.append(jnp.where(row_ids > col_ids, b_rows * mm_fine(k_rows, k_rows, NT), 0.0))
    inverse_t = lower_inverses(strict_t)
    w_t = [mm(t, b * k, NN) for t, b, k in zip(inverse_t, b_t, k_t)]
    u_t = [mm(t, b * v, NN) for t, b, v in zip(inverse_t, b_t, v_t)]
    for index, (chunk, head) in enumerate(tiles):
        rows = slice(chunk * CHUNK, (chunk + 1) * CHUNK)
        cols = slice(head * HD, (head + 1) * HD)
        state = state_now[head]
        state_ref[chunk, head] = state
        inverse_ref[chunk, head] = inverse_t[index]
        update = u_t[index] - mm(w_t[index], state, NN)
        core = mm(q_t[index], state, NN) + mm(score_t[index], update, NN)
        state_now[head] = state + mm(k_t[index], update, TN)
        core_ref[rows, cols] = core
        scale = lax.rsqrt(jnp.mean(core * core, axis=-1, keepdims=True) + EPS)
        gate = second_ref[rows, width + head * HD : width + (head + 1) * HD]
        y_ref[rows, cols] = (
            core * scale * gain_ref[...] * (gate * sigmoid(gate))
        ).astype(y_ref.dtype)


def mix_backward_kernel(
    first_ref, second_ref, first_before_ref, second_before_ref, dy_ref, core_ref, state_ref,
    inverse_ref, taps_ref, gain_ref, dproj_ref, dbeta_ref, gtaps_ref, ggain_ref, adjoint, rim, *, heads, blocks
):
    width = heads * HD
    step = first_ref.shape[0]
    chunks = step // CHUNK
    block = blocks - 1 - pl.program_id(0)

    @pl.when(pl.program_id(0) == 0)
    def _():
        adjoint[...] = jnp.zeros_like(adjoint)
        rim[...] = jnp.zeros_like(rim)
        gtaps_ref[...] = jnp.zeros_like(gtaps_ref)
        ggain_ref[...] = jnp.zeros_like(ggain_ref)

    before = conv_inputs(first_before_ref[...], second_before_ref[...], width)
    before = jnp.where(block > 0, before[before.shape[0] - 8 :], 0.0)
    extended = jnp.concatenate(
        [before, conv_inputs(first_ref[...], second_ref[...], width)], axis=0
    )
    taps = taps_ref[...]
    conv = conv_taps(extended, taps, step)
    conv_sig = sigmoid(conv)
    mixture = conv * conv_sig
    beta = sigmoid(first_ref[:, 2 * width : 2 * width + heads])
    gain = gain_ref[...]
    row_ids, col_ids = chunk_ids()
    causal, strict = row_ids >= col_ids, row_ids > col_ids
    tiles = [(chunk, head) for chunk in range(chunks) for head in range(heads)]
    held = {}
    ggain = jnp.zeros((1, HD), F32)
    for chunk, head in tiles:
        rows = slice(chunk * CHUNK, (chunk + 1) * CHUNK)
        cols = slice(head * HD, (head + 1) * HD)
        q_rows = mixture[rows, head * HD : (head + 1) * HD]
        k_rows, k_scale = unit_keys(mixture[rows, width + head * HD : width + (head + 1) * HD])
        v_rows = mixture[rows, 2 * width + head * HD : 2 * width + (head + 1) * HD]
        b_rows = beta[rows, head : head + 1]
        core = core_ref[rows, cols]
        scale = lax.rsqrt(jnp.mean(core * core, axis=-1, keepdims=True) + EPS)
        gate = second_ref[rows, width + head * HD : width + (head + 1) * HD]
        gate_sig = sigmoid(gate)
        dy = dy_ref[rows, cols].astype(F32)
        normed = core * scale
        ggain += jnp.sum(dy * (gate * gate_sig) * normed, axis=0, keepdims=True)
        dproj_ref[rows, 3 * width + head * HD : 3 * width + (head + 1) * HD] = (
            dy * normed * gain * (gate_sig * (1.0 + gate * (1.0 - gate_sig)))
        ).astype(dproj_ref.dtype)
        dnorm = dy * (gate * gate_sig) * gain
        dcore = scale * (dnorm - normed * jnp.mean(dnorm * normed, axis=-1, keepdims=True))
        state = state_ref[chunk, head]
        inverse = inverse_ref[chunk, head]
        scores = jnp.where(causal, mm(q_rows, k_rows, NT), 0.0)
        weighted = mm(inverse, b_rows * k_rows, NN)
        resid = v_rows - mm(k_rows, state, NN)
        update = mm(inverse, b_rows * resid, NN)
        dupdate = mm(scores, dcore, TN)
        dstate = mm(q_rows, dcore, TN)
        held[chunk, head] = [
            q_rows, k_rows, k_scale, b_rows, dcore, state, inverse, weighted, resid, update, dupdate,
            dstate
        ]
    later = {}
    for chunk in reversed(range(chunks)):
        for head in range(heads):
            entry = held[chunk, head]
            after = adjoint[head]
            later[chunk, head] = after
            entry[10] = entry[10] + mm(entry[1], after, NN)
            adjoint[head] = after + entry[11] - mm(entry[7], entry[10], TN)
    pieces = {}
    for chunk, head in tiles:
        (
            q_rows, k_rows, k_scale, b_rows, dcore, state, inverse, _, resid, update, dupdate, _
        ) = held[chunk, head]
        after = later[chunk, head]
        rows = slice(chunk * CHUNK, (chunk + 1) * CHUNK)
        dr = mm(inverse, dupdate, TN)
        dv = b_rows * dr
        dstrict = jnp.where(strict, -mm(dr, update, NT), 0.0)
        gram = mm(k_rows, k_rows, NT)
        dbeta = jnp.sum(dr * resid, axis=-1, keepdims=True) + jnp.sum(
            dstrict * gram, axis=-1, keepdims=True
        )
        dgram = b_rows * dstrict
        dscores = jnp.where(causal, mm(dcore, update, NT), 0.0)
        dq = mm(dcore, state, NT) + mm(dscores, k_rows, NN)
        dk = (
            mm(dscores, q_rows, TN)
            + mm(update, after, NT)
            - mm(dv, state, NT)
            + mm(dgram, k_rows, NN)
            + mm(dgram, k_rows, TN)
        )
        dkraw = k_scale * (dk - k_rows * jnp.sum(dk * k_rows, axis=-1, keepdims=True))
        pieces[0, head, chunk] = dq
        pieces[1, head, chunk] = dkraw
        pieces[2, head, chunk] = dv
        dbeta_ref[rows, head : head + 1] = dbeta * b_rows * (1.0 - b_rows)
    dmixture = jnp.concatenate(
        [
            jnp.concatenate([pieces[part, head, chunk] for chunk in range(chunks)], axis=0)
            for part in range(3)
            for head in range(heads)
        ],
        axis=1,
    )
    dconv = dmixture * (conv_sig * (1.0 + conv * (1.0 - conv_sig)))
    followed = jnp.concatenate([dconv, rim[...]], axis=0)
    rim[...] = dconv[:8]
    dpre = taps[CONV - 1 : CONV] * followed[0:step]
    for offset in range(CONV - 1):
        shift = CONV - 1 - offset
        dpre = dpre + taps[offset : offset + 1] * followed[shift : shift + step]
    dproj_ref[:, : 3 * width] = dpre.astype(dproj_ref.dtype)
    for offset in range(CONV):
        gtaps_ref[offset : offset + 1] += jnp.sum(
            dconv * extended[5 + offset : 5 + offset + step], axis=0, keepdims=True
        )
    ggain_ref[0:1] += ggain


def mix_forward(first, second, taps, gain):
    extent, width = first.shape[0], second.shape[1] // 2
    heads = width // HD
    step = min(STEP, extent)
    blocks, chunks = extent // step, step // CHUNK
    return pl.pallas_call(
        functools.partial(mix_forward_kernel, heads=heads),
        grid=(blocks,),
        in_specs=[
            pl.BlockSpec((step, first.shape[1]), lambda i: (i, 0)),
            pl.BlockSpec((step, 2 * width), lambda i: (i, 0)),
            pl.BlockSpec((8, 3 * width), lambda i: (0, 0)),
            pl.BlockSpec((1, HD), lambda i: (0, 0)),
        ],
        out_specs=[
            pl.BlockSpec((step, width), lambda i: (i, 0)),
            pl.BlockSpec((step, width), lambda i: (i, 0)),
            pl.BlockSpec((chunks, heads, HD, HD), lambda i: (i, 0, 0, 0)),
            pl.BlockSpec((chunks, heads, CHUNK, CHUNK), lambda i: (i, 0, 0, 0)),
        ],
        out_shape=[
            jax.ShapeDtypeStruct((extent, width), BF),
            jax.ShapeDtypeStruct((extent, width), F32),
            jax.ShapeDtypeStruct((extent // CHUNK, heads, HD, HD), F32),
            jax.ShapeDtypeStruct((extent // CHUNK, heads, CHUNK, CHUNK), F32),
        ],
        scratch_shapes=[pltpu.VMEM((heads, HD, HD), F32), pltpu.VMEM((8, 3 * width), F32)],
        compiler_params=pltpu.CompilerParams(
            dimension_semantics=("arbitrary",), vmem_limit_bytes=48 * 1024 * 1024
        ),
        cost_estimate=pl.CostEstimate(
            flops=90 * extent * width * CHUNK, bytes_accessed=40 * extent * width, transcendentals=0
        ),
        name="mix_forward",
    )(first, second, taps, gain)


def mix_backward(first, second, dy, core, states, inverses, taps, gain):
    extent, width = first.shape[0], second.shape[1] // 2
    width3 = 3 * width
    heads = width // HD
    step = min(STEP, extent)
    blocks, chunks = extent // step, step // CHUNK
    rows_before = 16

    def at(i):
        return (blocks - 1 - i, 0)

    def at_tiles(i):
        return (blocks - 1 - i, 0, 0, 0)

    def just_before(i):
        return (jnp.maximum((blocks - 1 - i) * (step // rows_before) - 1, 0), 0)

    return pl.pallas_call(
        functools.partial(mix_backward_kernel, heads=heads, blocks=blocks),
        grid=(blocks,),
        in_specs=[
            pl.BlockSpec((step, first.shape[1]), at),
            pl.BlockSpec((step, 2 * width), at),
            pl.BlockSpec((rows_before, first.shape[1]), just_before),
            pl.BlockSpec((rows_before, 2 * width), just_before),
            pl.BlockSpec((step, width), at),
            pl.BlockSpec((step, width), at),
            pl.BlockSpec((chunks, heads, HD, HD), at_tiles),
            pl.BlockSpec((chunks, heads, CHUNK, CHUNK), at_tiles),
            pl.BlockSpec((8, width3), lambda i: (0, 0)),
            pl.BlockSpec((1, HD), lambda i: (0, 0)),
        ],
        out_specs=[
            pl.BlockSpec((step, width3 + width), at),
            pl.BlockSpec((step, heads), at),
            pl.BlockSpec((8, width3), lambda i: (0, 0)),
            pl.BlockSpec((8, HD), lambda i: (0, 0)),
        ],
        out_shape=[
            jax.ShapeDtypeStruct((extent, width3 + width), BF),
            jax.ShapeDtypeStruct((extent, heads), F32),
            jax.ShapeDtypeStruct((8, width3), F32),
            jax.ShapeDtypeStruct((8, HD), F32),
        ],
        scratch_shapes=[pltpu.VMEM((heads, HD, HD), F32), pltpu.VMEM((8, width3), F32)],
        compiler_params=pltpu.CompilerParams(
            dimension_semantics=("arbitrary",), vmem_limit_bytes=48 * 1024 * 1024
        ),
        cost_estimate=pl.CostEstimate(
            flops=90 * extent * width * CHUNK, bytes_accessed=40 * extent * width, transcendentals=0
        ),
        name="mix_backward",
    )(first, second, first, second, dy, core, states, inverses, taps, gain)


def heads_of(ctx, ctxs, heads, row_part):
    blocks = HD // row_part
    groups = ctxs // blocks
    return [((ctx % blocks) * heads + slot) * groups + ctx // blocks for slot in range(heads)]


def pack_mix_kernel(
    qkv_ref, gate_ref, beta_ref, again_ref, fgain_ref, ogain_ref, taps_ref, first_ref, second_ref
):
    ctxs = first_ref.shape[0]
    rows, total = gate_ref.shape
    width = total // ctxs
    heads = beta_ref.shape[1] // ctxs
    row_ids = lax.broadcasted_iota(jnp.int32, (rows, SMALL), 0)

    def lanes(values):
        values = values.astype(F32)
        missing = SMALL - values.shape[1]
        if missing:
            values = jnp.concatenate([values, jnp.zeros((1, missing), F32)], axis=1)
        return values

    lines = [again_ref[...], fgain_ref[...], ogain_ref[...]]
    taps = taps_ref[...].astype(F32)
    for tap in range(CONV):
        for start in range(0, taps.shape[1], SMALL):
            lines.append(taps[tap : tap + 1, start : start + SMALL])
    small = jnp.zeros((rows, SMALL), F32)
    for row, line in enumerate(lines):
        small = jnp.where(row_ids == row, lanes(line), small)
    betas = beta_ref[...].astype(F32)
    for ctx in range(ctxs):
        own = []
        for slot, head in enumerate(heads_of(ctx, ctxs, heads, rows)):
            to, cols = slot * HD, slice(head * HD, (head + 1) * HD)
            for part in range(3):
                out_ref = second_ref if part == 2 else first_ref
                start = to + (width if part == 1 else 0)
                out_ref[ctx, :, start : start + HD] = qkv_ref[
                    :, part * total + head * HD : part * total + (head + 1) * HD
                ]
            second_ref[ctx, :, width + to : width + to + HD] = gate_ref[:, cols]
            own.append(betas[:, head : head + 1])
        own.append(jnp.zeros((rows, 128 - SMALL - heads), F32))
        first_ref[ctx, :, 2 * width :] = jnp.concatenate(own + [small], axis=1).astype(
            first_ref.dtype
        )


def pack_mix(w_qkv, w_gate_o, w_beta, attn_gain, ffn_gain, norm_gain_o, conv_weight, ctxs):
    rows, total = w_gate_o.shape
    width = total // ctxs
    return pl.pallas_call(
        pack_mix_kernel,
        out_shape=[
            jax.ShapeDtypeStruct((ctxs, rows, 2 * width + 128), w_qkv.dtype),
            jax.ShapeDtypeStruct((ctxs, rows, 2 * width), w_qkv.dtype),
        ],
        compiler_params=pltpu.CompilerParams(vmem_limit_bytes=48 * 1024 * 1024),
        name="pack_mix",
    )(
        w_qkv, w_gate_o, w_beta, attn_gain[None, :], ffn_gain[None, :], norm_gain_o[None, :],
        conv_weight,
    )


def read_small_kernel(
    in_ref, again_ref, fgain_ref, ogain_ref, taps_ref, all_taps, *, row_part, taps_part, gain_part
):
    values = in_ref[...].astype(F32)
    devices = values.shape[0] // row_part
    lines = -(-taps_part // SMALL)

    def line(row, size):
        starts = [device * row_part + row for device in range(devices)]
        return jnp.concatenate(
            [values[at : at + 1, 128 - SMALL : 128 - SMALL + size] for at in starts], axis=1
        )

    again_ref[...] = line(0, row_part)
    fgain_ref[...] = line(1, row_part)
    ogain_ref[...] = line(2, gain_part)
    for tap in range(CONV):
        pieces = []
        for device in range(devices):
            for index in range(lines):
                at = device * row_part + 3 + tap * lines + index
                size = min(SMALL, taps_part - index * SMALL)
                pieces.append(values[at : at + 1, 128 - SMALL : 128 - SMALL + size])
        all_taps[tap : tap + 1] = jnp.concatenate(pieces, axis=1)
    taps_ref[...] = jnp.zeros_like(taps_ref)
    total = all_taps.shape[1] // 3
    width = taps_ref.shape[1] // 3
    heads = width // HD
    ctxs = total // width
    ctx = lax.axis_index("ctx")
    blocks = HD // row_part
    for slot in range(heads):
        head = ((ctx % blocks) * heads + slot) * (ctxs // blocks) + ctx // blocks
        for part in range(3):
            start = pl.multiple_of(part * total + head * HD, HD)
            to = part * width + slot * HD
            taps_ref[0:CONV, to : to + HD] = all_taps[0:CONV, pl.ds(start, HD)]


def read_small(w_small, row_part, taps_part, gain_part, width):
    rows = w_small.shape[0]
    total = 3 * rows
    return pl.pallas_call(
        functools.partial(
            read_small_kernel, row_part=row_part, taps_part=taps_part, gain_part=gain_part
        ),
        out_shape=[
            jax.ShapeDtypeStruct((1, rows), F32),
            jax.ShapeDtypeStruct((1, rows), F32),
            jax.ShapeDtypeStruct((1, HD), F32),
            jax.ShapeDtypeStruct((8, 3 * width), F32),
        ],
        scratch_shapes=[pltpu.VMEM((8, total), F32)],
        compiler_params=pltpu.CompilerParams(vmem_limit_bytes=48 * 1024 * 1024),
        name="read_small",
    )(w_small)


def unpack_mix_kernel(
    in_ref, qkv_ref, gate_ref, beta_ref, gqkv_ref, ggate_ref, gbeta_ref, small_ref,
    rows_ref
):
    ctxs = in_ref.shape[0]
    rows, total = gate_ref.shape
    width = total // ctxs
    heads = gbeta_ref.shape[1] // ctxs
    row_sum = jnp.zeros(rows_ref.shape, F32)
    small_sum = jnp.zeros(small_ref.shape, F32)
    betas = [None] * (heads * ctxs)
    for ctx in range(ctxs):
        small = in_ref[ctx, :, 4 * width :].astype(F32)
        small_sum += small
        for slot, head in enumerate(heads_of(ctx, ctxs, heads, rows)):
            betas[head] = small[:, slot : slot + 1]
            for part in range(4):
                start = part * width + slot * HD
                grad = in_ref[ctx, :, start : start + HD].astype(F32)
                if part == 3:
                    cols = slice(head * HD, (head + 1) * HD)
                    ggate_ref[:, cols] = grad
                    weight = gate_ref[:, cols].astype(F32)
                else:
                    cols = slice(part * total + head * HD, part * total + (head + 1) * HD)
                    gqkv_ref[:, cols] = grad
                    weight = qkv_ref[:, cols].astype(F32)
                row_sum += jnp.sum(grad * weight, axis=1, keepdims=True)
    grad = jnp.concatenate(betas, axis=1)
    gbeta_ref[...] = grad
    small_ref[...] = small_sum
    rows_ref[...] = row_sum + jnp.sum(grad * beta_ref[...].astype(F32), axis=1, keepdims=True)


def unpack_mix(received, w_qkv, w_gate_o, w_beta):
    rows = w_qkv.shape[0]
    return pl.pallas_call(
        unpack_mix_kernel,
        out_shape=[
            jax.ShapeDtypeStruct(w_qkv.shape, F32),
            jax.ShapeDtypeStruct(w_gate_o.shape, F32),
            jax.ShapeDtypeStruct(w_beta.shape, F32),
            jax.ShapeDtypeStruct((rows, 128), F32),
            jax.ShapeDtypeStruct((rows, 1), F32),
        ],
        compiler_params=pltpu.CompilerParams(vmem_limit_bytes=48 * 1024 * 1024),
        name="unpack_mix",
    )(received, w_qkv, w_gate_o, w_beta)


def pack_ff_kernel(in_ref, out_ref, *, dps):
    ctxs = out_ref.shape[0]
    part = out_ref.shape[2] // (2 * dps)
    hidden = in_ref.shape[1] // 2
    for ctx in range(ctxs):
        starts = [
            side * hidden + (place * ctxs + ctx) * part for side in range(2) for place in range(dps)
        ]
        out_ref[ctx] = jnp.concatenate([in_ref[:, s : s + part] for s in starts], axis=1)


def pack_ff(w_gate_up, ctxs, dps):
    rows, total = w_gate_up.shape
    return pl.pallas_call(
        functools.partial(pack_ff_kernel, dps=dps),
        out_shape=jax.ShapeDtypeStruct((ctxs, rows, total // ctxs), w_gate_up.dtype),
        compiler_params=pltpu.CompilerParams(vmem_limit_bytes=48 * 1024 * 1024),
        name="pack_ff",
    )(w_gate_up)


def unpack_ff_kernel(in_ref, w_ref, out_ref, rows_ref, *, dps):
    ctxs = in_ref.shape[0]
    part = in_ref.shape[2] // (2 * dps)
    hidden = out_ref.shape[1] // 2
    row_sum = jnp.zeros(rows_ref.shape, F32)
    for side in range(2):
        pieces = []
        for place in range(dps):
            start = (side * dps + place) * part
            pieces.extend(in_ref[ctx, :, start : start + part] for ctx in range(ctxs))
        grad = jnp.concatenate(pieces, axis=1).astype(F32)
        cols = slice(side * hidden, (side + 1) * hidden)
        out_ref[:, cols] = grad
        row_sum += jnp.sum(grad * w_ref[:, cols].astype(F32), axis=1, keepdims=True)
    rows_ref[...] = row_sum


def unpack_ff(received, w_gate_up, dps):
    return pl.pallas_call(
        functools.partial(unpack_ff_kernel, dps=dps),
        out_shape=[
            jax.ShapeDtypeStruct(w_gate_up.shape, F32),
            jax.ShapeDtypeStruct((w_gate_up.shape[0], 1), F32),
        ],
        compiler_params=pltpu.CompilerParams(vmem_limit_bytes=48 * 1024 * 1024),
        name="unpack_ff",
    )(received, w_gate_up)


def dot(left, right, dims=NN):
    return lax.dot_general(left, right, (dims, ((), ())), preferred_element_type=F32)


def after(value, *others):
    return lax.optimization_barrier((value,) + others)[0]


def swapped(value, axis, distance):
    count = lax.axis_size(axis)
    return lax.ppermute(value, axis, [(i, i ^ distance) for i in range(count)])


def row_major(value):
    return with_layout_constraint(value, Layout(major_to_minor=tuple(range(value.ndim))))


def placed(parts, order):
    whole = row_major(jnp.zeros((len(parts),) + parts[0].shape, parts[0].dtype))
    for part, place in zip(parts, order):
        whole = lax.dynamic_update_index_in_dim(whole, part, place, 0)
    return row_major(lax.optimization_barrier(whole))


def shards_of(shard, axis):
    count = lax.axis_size(axis)
    return [shard] + [swapped(shard, axis, distance) for distance in range(1, count)]


def placed_shards(parts, axis):
    place = lax.axis_index(axis)
    return placed(parts, [place ^ distance for distance in range(len(parts))])


def gather_start(shard, axis):
    if lax.axis_size(axis) != 4:
        return shards_of(shard, axis)[1:]
    half = shard.shape[0] // 2
    return [swapped(shard[:half], axis, 1), swapped(shard[half:], axis, 2)]


def gather_end(shard, moved, axis):
    count, place = lax.axis_size(axis), lax.axis_index(axis)
    if count != 4:
        return placed_shards([shard] + moved, axis)
    half = shard.shape[0] // 2
    tops = swapped(jnp.stack([shard[:half], moved[0]]), axis, 2)
    ends = swapped(jnp.stack([shard[half:], moved[1]]), axis, 1)
    parts = [shard[:half], shard[half:], moved[0], moved[1], tops[0], ends[0], tops[1], ends[1]]
    order = [(0, 0), (0, 1), (1, 0), (2, 1), (2, 0), (1, 1), (3, 0), (3, 1)]
    whole = placed(parts, [2 * (place ^ distance) + side for distance, side in order])
    return whole.reshape((count,) + shard.shape)


def reduce_parts(part_of, axis):
    count, place = lax.axis_size(axis), lax.axis_index(axis)
    parts = [part_of(place ^ distance) for distance in range(count)]
    if count != 4:
        return parts[1:], parts[:1]
    half = parts[0].shape[0] // 2
    sent = [
        jnp.stack([parts[1][:half], parts[3][:half]]), jnp.stack([parts[2][half:], parts[3][half:]])
    ]
    return sent, [parts[0], parts[2][:half], parts[1][half:]]


def reduce_start(sent, axis):
    if lax.axis_size(axis) != 4:
        return [swapped(part, axis, index + 1) for index, part in enumerate(sent)]
    return [swapped(sent[0], axis, 1), swapped(sent[1], axis, 2)]


def reduce_end(moved, kept, axis):
    if lax.axis_size(axis) != 4:
        return total_of(moved + kept)
    own, top, end = kept
    half = own.shape[0] // 2
    top = swapped((top.astype(F32) + moved[0][1].astype(F32)).astype(BF), axis, 2)
    end = swapped((end.astype(F32) + moved[1][1].astype(F32)).astype(BF), axis, 1)
    top = total_of([moved[0][0], top, own[:half]])
    end = total_of([moved[1][0], end, own[half:]])
    return jnp.concatenate([top, end], axis=0)


def shard_parts(part_of, axis):
    count, place = lax.axis_size(axis), lax.axis_index(axis)
    sent = [part_of(place ^ distance) for distance in range(1, count)]
    return sent + [part_of(place)]


def swapped_parts(parts, axis):
    return [swapped(part, axis, index + 1) for index, part in enumerate(parts[:-1])] + parts[-1:]


def total_of(parts):
    total = parts[-1].astype(F32)
    for part in parts[:-1]:
        total = total + part.astype(F32)
    return total


def head_routes(row_part, turn):
    dps, ctxs = lax.axis_size("dp"), lax.axis_size("ctx")
    blocks = HD // row_part
    heads = dps // blocks
    routes = []
    for dp in range(dps):
        for ctx in range(ctxs):
            place = (dp % heads) * blocks + ctx % blocks
            user = (ctx // blocks) * blocks + dp // heads
            routes.append((dp * ctxs + ctx, (place ^ turn) * ctxs + user))
    return routes


def head_owner_parts(rows):
    turns = range(lax.axis_size("dp"))
    return [lax.ppermute(rows, ("dp", "ctx"), head_routes(rows.shape[0], turn)) for turn in turns]


def row_owner_parts(blocks):
    place = lax.axis_index("dp")
    parts = []
    for turn in range(lax.axis_size("dp")):
        routes = [(user, owner) for owner, user in head_routes(blocks.shape[1], turn)]
        block = lax.dynamic_index_in_dim(blocks, place ^ turn, 0, False)
        parts.append(lax.ppermute(block, ("dp", "ctx"), routes))
    return parts


def spread(value, axis):
    return lax.all_to_all(value, axis, 0, 0, tiled=True)


def rms_scale(values):
    return lax.rsqrt(jnp.mean(values * values, axis=-1, keepdims=True) + EPS)


def norm_pull(values, scale, gain, grad):
    weighted = grad * gain
    return scale * weighted - values * (
        scale * scale * scale * jnp.mean(weighted * values, axis=-1, keepdims=True)
    )


def per_device(
    tokens,
    cotangent,
    group_ids,
    group_scale,
    attn_gain,
    w_qkv,
    conv_weight,
    w_beta,
    w_gate_o,
    norm_gain_o,
    w_out,
    ffn_gain,
    w_gate_up,
    w_down,
):
    seg_len, width = tokens.shape[1:]
    dps, ctxs = lax.axis_size("dp"), lax.axis_size("ctx")
    devices = dps * ctxs
    ctx_place = lax.axis_index("ctx")
    head_count = w_beta.shape[1]
    heads = head_count // ctxs
    mix_width = heads * HD
    row_part = w_qkv.shape[0]
    dp_rows = ctxs * row_part
    ff_part = w_down.shape[0]
    ff_local = dps * ff_part
    taps_part = conv_weight.shape[1]
    taps_cols = CONV * taps_part // row_part
    gain_part = norm_gain_o.shape[0]
    head_dims = (HD // row_part, heads, ctxs * row_part // HD)

    x_full = lax.all_gather(tokens[0], "ctx", axis=0, tiled=True)
    matches = group_ids[:, None] == lax.broadcasted_iota(
        jnp.int32, (group_ids.shape[0], group_scale.shape[0]), 1
    )
    seq_scale = jnp.sum(jnp.where(matches, group_scale[None, :], 0.0), axis=1)
    d_out = cotangent[0].astype(F32) * seq_scale[0]
    d_out_full = lax.all_gather(after(d_out.astype(BF), x_full), "ctx", axis=0, tiled=True)
    first_rows, second_rows = pack_mix(
        w_qkv, w_gate_o, w_beta, attn_gain, ffn_gain, norm_gain_o, conv_weight, ctxs
    )
    first_half = spread(first_rows, "ctx").reshape(dp_rows, first_rows.shape[2])
    down_parts = shards_of(w_down, "dp")
    first_half, *down_parts = lax.optimization_barrier((first_half, *down_parts))
    second_half = spread(after(second_rows, first_half), "ctx").reshape(dp_rows, 2 * mix_width)
    first_parts = shards_of(first_half, "dp")
    second_half, *first_parts[1:3] = lax.optimization_barrier((second_half, *first_parts[1:3]))
    second_parts = shards_of(second_half, "dp")
    gate_up_rows = pack_ff(w_gate_up, ctxs, dps)
    gate_up_half = spread(after(gate_up_rows, second_half), "ctx").reshape(dp_rows, 2 * ff_local)

    x_rows = x_full.astype(F32)
    x_scale = rms_scale(x_rows)
    x_scale, *first_parts = lax.optimization_barrier((x_scale, *first_parts))
    w_first = placed_shards(first_parts, "dp").reshape(width, first_rows.shape[2])
    w_small = lax.optimization_barrier(w_first[:, 2 * mix_width :])
    attn_full, ffn_full, norm_o_full, taps = read_small(
        w_small, row_part, taps_part, gain_part, mix_width
    )

    h1_low = (x_rows * x_scale * attn_full).astype(BF)
    first = dot(h1_low, w_first)
    first, taps, *second_parts = lax.optimization_barrier((first, taps, *second_parts))
    w_second = placed_shards(second_parts, "dp").reshape(width, 2 * mix_width)
    second = dot(h1_low, w_second)
    out_parts = head_owner_parts(after(w_out, *second_parts))
    y_local, core, states, inverses = mix_forward(first, second, taps, norm_o_full)
    y_local, d_out_full, gate_up_half, *out_parts = lax.optimization_barrier(
        (y_local, d_out_full, gate_up_half, *out_parts)
    )
    gate_up_moved = gather_start(gate_up_half, "dp")
    w_dn = placed_shards(down_parts, "dp").reshape(ff_local, width)
    w_out_own = placed_shards(out_parts, "dp").reshape(mix_width, width)
    attn_part = dot(y_local, w_out_own).astype(BF)
    attn_sum = lax.psum_scatter(attn_part, "ctx", scatter_dimension=0, tiled=True)

    x_own = tokens[0].astype(F32)
    w_mix = jnp.concatenate([w_first[:, : 2 * mix_width], w_second, w_small], axis=1)
    attn_sum, gate_up_moved, w_dn, w_mix = lax.optimization_barrier(
        (attn_sum, gate_up_moved, w_dn, w_mix)
    )
    resid = x_own + attn_sum.astype(F32)
    resid_scale = rms_scale(resid)
    h2_own = (resid * resid_scale * ffn_full).astype(BF)
    h2_low = lax.all_gather(h2_own, "ctx", axis=0, tiled=True)

    w_gu = gather_end(gate_up_half, gate_up_moved, "dp").reshape(width, 2 * ff_local)
    gate_up = dot(h2_low, w_gu)
    gate, up = gate_up[:, :ff_local], gate_up[:, ff_local:]
    gate_sig = jax.nn.sigmoid(gate)
    hidden_low = (gate * gate_sig * up).astype(BF)
    d_hidden = dot(d_out_full, w_dn, NT).astype(BF).astype(F32)
    d_gate_up = jnp.concatenate(
        [
            (d_hidden * up * (gate_sig * (1.0 + gate * (1.0 - gate_sig)))).astype(BF),
            (d_hidden * (gate * gate_sig)).astype(BF),
        ],
        axis=1,
    )
    d_h2_part = dot(d_gate_up, w_gu, NT).astype(BF)
    d_h2 = lax.psum_scatter(d_h2_part, "ctx", scatter_dimension=0, tiled=True)
    hidden_later, d_gate_up_later = lax.optimization_barrier((hidden_low, d_gate_up, d_h2_part))[:2]
    out_part = dot(hidden_later, w_dn).astype(BF)

    def down_part(place):
        hidden_cols = lax.dynamic_slice_in_dim(hidden_later, place * ff_part, ff_part, 1)
        return dot(hidden_cols, d_out_full, TN).astype(BF)

    def gate_up_part(place):
        h2_cols = lax.dynamic_slice_in_dim(h2_low, place * dp_rows, dp_rows, 1)
        return dot(h2_cols, d_gate_up_later, TN).astype(BF)

    g_gate_up_sent, g_gate_up_kept = reduce_parts(gate_up_part, "dp")
    g_down_parts = shard_parts(down_part, "dp")
    g_gate_up_moved = reduce_start(g_gate_up_sent, "dp")
    d_h2, out_part, g_gate_up_moved, *g_down_parts = lax.optimization_barrier(
        (d_h2, out_part, g_gate_up_moved, *g_down_parts)
    )
    g_down_parts = swapped_parts(g_down_parts, "dp")

    d_resid = d_out + norm_pull(resid, resid_scale, ffn_full, d_h2.astype(F32))
    d_attn = lax.all_gather(d_resid.astype(BF), "ctx", axis=0, tiled=True)
    g_gate_up = reduce_end(g_gate_up_moved, g_gate_up_kept, "dp").astype(BF)
    d_attn, g_gate_up = lax.optimization_barrier((d_attn, g_gate_up))
    out_sum = lax.psum_scatter(after(out_part, d_attn), "ctx", scatter_dimension=0, tiled=True)
    d_y = dot(d_attn, w_out_own, NT).astype(BF)
    g_gate_up = spread(g_gate_up.reshape(ctxs, row_part, 2 * ff_local), "ctx")

    d_proj, d_beta, g_taps, g_gain_o = mix_backward(
        first, second, d_y, core, states, inverses, taps, norm_o_full
    )

    def mix_part(place):
        h1_cols = lax.dynamic_slice_in_dim(h1_low, place * dp_rows, dp_rows, 1)
        return dot(h1_cols, d_proj, TN).astype(BF)

    g_mix_sent, g_mix_kept = reduce_parts(mix_part, "dp")
    d_proj_later, g_mix_sent, *g_down_parts = lax.optimization_barrier(
        (d_proj, g_mix_sent, *g_down_parts)
    )
    g_mix_moved = reduce_start(g_mix_sent, "dp")
    d_beta_low = jnp.pad(d_beta.astype(BF), ((0, 0), (0, 128 - heads)))
    d_h1_part = dot(jnp.concatenate([d_proj_later, d_beta_low], axis=1), w_mix, NT).astype(BF)
    d_h1_part, out_sum, g_gate_up, g_mix_moved = lax.optimization_barrier(
        (d_h1_part, out_sum, g_gate_up, g_mix_moved)
    )
    block_out = (resid + out_sum.astype(F32)).astype(BF)[None]
    d_h1 = lax.psum_scatter(d_h1_part, "ctx", scatter_dimension=0, tiled=True).astype(F32)
    d_tokens = (d_resid + norm_pull(x_own, rms_scale(x_own), attn_full, d_h1))[None]

    taps_grad = jnp.zeros((ctxs, CONV, 3 * mix_width), F32)
    taps_grad = lax.dynamic_update_index_in_dim(taps_grad, g_taps[:CONV], ctx_place, 0)
    taps_grad = (
        taps_grad.reshape(head_dims[2], head_dims[0], CONV, 3, heads, HD)
        .transpose(2, 3, 1, 4, 0, 5)
        .reshape(CONV, devices, taps_part)
        .transpose(1, 0, 2)
        .reshape(width, taps_cols)
    )
    gain_grad = jnp.pad(g_gain_o[0].reshape(devices, gain_part), ((0, 0), (0, row_part - gain_part)))
    small_grad = jnp.concatenate(
        [jnp.zeros((width, heads), F32), gain_grad.reshape(width, 1), taps_grad], axis=1
    )
    small_grad = jnp.pad(small_grad, ((0, 0), (0, 128 - small_grad.shape[1])))
    small_grad = (small_grad + dot(h1_low, d_beta_low, TN)).astype(BF)
    small_grad = small_grad.reshape(dps, dp_rows, 128)

    def small_part(place):
        return lax.dynamic_index_in_dim(small_grad, place, 0, False)

    g_small = total_of(swapped_parts(shard_parts(small_part, "dp"), "dp")).astype(BF)
    g_mix = reduce_end(g_mix_moved, g_mix_kept, "dp").astype(BF)
    g_mix = jnp.concatenate([g_mix, g_small], axis=1)
    g_out = dot(y_local, after(d_attn, g_mix), TN).astype(BF)
    g_w_out = total_of(row_owner_parts(g_out.reshape(dps, row_part, width)))
    g_w_down = total_of(g_down_parts)

    g_w_gate_up, ffn_sum = unpack_ff(g_gate_up, w_gate_up, dps)
    g_ffn_gain = ffn_sum[:, 0] / ffn_gain.astype(F32)
    g_mix = spread(g_mix.reshape(ctxs, row_part, g_mix.shape[1]), "ctx")
    g_mix, d_tokens, g_w_gate_up, g_w_down, g_w_out = lax.optimization_barrier(
        (g_mix, d_tokens, g_w_gate_up, g_w_down, g_w_out)
    )
    g_w_qkv, g_w_gate_o, g_w_beta, small_sum, attn_row_sum = unpack_mix(
        g_mix, w_qkv, w_gate_o, w_beta
    )
    g_attn_gain = attn_row_sum[:, 0] / attn_gain.astype(F32)
    g_norm_gain_o = small_sum[:gain_part, heads]
    g_conv = small_sum[:, heads + 1 : heads + 1 + taps_cols].reshape(CONV, taps_part)
    return (
        block_out,
        d_tokens,
        g_attn_gain,
        g_w_qkv,
        g_conv,
        g_w_beta,
        g_w_gate_o,
        g_norm_gain_o,
        g_w_out,
        g_ffn_gain,
        g_w_gate_up,
        g_w_down,
    )


def solution(mesh):
    rows = P(("dp", "ctx"), None)
    flat = P(("dp", "ctx"))
    taps = P(None, ("dp", "ctx"))
    acts = P("dp", "ctx", None)
    return jax.shard_map(
        per_device,
        mesh=mesh,
        in_specs=(
            acts, acts, P("dp"), P(), flat, rows, taps, rows, rows, flat, rows, flat, rows, rows
        ),
        out_specs=(acts, acts, flat, rows, taps, rows, rows, flat, rows, flat, rows, rows),
        check_vma=False,
    )
```

```python
import functools

import jax
import jax.numpy as jnp
from jax import lax
from jax.experimental import pallas as pl
from jax.experimental.layout import Layout, with_layout_constraint
from jax.experimental.pallas import tpu as pltpu
from jax.sharding import PartitionSpec as P

CONV = 4
HD = 128
CHUNK = 128
STEP = 512
SMALL = 64
FF_STEP = 256
EPS = 1e-05
KEY_EPS = 1e-06
BF = jnp.bfloat16
F32 = jnp.float32
NN = ((1,), (0,))
NT = ((1,), (1,))
TN = ((0,), (0,))


def mm(left, right, dims):
    return lax.dot_general(
        left.astype(BF), right.astype(BF), (dims, ((), ())), preferred_element_type=F32
    )


def halves(values):
    high = values.astype(BF)
    return high, (values - high.astype(F32)).astype(BF)


def mm_fine(left, right, dims):
    left_hi, left_lo = halves(left)
    right_hi, right_lo = halves(right)

    def product(a, b):
        return lax.dot_general(a, b, (dims, ((), ())), preferred_element_type=F32)

    return product(left_hi, right_hi) + (product(left_hi, right_lo) + product(left_lo, right_hi))


def sigmoid(values):
    return 1.0 / (1.0 + jnp.exp(-values))


def chunk_ids():
    row_ids = lax.broadcasted_iota(jnp.int32, (CHUNK, CHUNK), 0)
    col_ids = lax.broadcasted_iota(jnp.int32, (CHUNK, CHUNK), 1)
    return row_ids, col_ids


def lower_inverses(strict_parts):
    row_ids, col_ids = chunk_ids()
    results = None
    size = 1
    while size < CHUNK:
        pair_mask = (row_ids // (2 * size) == col_ids // (2 * size)) & (
            (row_ids // size) != (col_ids // size)
        )
        corners = [jnp.where(pair_mask, part, 0.0) for part in strict_parts]
        if results is None:
            ident = jnp.where(row_ids == col_ids, 1.0, 0.0)
            results = [ident - corner for corner in corners]
        else:
            moved = [mm_fine(corner, result, NN) for corner, result in zip(corners, results)]
            results = [result - mm_fine(result, part, NN) for result, part in zip(results, moved)]
        size *= 2
    return results


def conv_taps(extended, taps, extent):
    total = taps[0:1] * extended[5 : 5 + extent]
    for offset in range(1, CONV):
        total = total + taps[offset : offset + 1] * extended[5 + offset : 5 + offset + extent]
    return total


def unit_keys(raw):
    scale = lax.rsqrt(jnp.sum(raw * raw, axis=-1, keepdims=True) + KEY_EPS)
    return raw * scale, scale


def conv_inputs(first, second, width):
    pre = jnp.concatenate([first[:, : 2 * width], second[:, :width]], axis=1)
    return pre.astype(BF).astype(F32)


def mix_forward_kernel(
    first_ref, second_ref, taps_ref, gain_ref, y_ref, core_ref, state_ref, inverse_ref, state_now,
    rim, *, heads
):
    width = heads * HD
    step = first_ref.shape[0]
    chunks = step // CHUNK

    @pl.when(pl.program_id(0) == 0)
    def _():
        state_now[...] = jnp.zeros_like(state_now)
        rim[...] = jnp.zeros_like(rim)

    pre = conv_inputs(first_ref[...], second_ref[...], width)
    extended = jnp.concatenate([rim[...], pre], axis=0)
    rim[...] = pre[step - 8 :]
    conv = conv_taps(extended, taps_ref[...], step)
    mixture = conv * sigmoid(conv)
    beta = sigmoid(first_ref[:, 2 * width : 2 * width + heads])
    row_ids, col_ids = chunk_ids()
    tiles = [(chunk, head) for chunk in range(chunks) for head in range(heads)]
    q_t, k_t, v_t, b_t, score_t, strict_t = [], [], [], [], [], []
    for chunk, head in tiles:
        rows = slice(chunk * CHUNK, (chunk + 1) * CHUNK)
        q_rows = mixture[rows, head * HD : (head + 1) * HD]
        k_rows, _ = unit_keys(mixture[rows, width + head * HD : width + (head + 1) * HD])
        v_rows = mixture[rows, 2 * width + head * HD : 2 * width + (head + 1) * HD]
        b_rows = beta[rows, head : head + 1]
        q_t.append(q_rows)
        k_t.append(k_rows)
        v_t.append(v_rows)
        b_t.append(b_rows)
        score_t.append(jnp.where(row_ids >= col_ids, mm(q_rows, k_rows, NT), 0.0))
        strict_t.append(jnp.where(row_ids > col_ids, b_rows * mm_fine(k_rows, k_rows, NT), 0.0))
    inverse_t = lower_inverses(strict_t)
    w_t = [mm(t, b * k, NN) for t, b, k in zip(inverse_t, b_t, k_t)]
    u_t = [mm(t, b * v, NN) for t, b, v in zip(inverse_t, b_t, v_t)]
    for index, (chunk, head) in enumerate(tiles):
        rows = slice(chunk * CHUNK, (chunk + 1) * CHUNK)
        cols = slice(head * HD, (head + 1) * HD)
        state = state_now[head]
        state_ref[chunk, head] = state
        inverse_ref[chunk, head] = inverse_t[index]
        update = u_t[index] - mm(w_t[index], state, NN)
        core = mm(q_t[index], state, NN) + mm(score_t[index], update, NN)
        state_now[head] = state + mm(k_t[index], update, TN)
        core_ref[rows, cols] = core
        scale = lax.rsqrt(jnp.mean(core * core, axis=-1, keepdims=True) + EPS)
        gate = second_ref[rows, width + head * HD : width + (head + 1) * HD]
        y_ref[rows, cols] = (
            core * scale * gain_ref[...] * (gate * sigmoid(gate))
        ).astype(y_ref.dtype)


def mix_backward_kernel(
    first_ref, second_ref, first_before_ref, second_before_ref, dy_ref, core_ref, state_ref,
    inverse_ref, taps_ref, gain_ref, dproj_ref, dbeta_ref, gtaps_ref, ggain_ref, adjoint, rim, *, heads, blocks
):
    width = heads * HD
    step = first_ref.shape[0]
    chunks = step // CHUNK
    block = blocks - 1 - pl.program_id(0)

    @pl.when(pl.program_id(0) == 0)
    def _():
        adjoint[...] = jnp.zeros_like(adjoint)
        rim[...] = jnp.zeros_like(rim)
        gtaps_ref[...] = jnp.zeros_like(gtaps_ref)
        ggain_ref[...] = jnp.zeros_like(ggain_ref)

    before = conv_inputs(first_before_ref[...], second_before_ref[...], width)
    before = jnp.where(block > 0, before[before.shape[0] - 8 :], 0.0)
    extended = jnp.concatenate(
        [before, conv_inputs(first_ref[...], second_ref[...], width)], axis=0
    )
    taps = taps_ref[...]
    conv = conv_taps(extended, taps, step)
    conv_sig = sigmoid(conv)
    mixture = conv * conv_sig
    beta = sigmoid(first_ref[:, 2 * width : 2 * width + heads])
    gain = gain_ref[...]
    row_ids, col_ids = chunk_ids()
    causal, strict = row_ids >= col_ids, row_ids > col_ids
    tiles = [(chunk, head) for chunk in range(chunks) for head in range(heads)]
    held = {}
    ggain = jnp.zeros((1, HD), F32)
    for chunk, head in tiles:
        rows = slice(chunk * CHUNK, (chunk + 1) * CHUNK)
        cols = slice(head * HD, (head + 1) * HD)
        q_rows = mixture[rows, head * HD : (head + 1) * HD]
        k_rows, k_scale = unit_keys(mixture[rows, width + head * HD : width + (head + 1) * HD])
        v_rows = mixture[rows, 2 * width + head * HD : 2 * width + (head + 1) * HD]
        b_rows = beta[rows, head : head + 1]
        core = core_ref[rows, cols]
        scale = lax.rsqrt(jnp.mean(core * core, axis=-1, keepdims=True) + EPS)
        gate = second_ref[rows, width + head * HD : width + (head + 1) * HD]
        gate_sig = sigmoid(gate)
        dy = dy_ref[rows, cols].astype(F32)
        normed = core * scale
        ggain += jnp.sum(dy * (gate * gate_sig) * normed, axis=0, keepdims=True)
        dproj_ref[rows, 3 * width + head * HD : 3 * width + (head + 1) * HD] = (
            dy * normed * gain * (gate_sig * (1.0 + gate * (1.0 - gate_sig)))
        ).astype(dproj_ref.dtype)
        dnorm = dy * (gate * gate_sig) * gain
        dcore = scale * (dnorm - normed * jnp.mean(dnorm * normed, axis=-1, keepdims=True))
        state = state_ref[chunk, head]
        inverse = inverse_ref[chunk, head]
        scores = jnp.where(causal, mm(q_rows, k_rows, NT), 0.0)
        weighted = mm(inverse, b_rows * k_rows, NN)
        resid = v_rows - mm(k_rows, state, NN)
        update = mm(inverse, b_rows * resid, NN)
        dupdate = mm(scores, dcore, TN)
        dstate = mm(q_rows, dcore, TN)
        held[chunk, head] = [
            q_rows, k_rows, k_scale, b_rows, dcore, state, inverse, weighted, resid, update, dupdate,
            dstate
        ]
    later = {}
    for chunk in reversed(range(chunks)):
        for head in range(heads):
            entry = held[chunk, head]
            after = adjoint[head]
            later[chunk, head] = after
            entry[10] = entry[10] + mm(entry[1], after, NN)
            adjoint[head] = after + entry[11] - mm(entry[7], entry[10], TN)
    pieces = {}
    for chunk, head in tiles:
        (
            q_rows, k_rows, k_scale, b_rows, dcore, state, inverse, _, resid, update, dupdate, _
        ) = held[chunk, head]
        after = later[chunk, head]
        rows = slice(chunk * CHUNK, (chunk + 1) * CHUNK)
        dr = mm(inverse, dupdate, TN)
        dv = b_rows * dr
        dstrict = jnp.where(strict, -mm(dr, update, NT), 0.0)
        gram = mm(k_rows, k_rows, NT)
        dbeta = jnp.sum(dr * resid, axis=-1, keepdims=True) + jnp.sum(
            dstrict * gram, axis=-1, keepdims=True
        )
        dgram = b_rows * dstrict
        dscores = jnp.where(causal, mm(dcore, update, NT), 0.0)
        dq = mm(dcore, state, NT) + mm(dscores, k_rows, NN)
        dk = (
            mm(dscores, q_rows, TN)
            + mm(update, after, NT)
            - mm(dv, state, NT)
            + mm(dgram, k_rows, NN)
            + mm(dgram, k_rows, TN)
        )
        dkraw = k_scale * (dk - k_rows * jnp.sum(dk * k_rows, axis=-1, keepdims=True))
        pieces[0, head, chunk] = dq
        pieces[1, head, chunk] = dkraw
        pieces[2, head, chunk] = dv
        dbeta_ref[rows, head : head + 1] = dbeta * b_rows * (1.0 - b_rows)
    dmixture = jnp.concatenate(
        [
            jnp.concatenate([pieces[part, head, chunk] for chunk in range(chunks)], axis=0)
            for part in range(3)
            for head in range(heads)
        ],
        axis=1,
    )
    dconv = dmixture * (conv_sig * (1.0 + conv * (1.0 - conv_sig)))
    followed = jnp.concatenate([dconv, rim[...]], axis=0)
    rim[...] = dconv[:8]
    dpre = taps[CONV - 1 : CONV] * followed[0:step]
    for offset in range(CONV - 1):
        shift = CONV - 1 - offset
        dpre = dpre + taps[offset : offset + 1] * followed[shift : shift + step]
    dproj_ref[:, : 3 * width] = dpre.astype(dproj_ref.dtype)
    for offset in range(CONV):
        gtaps_ref[offset : offset + 1] += jnp.sum(
            dconv * extended[5 + offset : 5 + offset + step], axis=0, keepdims=True
        )
    ggain_ref[0:1] += ggain


def mix_forward(first, second, taps, gain):
    extent, width = first.shape[0], second.shape[1] // 2
    heads = width // HD
    step = min(STEP, extent)
    blocks, chunks = extent // step, step // CHUNK
    return pl.pallas_call(
        functools.partial(mix_forward_kernel, heads=heads),
        grid=(blocks,),
        in_specs=[
            pl.BlockSpec((step, first.shape[1]), lambda i: (i, 0)),
            pl.BlockSpec((step, 2 * width), lambda i: (i, 0)),
            pl.BlockSpec((8, 3 * width), lambda i: (0, 0)),
            pl.BlockSpec((1, HD), lambda i: (0, 0)),
        ],
        out_specs=[
            pl.BlockSpec((step, width), lambda i: (i, 0)),
            pl.BlockSpec((step, width), lambda i: (i, 0)),
            pl.BlockSpec((chunks, heads, HD, HD), lambda i: (i, 0, 0, 0)),
            pl.BlockSpec((chunks, heads, CHUNK, CHUNK), lambda i: (i, 0, 0, 0)),
        ],
        out_shape=[
            jax.ShapeDtypeStruct((extent, width), BF),
            pltpu.HBM((extent, width), F32),
            pltpu.HBM((extent // CHUNK, heads, HD, HD), F32),
            pltpu.HBM((extent // CHUNK, heads, CHUNK, CHUNK), F32),
        ],
        scratch_shapes=[pltpu.VMEM((heads, HD, HD), F32), pltpu.VMEM((8, 3 * width), F32)],
        compiler_params=pltpu.CompilerParams(
            dimension_semantics=("arbitrary",), vmem_limit_bytes=48 * 1024 * 1024
        ),
        cost_estimate=pl.CostEstimate(
            flops=90 * extent * width * CHUNK, bytes_accessed=40 * extent * width, transcendentals=0
        ),
        name="mix_forward",
    )(first, second, taps, gain)


def mix_backward(first, second, dy, core, states, inverses, taps, gain):
    extent, width = first.shape[0], second.shape[1] // 2
    width3 = 3 * width
    heads = width // HD
    step = min(STEP, extent)
    blocks, chunks = extent // step, step // CHUNK
    rows_before = 16

    def at(i):
        return (blocks - 1 - i, 0)

    def at_tiles(i):
        return (blocks - 1 - i, 0, 0, 0)

    def just_before(i):
        return (jnp.maximum((blocks - 1 - i) * (step // rows_before) - 1, 0), 0)

    return pl.pallas_call(
        functools.partial(mix_backward_kernel, heads=heads, blocks=blocks),
        grid=(blocks,),
        in_specs=[
            pl.BlockSpec((step, first.shape[1]), at),
            pl.BlockSpec((step, 2 * width), at),
            pl.BlockSpec((rows_before, first.shape[1]), just_before),
            pl.BlockSpec((rows_before, 2 * width), just_before),
            pl.BlockSpec((step, width), at),
            pl.BlockSpec((step, width), at),
            pl.BlockSpec((chunks, heads, HD, HD), at_tiles),
            pl.BlockSpec((chunks, heads, CHUNK, CHUNK), at_tiles),
            pl.BlockSpec((8, width3), lambda i: (0, 0)),
            pl.BlockSpec((1, HD), lambda i: (0, 0)),
        ],
        out_specs=[
            pl.BlockSpec((step, width3 + width), at),
            pl.BlockSpec((step, heads), at),
            pl.BlockSpec((8, width3), lambda i: (0, 0)),
            pl.BlockSpec((8, HD), lambda i: (0, 0)),
        ],
        out_shape=[
            jax.ShapeDtypeStruct((extent, width3 + width), BF),
            jax.ShapeDtypeStruct((extent, heads), F32),
            jax.ShapeDtypeStruct((8, width3), F32),
            jax.ShapeDtypeStruct((8, HD), F32),
        ],
        scratch_shapes=[pltpu.VMEM((heads, HD, HD), F32), pltpu.VMEM((8, width3), F32)],
        compiler_params=pltpu.CompilerParams(
            dimension_semantics=("arbitrary",), vmem_limit_bytes=48 * 1024 * 1024
        ),
        cost_estimate=pl.CostEstimate(
            flops=90 * extent * width * CHUNK, bytes_accessed=40 * extent * width, transcendentals=0
        ),
        name="mix_backward",
    )(first, second, first, second, dy, core, states, inverses, taps, gain)


def heads_of(ctx, ctxs, heads, row_part):
    blocks = HD // row_part
    groups = ctxs // blocks
    return [((ctx % blocks) * heads + slot) * groups + ctx // blocks for slot in range(heads)]


def pack_mix_kernel(
    qkv_ref, gate_ref, beta_ref, again_ref, fgain_ref, ogain_ref, taps_ref, first_ref, second_ref
):
    ctxs = first_ref.shape[0]
    rows, total = gate_ref.shape
    width = total // ctxs
    heads = beta_ref.shape[1] // ctxs
    row_ids = lax.broadcasted_iota(jnp.int32, (rows, SMALL), 0)

    def lanes(values):
        values = values.astype(F32)
        missing = SMALL - values.shape[1]
        if missing:
            values = jnp.concatenate([values, jnp.zeros((1, missing), F32)], axis=1)
        return values

    lines = [again_ref[...], fgain_ref[...], ogain_ref[...]]
    taps = taps_ref[...].astype(F32)
    for tap in range(CONV):
        for start in range(0, taps.shape[1], SMALL):
            lines.append(taps[tap : tap + 1, start : start + SMALL])
    small = jnp.zeros((rows, SMALL), F32)
    for row, line in enumerate(lines):
        small = jnp.where(row_ids == row, lanes(line), small)
    betas = beta_ref[...].astype(F32)
    for ctx in range(ctxs):
        own = []
        for slot, head in enumerate(heads_of(ctx, ctxs, heads, rows)):
            to, cols = slot * HD, slice(head * HD, (head + 1) * HD)
            for part in range(3):
                out_ref = second_ref if part == 2 else first_ref
                start = to + (width if part == 1 else 0)
                out_ref[ctx, :, start : start + HD] = qkv_ref[
                    :, part * total + head * HD : part * total + (head + 1) * HD
                ]
            second_ref[ctx, :, width + to : width + to + HD] = gate_ref[:, cols]
            own.append(betas[:, head : head + 1])
        own.append(jnp.zeros((rows, 128 - SMALL - heads), F32))
        first_ref[ctx, :, 2 * width :] = jnp.concatenate(own + [small], axis=1).astype(
            first_ref.dtype
        )


def pack_mix(w_qkv, w_gate_o, w_beta, attn_gain, ffn_gain, norm_gain_o, conv_weight, ctxs):
    rows, total = w_gate_o.shape
    width = total // ctxs
    return pl.pallas_call(
        pack_mix_kernel,
        out_shape=[
            jax.ShapeDtypeStruct((ctxs, rows, 2 * width + 128), w_qkv.dtype),
            jax.ShapeDtypeStruct((ctxs, rows, 2 * width), w_qkv.dtype),
        ],
        compiler_params=pltpu.CompilerParams(vmem_limit_bytes=48 * 1024 * 1024),
        name="pack_mix",
    )(
        w_qkv, w_gate_o, w_beta, attn_gain[None, :], ffn_gain[None, :], norm_gain_o[None, :],
        conv_weight,
    )


def read_small_kernel(
    in_ref, again_ref, fgain_ref, ogain_ref, taps_ref, all_taps, *, row_part, taps_part, gain_part
):
    values = in_ref[...].astype(F32)
    devices = values.shape[0] // row_part
    lines = -(-taps_part // SMALL)

    def line(row, size):
        starts = [device * row_part + row for device in range(devices)]
        return jnp.concatenate(
            [values[at : at + 1, 128 - SMALL : 128 - SMALL + size] for at in starts], axis=1
        )

    again_ref[...] = line(0, row_part)
    fgain_ref[...] = line(1, row_part)
    ogain_ref[...] = line(2, gain_part)
    for tap in range(CONV):
        pieces = []
        for device in range(devices):
            for index in range(lines):
                at = device * row_part + 3 + tap * lines + index
                size = min(SMALL, taps_part - index * SMALL)
                pieces.append(values[at : at + 1, 128 - SMALL : 128 - SMALL + size])
        all_taps[tap : tap + 1] = jnp.concatenate(pieces, axis=1)
    taps_ref[...] = jnp.zeros_like(taps_ref)
    total = all_taps.shape[1] // 3
    width = taps_ref.shape[1] // 3
    heads = width // HD
    ctxs = total // width
    ctx = lax.axis_index("ctx")
    blocks = HD // row_part
    for slot in range(heads):
        head = ((ctx % blocks) * heads + slot) * (ctxs // blocks) + ctx // blocks
        for part in range(3):
            start = pl.multiple_of(part * total + head * HD, HD)
            to = part * width + slot * HD
            taps_ref[0:CONV, to : to + HD] = all_taps[0:CONV, pl.ds(start, HD)]


def read_small(w_small, row_part, taps_part, gain_part, width):
    rows = w_small.shape[0]
    total = 3 * rows
    return pl.pallas_call(
        functools.partial(
            read_small_kernel, row_part=row_part, taps_part=taps_part, gain_part=gain_part
        ),
        out_shape=[
            jax.ShapeDtypeStruct((1, rows), F32),
            jax.ShapeDtypeStruct((1, rows), F32),
            jax.ShapeDtypeStruct((1, HD), F32),
            jax.ShapeDtypeStruct((8, 3 * width), F32),
        ],
        scratch_shapes=[pltpu.VMEM((8, total), F32)],
        compiler_params=pltpu.CompilerParams(vmem_limit_bytes=48 * 1024 * 1024),
        name="read_small",
    )(w_small)


def unpack_mix_kernel(
    in_ref, qkv_ref, gate_ref, beta_ref, gqkv_ref, ggate_ref, gbeta_ref, small_ref,
    rows_ref
):
    ctxs = in_ref.shape[0]
    rows, total = gate_ref.shape
    width = total // ctxs
    heads = gbeta_ref.shape[1] // ctxs
    row_sum = jnp.zeros(rows_ref.shape, F32)
    small_sum = jnp.zeros(small_ref.shape, F32)
    betas = [None] * (heads * ctxs)
    for ctx in range(ctxs):
        small = in_ref[ctx, :, 4 * width :].astype(F32)
        small_sum += small
        for slot, head in enumerate(heads_of(ctx, ctxs, heads, rows)):
            betas[head] = small[:, slot : slot + 1]
            for part in range(4):
                start = part * width + slot * HD
                grad = in_ref[ctx, :, start : start + HD].astype(F32)
                if part == 3:
                    cols = slice(head * HD, (head + 1) * HD)
                    ggate_ref[:, cols] = grad
                    weight = gate_ref[:, cols].astype(F32)
                else:
                    cols = slice(part * total + head * HD, part * total + (head + 1) * HD)
                    gqkv_ref[:, cols] = grad
                    weight = qkv_ref[:, cols].astype(F32)
                row_sum += jnp.sum(grad * weight, axis=1, keepdims=True)
    grad = jnp.concatenate(betas, axis=1)
    gbeta_ref[...] = grad
    small_ref[...] = small_sum
    rows_ref[...] = row_sum + jnp.sum(grad * beta_ref[...].astype(F32), axis=1, keepdims=True)


def unpack_mix(received, w_qkv, w_gate_o, w_beta):
    rows = w_qkv.shape[0]
    return pl.pallas_call(
        unpack_mix_kernel,
        out_shape=[
            jax.ShapeDtypeStruct(w_qkv.shape, F32),
            jax.ShapeDtypeStruct(w_gate_o.shape, F32),
            jax.ShapeDtypeStruct(w_beta.shape, F32),
            jax.ShapeDtypeStruct((rows, 128), F32),
            jax.ShapeDtypeStruct((rows, 1), F32),
        ],
        compiler_params=pltpu.CompilerParams(vmem_limit_bytes=48 * 1024 * 1024),
        name="unpack_mix",
    )(received, w_qkv, w_gate_o, w_beta)


def pack_ff_kernel(in_ref, out_ref, *, dps):
    ctxs = out_ref.shape[0]
    part = out_ref.shape[2] // (2 * dps)
    hidden = in_ref.shape[1] // 2
    for ctx in range(ctxs):
        starts = [
            side * hidden + (place * ctxs + ctx) * part for side in range(2) for place in range(dps)
        ]
        out_ref[ctx] = jnp.concatenate([in_ref[:, s : s + part] for s in starts], axis=1)


def pack_ff(w_gate_up, ctxs, dps):
    rows, total = w_gate_up.shape
    return pl.pallas_call(
        functools.partial(pack_ff_kernel, dps=dps),
        out_shape=jax.ShapeDtypeStruct((ctxs, rows, total // ctxs), w_gate_up.dtype),
        compiler_params=pltpu.CompilerParams(vmem_limit_bytes=48 * 1024 * 1024),
        name="pack_ff",
    )(w_gate_up)


def unpack_ff_kernel(in_ref, w_ref, out_ref, rows_ref, *, dps):
    ctxs = in_ref.shape[0]
    part = in_ref.shape[2] // (2 * dps)
    hidden = out_ref.shape[1] // 2
    row_sum = jnp.zeros(rows_ref.shape, F32)
    for side in range(2):
        pieces = []
        for place in range(dps):
            start = (side * dps + place) * part
            pieces.extend(in_ref[ctx, :, start : start + part] for ctx in range(ctxs))
        grad = jnp.concatenate(pieces, axis=1).astype(F32)
        cols = slice(side * hidden, (side + 1) * hidden)
        out_ref[:, cols] = grad
        row_sum += jnp.sum(grad * w_ref[:, cols].astype(F32), axis=1, keepdims=True)
    rows_ref[...] = row_sum


def unpack_ff(received, w_gate_up, dps):
    return pl.pallas_call(
        functools.partial(unpack_ff_kernel, dps=dps),
        out_shape=[
            jax.ShapeDtypeStruct(w_gate_up.shape, F32),
            jax.ShapeDtypeStruct((w_gate_up.shape[0], 1), F32),
        ],
        compiler_params=pltpu.CompilerParams(vmem_limit_bytes=48 * 1024 * 1024),
        name="unpack_ff",
    )(received, w_gate_up)


def gate_up_kernel(h2_ref, dhidden_ref, weight_ref, hidden_ref, dgate_up_ref, dh2_ref):
    half = hidden_ref.shape[1]
    weight = weight_ref[...]
    gate_up = lax.dot_general(h2_ref[...], weight, (NN, ((), ())), preferred_element_type=F32)
    gate, up = gate_up[:, :half], gate_up[:, half:]
    gate_sig = sigmoid(gate)
    gate_act = gate * gate_sig
    dhidden = dhidden_ref[...].astype(F32)
    hidden_ref[...] = (gate_act * up).astype(BF)
    dgate = dhidden * up * (gate_sig * (1.0 + gate * (1.0 - gate_sig)))
    dgate_up = jnp.concatenate([dgate, dhidden * gate_act], axis=1).astype(BF)
    dgate_up_ref[...] = dgate_up
    dh2_ref[...] = lax.dot_general(
        dgate_up, weight, (NT, ((), ())), preferred_element_type=F32
    ).astype(BF)


def gate_up_both_ways(h2_low, d_hidden, w_gu):
    extent, width = h2_low.shape
    cols = w_gu.shape[1]
    half = cols // 2
    step = min(FF_STEP, extent)

    def rows(size):
        return pl.BlockSpec((step, size), lambda i: (i, 0))

    return pl.pallas_call(
        gate_up_kernel,
        grid=(extent // step,),
        in_specs=[
            rows(width),
            rows(half),
            pl.BlockSpec((width, cols), lambda i: (0, 0), pipeline_mode=pl.Buffered(1)),
        ],
        out_specs=[rows(half), rows(cols), rows(width)],
        out_shape=[
            jax.ShapeDtypeStruct((extent, half), BF),
            jax.ShapeDtypeStruct((extent, cols), BF),
            jax.ShapeDtypeStruct((extent, width), BF),
        ],
        compiler_params=pltpu.CompilerParams(
            dimension_semantics=("arbitrary",), vmem_limit_bytes=52 * 1024 * 1024
        ),
        cost_estimate=pl.CostEstimate(
            flops=4 * extent * width * cols, bytes_accessed=6 * extent * width, transcendentals=0
        ),
        name="gate_up_both_ways",
    )(h2_low, d_hidden, w_gu)


def dot(left, right, dims=NN):
    return lax.dot_general(left, right, (dims, ((), ())), preferred_element_type=F32)


def after(value, *others):
    return lax.optimization_barrier((value,) + others)[0]


def swapped(value, axis, distance):
    count = lax.axis_size(axis)
    return lax.ppermute(value, axis, [(i, i ^ distance) for i in range(count)])


def row_major(value):
    return with_layout_constraint(value, Layout(major_to_minor=tuple(range(value.ndim))))


def placed(parts, order):
    whole = row_major(jnp.zeros((len(parts),) + parts[0].shape, parts[0].dtype))
    for part, place in zip(parts, order):
        whole = lax.dynamic_update_index_in_dim(whole, part, place, 0)
    return row_major(lax.optimization_barrier(whole))


def shards_of(shard, axis):
    count = lax.axis_size(axis)
    return [shard] + [swapped(shard, axis, distance) for distance in range(1, count)]


def placed_shards(parts, axis):
    place = lax.axis_index(axis)
    return placed(parts, [place ^ distance for distance in range(len(parts))])


def gather_start(shard, axis):
    if lax.axis_size(axis) != 4:
        return shards_of(shard, axis)[1:]
    half = shard.shape[0] // 2
    return [swapped(shard[:half], axis, 1), swapped(shard[half:], axis, 2)]


def gather_end(shard, moved, axis):
    count, place = lax.axis_size(axis), lax.axis_index(axis)
    if count != 4:
        return placed_shards([shard] + moved, axis)
    half = shard.shape[0] // 2
    tops = swapped(jnp.stack([shard[:half], moved[0]]), axis, 2)
    ends = swapped(jnp.stack([shard[half:], moved[1]]), axis, 1)
    parts = [shard[:half], shard[half:], moved[0], moved[1], tops[0], ends[0], tops[1], ends[1]]
    order = [(0, 0), (0, 1), (1, 0), (2, 1), (2, 0), (1, 1), (3, 0), (3, 1)]
    whole = placed(parts, [2 * (place ^ distance) + side for distance, side in order])
    return whole.reshape((count,) + shard.shape)


def reduce_parts(part_of, axis):
    count, place = lax.axis_size(axis), lax.axis_index(axis)
    parts = [part_of(place ^ distance) for distance in range(count)]
    if count != 4:
        return parts[1:], parts[:1]
    half = parts[0].shape[0] // 2
    sent = [
        jnp.stack([parts[1][:half], parts[3][:half]]), jnp.stack([parts[2][half:], parts[3][half:]])
    ]
    return sent, [parts[0], parts[2][:half], parts[1][half:]]


def reduce_start(sent, axis):
    if lax.axis_size(axis) != 4:
        return [swapped(part, axis, index + 1) for index, part in enumerate(sent)]
    return [swapped(sent[0], axis, 1), swapped(sent[1], axis, 2)]


def reduce_end(moved, kept, axis):
    if lax.axis_size(axis) != 4:
        return total_of(moved + kept)
    own, top, end = kept
    half = own.shape[0] // 2
    top = swapped((top.astype(F32) + moved[0][1].astype(F32)).astype(BF), axis, 2)
    end = swapped((end.astype(F32) + moved[1][1].astype(F32)).astype(BF), axis, 1)
    top = total_of([moved[0][0], top, own[:half]])
    end = total_of([moved[1][0], end, own[half:]])
    return jnp.concatenate([top, end], axis=0)


def shard_parts(part_of, axis):
    count, place = lax.axis_size(axis), lax.axis_index(axis)
    sent = [part_of(place ^ distance) for distance in range(1, count)]
    return sent + [part_of(place)]


def swapped_parts(parts, axis):
    return [swapped(part, axis, index + 1) for index, part in enumerate(parts[:-1])] + parts[-1:]


def total_of(parts):
    total = parts[-1].astype(F32)
    for part in parts[:-1]:
        total = total + part.astype(F32)
    return total


def head_routes(row_part, turn):
    dps, ctxs = lax.axis_size("dp"), lax.axis_size("ctx")
    blocks = HD // row_part
    heads = dps // blocks
    routes = []
    for dp in range(dps):
        for ctx in range(ctxs):
            place = (dp % heads) * blocks + ctx % blocks
            user = (ctx // blocks) * blocks + dp // heads
            routes.append((dp * ctxs + ctx, (place ^ turn) * ctxs + user))
    return routes


def head_owner_parts(rows):
    turns = range(lax.axis_size("dp"))
    return [lax.ppermute(rows, ("dp", "ctx"), head_routes(rows.shape[0], turn)) for turn in turns]


def row_owner_parts(blocks):
    place = lax.axis_index("dp")
    parts = []
    for turn in range(lax.axis_size("dp")):
        routes = [(user, owner) for owner, user in head_routes(blocks.shape[1], turn)]
        block = lax.dynamic_index_in_dim(blocks, place ^ turn, 0, False)
        parts.append(lax.ppermute(block, ("dp", "ctx"), routes))
    return parts


def spread(value, axis):
    return lax.all_to_all(value, axis, 0, 0, tiled=True)


def rms_scale(values):
    return lax.rsqrt(jnp.mean(values * values, axis=-1, keepdims=True) + EPS)


def norm_pull(values, scale, gain, grad):
    weighted = grad * gain
    return scale * weighted - values * (
        scale * scale * scale * jnp.mean(weighted * values, axis=-1, keepdims=True)
    )


def per_device(
    tokens,
    cotangent,
    group_ids,
    group_scale,
    attn_gain,
    w_qkv,
    conv_weight,
    w_beta,
    w_gate_o,
    norm_gain_o,
    w_out,
    ffn_gain,
    w_gate_up,
    w_down,
):
    seg_len, width = tokens.shape[1:]
    dps, ctxs = lax.axis_size("dp"), lax.axis_size("ctx")
    devices = dps * ctxs
    ctx_place = lax.axis_index("ctx")
    head_count = w_beta.shape[1]
    heads = head_count // ctxs
    mix_width = heads * HD
    row_part = w_qkv.shape[0]
    dp_rows = ctxs * row_part
    ff_part = w_down.shape[0]
    ff_local = dps * ff_part
    taps_part = conv_weight.shape[1]
    taps_cols = CONV * taps_part // row_part
    gain_part = norm_gain_o.shape[0]
    head_dims = (HD // row_part, heads, ctxs * row_part // HD)

    x_full = lax.all_gather(tokens[0], "ctx", axis=0, tiled=True)
    first_rows, second_rows = pack_mix(
        w_qkv, w_gate_o, w_beta, attn_gain, ffn_gain, norm_gain_o, conv_weight, ctxs
    )
    matches = group_ids[:, None] == lax.broadcasted_iota(
        jnp.int32, (group_ids.shape[0], group_scale.shape[0]), 1
    )
    seq_scale = jnp.sum(jnp.where(matches, group_scale[None, :], 0.0), axis=1)
    d_out = after(cotangent[0], first_rows).astype(F32) * seq_scale[0]
    d_out_full = lax.all_gather(after(d_out.astype(BF), x_full), "ctx", axis=0, tiled=True)
    first_half = spread(first_rows, "ctx").reshape(dp_rows, first_rows.shape[2])
    down_parts = shards_of(w_down, "dp")
    out_parts = head_owner_parts(after(w_out, *down_parts[1:3]))
    first_half, *down_parts = lax.optimization_barrier((first_half, *down_parts))
    second_half = spread(after(second_rows, first_half), "ctx").reshape(dp_rows, 2 * mix_width)
    first_parts = shards_of(first_half, "dp")
    second_half, *parts = lax.optimization_barrier((second_half, *first_parts[1:3], *out_parts))
    first_parts[1:3], out_parts = parts[:2], parts[2:]
    second_parts = shards_of(second_half, "dp")
    gate_up_rows = pack_ff(w_gate_up, ctxs, dps)
    gate_up_half = spread(after(gate_up_rows, second_half), "ctx").reshape(dp_rows, 2 * ff_local)

    x_rows = x_full.astype(F32)
    x_scale = rms_scale(x_rows)
    w_out_own = placed_shards(out_parts, "dp").reshape(mix_width, width)
    x_scale, w_out_own, *first_parts = lax.optimization_barrier(
        (x_scale, w_out_own, *first_parts)
    )
    w_first = placed_shards(first_parts, "dp").reshape(width, first_rows.shape[2])
    w_small = lax.optimization_barrier(w_first[:, 2 * mix_width :])
    attn_full, ffn_full, norm_o_full, taps = read_small(
        w_small, row_part, taps_part, gain_part, mix_width
    )

    h1_low = (x_rows * x_scale * attn_full).astype(BF)
    first = dot(h1_low, w_first)
    first, taps, *second_parts = lax.optimization_barrier((first, taps, *second_parts))
    w_second = placed_shards(second_parts, "dp").reshape(width, 2 * mix_width)
    second = dot(h1_low, w_second)
    y_local, core, states, inverses = mix_forward(first, second, taps, norm_o_full)
    y_local, d_out_full, gate_up_half = lax.optimization_barrier(
        (y_local, d_out_full, gate_up_half)
    )
    gate_up_moved = gather_start(gate_up_half, "dp")
    w_dn = placed_shards(down_parts, "dp").reshape(ff_local, width)
    attn_part = dot(y_local, w_out_own).astype(BF)
    attn_sum = lax.psum_scatter(attn_part, "ctx", scatter_dimension=0, tiled=True)

    x_own = tokens[0].astype(F32)
    w_mix = jnp.concatenate([w_first[:, : 2 * mix_width], w_second, w_small], axis=1)
    attn_sum, gate_up_moved, w_dn, w_mix = lax.optimization_barrier(
        (attn_sum, gate_up_moved, w_dn, w_mix)
    )
    resid = x_own + attn_sum.astype(F32)
    resid_scale = rms_scale(resid)
    h2_own = (resid * resid_scale * ffn_full).astype(BF)
    h2_low = lax.all_gather(h2_own, "ctx", axis=0, tiled=True)

    w_gu = gather_end(gate_up_half, gate_up_moved, "dp").reshape(width, 2 * ff_local)
    d_hidden = dot(d_out_full, w_dn, NT).astype(BF)
    h2_low, d_hidden = lax.optimization_barrier((h2_low, d_hidden))
    hidden_low, d_gate_up, d_h2_part = gate_up_both_ways(h2_low, d_hidden, w_gu)
    d_h2 = lax.psum_scatter(d_h2_part, "ctx", scatter_dimension=0, tiled=True)
    hidden_later, d_gate_up_later = lax.optimization_barrier((hidden_low, d_gate_up, d_h2_part))[:2]
    out_part = dot(hidden_later, w_dn).astype(BF)

    def down_part(place):
        hidden_cols = lax.dynamic_slice_in_dim(hidden_later, place * ff_part, ff_part, 1)
        return dot(hidden_cols, d_out_full, TN).astype(BF)

    def gate_up_part(place):
        h2_cols = lax.dynamic_slice_in_dim(h2_low, place * dp_rows, dp_rows, 1)
        return dot(h2_cols, d_gate_up_later, TN).astype(BF)

    g_gate_up_sent, g_gate_up_kept = reduce_parts(gate_up_part, "dp")
    g_down_parts = shard_parts(down_part, "dp")
    g_gate_up_moved = reduce_start(g_gate_up_sent, "dp")
    d_h2, g_gate_up_moved = lax.optimization_barrier((d_h2, g_gate_up_moved))

    d_resid = d_out + norm_pull(resid, resid_scale, ffn_full, d_h2.astype(F32))
    d_attn = lax.all_gather(d_resid.astype(BF), "ctx", axis=0, tiled=True)
    g_gate_up = reduce_end(g_gate_up_moved, g_gate_up_kept, "dp").astype(BF)
    g_down_moved = swapped_parts(g_down_parts, "dp")
    d_attn, g_gate_up, out_part, *g_down_moved[:2] = lax.optimization_barrier(
        (d_attn, g_gate_up, out_part, *g_down_moved[:2])
    )
    out_sum = lax.psum_scatter(after(out_part, d_attn), "ctx", scatter_dimension=0, tiled=True)
    d_y = dot(d_attn, w_out_own, NT).astype(BF)
    g_gate_up = spread(g_gate_up.reshape(ctxs, row_part, 2 * ff_local), "ctx")

    d_proj, d_beta, g_taps, g_gain_o = mix_backward(
        first, second, d_y, core, states, inverses, taps, norm_o_full
    )

    def mix_part(place):
        h1_cols = lax.dynamic_slice_in_dim(h1_low, place * dp_rows, dp_rows, 1)
        return dot(h1_cols, d_proj, TN).astype(BF)

    g_mix_sent, g_mix_kept = reduce_parts(mix_part, "dp")
    d_proj_later, g_mix_sent, d_beta, g_taps, g_gain_o, d_attn_later = lax.optimization_barrier(
        (d_proj, g_mix_sent, d_beta, g_taps, g_gain_o, d_attn)
    )
    g_mix_moved = reduce_start(g_mix_sent, "dp")
    d_beta_low = jnp.pad(d_beta.astype(BF), ((0, 0), (0, 128 - heads)))
    d_h1_part = dot(jnp.concatenate([d_proj_later, d_beta_low], axis=1), w_mix, NT).astype(BF)
    taps_grad = jnp.zeros((ctxs, CONV, 3 * mix_width), F32)
    taps_grad = lax.dynamic_update_index_in_dim(taps_grad, g_taps[:CONV], ctx_place, 0)
    taps_grad = (
        taps_grad.reshape(head_dims[2], head_dims[0], CONV, 3, heads, HD)
        .transpose(2, 3, 1, 4, 0, 5)
        .reshape(CONV, devices, taps_part)
        .transpose(1, 0, 2)
        .reshape(width, taps_cols)
    )
    gain_grad = jnp.pad(g_gain_o[0].reshape(devices, gain_part), ((0, 0), (0, row_part - gain_part)))
    small_grad = jnp.concatenate(
        [jnp.zeros((width, heads), F32), gain_grad.reshape(width, 1), taps_grad], axis=1
    )
    small_grad = jnp.pad(small_grad, ((0, 0), (0, 128 - small_grad.shape[1])))
    small_grad = (small_grad + dot(h1_low, d_beta_low, TN)).astype(BF)
    small_grad = small_grad.reshape(dps, dp_rows, 128)

    g_out = dot(y_local, d_attn_later, TN).astype(BF)
    g_out_parts = row_owner_parts(g_out.reshape(dps, row_part, width))
    d_h1_part, out_sum, g_gate_up, g_mix_moved, small_grad, *g_out_parts = lax.optimization_barrier(
        (d_h1_part, out_sum, g_gate_up, g_mix_moved, small_grad, *g_out_parts)
    )
    block_out = (resid + out_sum.astype(F32)).astype(BF)[None]
    d_h1 = lax.psum_scatter(d_h1_part, "ctx", scatter_dimension=0, tiled=True).astype(F32)
    d_tokens = (d_resid + norm_pull(x_own, rms_scale(x_own), attn_full, d_h1))[None]

    def small_part(place):
        return lax.dynamic_index_in_dim(small_grad, place, 0, False)

    g_small = total_of(swapped_parts(shard_parts(small_part, "dp"), "dp")).astype(BF)
    g_mix = reduce_end(g_mix_moved, g_mix_kept, "dp").astype(BF)
    g_mix = jnp.concatenate([g_mix, g_small], axis=1)
    g_w_out = total_of(g_out_parts)
    g_w_down = total_of(g_down_moved)

    g_w_gate_up, ffn_sum = unpack_ff(g_gate_up, w_gate_up, dps)
    g_ffn_gain = ffn_sum[:, 0] / ffn_gain.astype(F32)
    g_mix = spread(g_mix.reshape(ctxs, row_part, g_mix.shape[1]), "ctx")
    g_mix, d_tokens, g_w_gate_up, g_w_down, g_w_out = lax.optimization_barrier(
        (g_mix, d_tokens, g_w_gate_up, g_w_down, g_w_out)
    )
    g_w_qkv, g_w_gate_o, g_w_beta, small_sum, attn_row_sum = unpack_mix(
        g_mix, w_qkv, w_gate_o, w_beta
    )
    g_attn_gain = attn_row_sum[:, 0] / attn_gain.astype(F32)
    g_norm_gain_o = small_sum[:gain_part, heads]
    g_conv = small_sum[:, heads + 1 : heads + 1 + taps_cols].reshape(CONV, taps_part)
    return (
        block_out,
        d_tokens,
        g_attn_gain,
        g_w_qkv,
        g_conv,
        g_w_beta,
        g_w_gate_o,
        g_norm_gain_o,
        g_w_out,
        g_ffn_gain,
        g_w_gate_up,
        g_w_down,
    )


def solution(mesh):
    rows = P(("dp", "ctx"), None)
    flat = P(("dp", "ctx"))
    taps = P(None, ("dp", "ctx"))
    acts = P("dp", "ctx", None)
    return jax.shard_map(
        per_device,
        mesh=mesh,
        in_specs=(
            acts, acts, P("dp"), P(), flat, rows, taps, rows, rows, flat, rows, flat, rows, rows
        ),
        out_specs=(acts, acts, flat, rows, taps, rows, rows, flat, rows, flat, rows, rows),
        check_vma=False,
    )
```

```python
import functools

import jax
import jax.numpy as jnp
from jax import lax
from jax.experimental import pallas as pl
from jax.experimental.layout import Layout, with_layout_constraint
from jax.experimental.pallas import tpu as pltpu
from jax.sharding import PartitionSpec as P

CONV = 4
HD = 128
CHUNK = 128
STEP = 512
SMALL = 64
FF_STEP = 256
EPS = 1e-05
KEY_EPS = 1e-06
BF = jnp.bfloat16
F32 = jnp.float32
NN = ((1,), (0,))
NT = ((1,), (1,))
TN = ((0,), (0,))


def mm(left, right, dims):
    return lax.dot_general(
        left.astype(BF), right.astype(BF), (dims, ((), ())), preferred_element_type=F32
    )


def halves(values):
    high = values.astype(BF)
    return high, (values - high.astype(F32)).astype(BF)


def mm_fine(left, right, dims):
    left_hi, left_lo = halves(left)
    right_hi, right_lo = halves(right)

    def product(a, b):
        return lax.dot_general(a, b, (dims, ((), ())), preferred_element_type=F32)

    return product(left_hi, right_hi) + (product(left_hi, right_lo) + product(left_lo, right_hi))


def sigmoid(values):
    return 1.0 / (1.0 + jnp.exp(-values))


def chunk_ids():
    row_ids = lax.broadcasted_iota(jnp.int32, (CHUNK, CHUNK), 0)
    col_ids = lax.broadcasted_iota(jnp.int32, (CHUNK, CHUNK), 1)
    return row_ids, col_ids


def lower_inverses(strict_parts):
    row_ids, col_ids = chunk_ids()
    results = None
    size = 1
    while size < CHUNK:
        pair_mask = (row_ids // (2 * size) == col_ids // (2 * size)) & (
            (row_ids // size) != (col_ids // size)
        )
        corners = [jnp.where(pair_mask, part, 0.0) for part in strict_parts]
        if results is None:
            ident = jnp.where(row_ids == col_ids, 1.0, 0.0)
            results = [ident - corner for corner in corners]
        else:
            moved = [mm_fine(corner, result, NN) for corner, result in zip(corners, results)]
            results = [result - mm_fine(result, part, NN) for result, part in zip(results, moved)]
        size *= 2
    return results


def conv_taps(extended, taps, extent):
    total = taps[0:1] * extended[5 : 5 + extent]
    for offset in range(1, CONV):
        total = total + taps[offset : offset + 1] * extended[5 + offset : 5 + offset + extent]
    return total


def unit_keys(raw):
    scale = lax.rsqrt(jnp.sum(raw * raw, axis=-1, keepdims=True) + KEY_EPS)
    return raw * scale, scale


def conv_inputs(first, second, width):
    pre = jnp.concatenate([first[:, : 2 * width], second[:, :width]], axis=1)
    return pre.astype(BF).astype(F32)


def mix_forward_kernel(
    first_ref, second_ref, taps_ref, gain_ref, y_ref, core_ref, state_ref, inverse_ref, state_now,
    rim, *, heads
):
    width = heads * HD
    step = first_ref.shape[0]
    chunks = step // CHUNK

    @pl.when(pl.program_id(0) == 0)
    def _():
        state_now[...] = jnp.zeros_like(state_now)
        rim[...] = jnp.zeros_like(rim)

    pre = conv_inputs(first_ref[...], second_ref[...], width)
    extended = jnp.concatenate([rim[...], pre], axis=0)
    rim[...] = pre[step - 8 :]
    conv = conv_taps(extended, taps_ref[...], step)
    mixture = conv * sigmoid(conv)
    beta = sigmoid(first_ref[:, 2 * width : 2 * width + heads])
    row_ids, col_ids = chunk_ids()
    tiles = [(chunk, head) for chunk in range(chunks) for head in range(heads)]
    q_t, k_t, v_t, b_t, score_t, strict_t = [], [], [], [], [], []
    for chunk, head in tiles:
        rows = slice(chunk * CHUNK, (chunk + 1) * CHUNK)
        q_rows = mixture[rows, head * HD : (head + 1) * HD]
        k_rows, _ = unit_keys(mixture[rows, width + head * HD : width + (head + 1) * HD])
        v_rows = mixture[rows, 2 * width + head * HD : 2 * width + (head + 1) * HD]
        b_rows = beta[rows, head : head + 1]
        q_t.append(q_rows)
        k_t.append(k_rows)
        v_t.append(v_rows)
        b_t.append(b_rows)
        score_t.append(jnp.where(row_ids >= col_ids, mm(q_rows, k_rows, NT), 0.0))
        strict_t.append(jnp.where(row_ids > col_ids, b_rows * mm_fine(k_rows, k_rows, NT), 0.0))
    inverse_t = lower_inverses(strict_t)
    w_t = [mm(t, b * k, NN) for t, b, k in zip(inverse_t, b_t, k_t)]
    u_t = [mm(t, b * v, NN) for t, b, v in zip(inverse_t, b_t, v_t)]
    for index, (chunk, head) in enumerate(tiles):
        rows = slice(chunk * CHUNK, (chunk + 1) * CHUNK)
        cols = slice(head * HD, (head + 1) * HD)
        state = state_now[head]
        state_ref[chunk, head] = state
        inverse_ref[chunk, head] = inverse_t[index]
        update = u_t[index] - mm(w_t[index], state, NN)
        core = mm(q_t[index], state, NN) + mm(score_t[index], update, NN)
        state_now[head] = state + mm(k_t[index], update, TN)
        core_ref[rows, cols] = core
        scale = lax.rsqrt(jnp.mean(core * core, axis=-1, keepdims=True) + EPS)
        gate = second_ref[rows, width + head * HD : width + (head + 1) * HD]
        y_ref[rows, cols] = (
            core * scale * gain_ref[...] * (gate * sigmoid(gate))
        ).astype(y_ref.dtype)


def mix_backward_kernel(
    first_ref, second_ref, first_before_ref, second_before_ref, dy_ref, core_ref, state_ref,
    inverse_ref, taps_ref, gain_ref, dproj_ref, dbeta_ref, gtaps_ref, ggain_ref, adjoint, rim, *, heads, blocks
):
    width = heads * HD
    step = first_ref.shape[0]
    chunks = step // CHUNK
    block = blocks - 1 - pl.program_id(0)

    @pl.when(pl.program_id(0) == 0)
    def _():
        adjoint[...] = jnp.zeros_like(adjoint)
        rim[...] = jnp.zeros_like(rim)
        gtaps_ref[...] = jnp.zeros_like(gtaps_ref)
        ggain_ref[...] = jnp.zeros_like(ggain_ref)

    before = conv_inputs(first_before_ref[...], second_before_ref[...], width)
    before = jnp.where(block > 0, before[before.shape[0] - 8 :], 0.0)
    extended = jnp.concatenate(
        [before, conv_inputs(first_ref[...], second_ref[...], width)], axis=0
    )
    taps = taps_ref[...]
    conv = conv_taps(extended, taps, step)
    conv_sig = sigmoid(conv)
    mixture = conv * conv_sig
    beta = sigmoid(first_ref[:, 2 * width : 2 * width + heads])
    gain = gain_ref[...]
    row_ids, col_ids = chunk_ids()
    causal, strict = row_ids >= col_ids, row_ids > col_ids
    tiles = [(chunk, head) for chunk in range(chunks) for head in range(heads)]
    held = {}
    ggain = jnp.zeros((1, HD), F32)
    for chunk, head in tiles:
        rows = slice(chunk * CHUNK, (chunk + 1) * CHUNK)
        cols = slice(head * HD, (head + 1) * HD)
        q_rows = mixture[rows, head * HD : (head + 1) * HD]
        k_rows, k_scale = unit_keys(mixture[rows, width + head * HD : width + (head + 1) * HD])
        v_rows = mixture[rows, 2 * width + head * HD : 2 * width + (head + 1) * HD]
        b_rows = beta[rows, head : head + 1]
        core = core_ref[rows, cols]
        scale = lax.rsqrt(jnp.mean(core * core, axis=-1, keepdims=True) + EPS)
        gate = second_ref[rows, width + head * HD : width + (head + 1) * HD]
        gate_sig = sigmoid(gate)
        dy = dy_ref[rows, cols].astype(F32)
        normed = core * scale
        ggain += jnp.sum(dy * (gate * gate_sig) * normed, axis=0, keepdims=True)
        dproj_ref[rows, 3 * width + head * HD : 3 * width + (head + 1) * HD] = (
            dy * normed * gain * (gate_sig * (1.0 + gate * (1.0 - gate_sig)))
        ).astype(dproj_ref.dtype)
        dnorm = dy * (gate * gate_sig) * gain
        dcore = scale * (dnorm - normed * jnp.mean(dnorm * normed, axis=-1, keepdims=True))
        state = state_ref[chunk, head]
        inverse = inverse_ref[chunk, head]
        scores = jnp.where(causal, mm(q_rows, k_rows, NT), 0.0)
        weighted = mm(inverse, b_rows * k_rows, NN)
        resid = v_rows - mm(k_rows, state, NN)
        update = mm(inverse, b_rows * resid, NN)
        dupdate = mm(scores, dcore, TN)
        dstate = mm(q_rows, dcore, TN)
        held[chunk, head] = [
            q_rows, k_rows, k_scale, b_rows, dcore, state, inverse, weighted, resid, update, dupdate,
            dstate
        ]
    later = {}
    for chunk in reversed(range(chunks)):
        for head in range(heads):
            entry = held[chunk, head]
            after = adjoint[head]
            later[chunk, head] = after
            entry[10] = entry[10] + mm(entry[1], after, NN)
            adjoint[head] = after + entry[11] - mm(entry[7], entry[10], TN)
    pieces = {}
    for chunk, head in tiles:
        (
            q_rows, k_rows, k_scale, b_rows, dcore, state, inverse, _, resid, update, dupdate, _
        ) = held[chunk, head]
        after = later[chunk, head]
        rows = slice(chunk * CHUNK, (chunk + 1) * CHUNK)
        dr = mm(inverse, dupdate, TN)
        dv = b_rows * dr
        dstrict = jnp.where(strict, -mm(dr, update, NT), 0.0)
        gram = mm(k_rows, k_rows, NT)
        dbeta = jnp.sum(dr * resid, axis=-1, keepdims=True) + jnp.sum(
            dstrict * gram, axis=-1, keepdims=True
        )
        dgram = b_rows * dstrict
        dscores = jnp.where(causal, mm(dcore, update, NT), 0.0)
        dq = mm(dcore, state, NT) + mm(dscores, k_rows, NN)
        dk = (
            mm(dscores, q_rows, TN)
            + mm(update, after, NT)
            - mm(dv, state, NT)
            + mm(dgram, k_rows, NN)
            + mm(dgram, k_rows, TN)
        )
        dkraw = k_scale * (dk - k_rows * jnp.sum(dk * k_rows, axis=-1, keepdims=True))
        pieces[0, head, chunk] = dq
        pieces[1, head, chunk] = dkraw
        pieces[2, head, chunk] = dv
        dbeta_ref[rows, head : head + 1] = dbeta * b_rows * (1.0 - b_rows)
    dmixture = jnp.concatenate(
        [
            jnp.concatenate([pieces[part, head, chunk] for chunk in range(chunks)], axis=0)
            for part in range(3)
            for head in range(heads)
        ],
        axis=1,
    )
    dconv = dmixture * (conv_sig * (1.0 + conv * (1.0 - conv_sig)))
    followed = jnp.concatenate([dconv, rim[...]], axis=0)
    rim[...] = dconv[:8]
    dpre = taps[CONV - 1 : CONV] * followed[0:step]
    for offset in range(CONV - 1):
        shift = CONV - 1 - offset
        dpre = dpre + taps[offset : offset + 1] * followed[shift : shift + step]
    dproj_ref[:, : 3 * width] = dpre.astype(dproj_ref.dtype)
    for offset in range(CONV):
        gtaps_ref[offset : offset + 1] += jnp.sum(
            dconv * extended[5 + offset : 5 + offset + step], axis=0, keepdims=True
        )
    ggain_ref[0:1] += ggain


def mix_forward(first, second, taps, gain):
    extent, width = first.shape[0], second.shape[1] // 2
    heads = width // HD
    step = min(STEP, extent)
    blocks, chunks = extent // step, step // CHUNK
    return pl.pallas_call(
        functools.partial(mix_forward_kernel, heads=heads),
        grid=(blocks,),
        in_specs=[
            pl.BlockSpec((step, first.shape[1]), lambda i: (i, 0)),
            pl.BlockSpec((step, 2 * width), lambda i: (i, 0)),
            pl.BlockSpec((8, 3 * width), lambda i: (0, 0)),
            pl.BlockSpec((1, HD), lambda i: (0, 0)),
        ],
        out_specs=[
            pl.BlockSpec((step, width), lambda i: (i, 0)),
            pl.BlockSpec((step, width), lambda i: (i, 0)),
            pl.BlockSpec((chunks, heads, HD, HD), lambda i: (i, 0, 0, 0)),
            pl.BlockSpec((chunks, heads, CHUNK, CHUNK), lambda i: (i, 0, 0, 0)),
        ],
        out_shape=[
            jax.ShapeDtypeStruct((extent, width), BF),
            pltpu.HBM((extent, width), F32),
            pltpu.HBM((extent // CHUNK, heads, HD, HD), F32),
            pltpu.HBM((extent // CHUNK, heads, CHUNK, CHUNK), F32),
        ],
        scratch_shapes=[pltpu.VMEM((heads, HD, HD), F32), pltpu.VMEM((8, 3 * width), F32)],
        compiler_params=pltpu.CompilerParams(
            dimension_semantics=("arbitrary",), vmem_limit_bytes=48 * 1024 * 1024
        ),
        cost_estimate=pl.CostEstimate(
            flops=90 * extent * width * CHUNK, bytes_accessed=40 * extent * width, transcendentals=0
        ),
        name="mix_forward",
    )(first, second, taps, gain)


def mix_backward(first, second, dy, core, states, inverses, taps, gain):
    extent, width = first.shape[0], second.shape[1] // 2
    width3 = 3 * width
    heads = width // HD
    step = min(STEP, extent)
    blocks, chunks = extent // step, step // CHUNK
    rows_before = 16

    def at(i):
        return (blocks - 1 - i, 0)

    def at_tiles(i):
        return (blocks - 1 - i, 0, 0, 0)

    def just_before(i):
        return (jnp.maximum((blocks - 1 - i) * (step // rows_before) - 1, 0), 0)

    return pl.pallas_call(
        functools.partial(mix_backward_kernel, heads=heads, blocks=blocks),
        grid=(blocks,),
        in_specs=[
            pl.BlockSpec((step, first.shape[1]), at),
            pl.BlockSpec((step, 2 * width), at),
            pl.BlockSpec((rows_before, first.shape[1]), just_before),
            pl.BlockSpec((rows_before, 2 * width), just_before),
            pl.BlockSpec((step, width), at),
            pl.BlockSpec((step, width), at),
            pl.BlockSpec((chunks, heads, HD, HD), at_tiles),
            pl.BlockSpec((chunks, heads, CHUNK, CHUNK), at_tiles),
            pl.BlockSpec((8, width3), lambda i: (0, 0)),
            pl.BlockSpec((1, HD), lambda i: (0, 0)),
        ],
        out_specs=[
            pl.BlockSpec((step, width3 + width), at),
            pl.BlockSpec((step, heads), at),
            pl.BlockSpec((8, width3), lambda i: (0, 0)),
            pl.BlockSpec((8, HD), lambda i: (0, 0)),
        ],
        out_shape=[
            jax.ShapeDtypeStruct((extent, width3 + width), BF),
            jax.ShapeDtypeStruct((extent, heads), F32),
            jax.ShapeDtypeStruct((8, width3), F32),
            jax.ShapeDtypeStruct((8, HD), F32),
        ],
        scratch_shapes=[pltpu.VMEM((heads, HD, HD), F32), pltpu.VMEM((8, width3), F32)],
        compiler_params=pltpu.CompilerParams(
            dimension_semantics=("arbitrary",), vmem_limit_bytes=48 * 1024 * 1024
        ),
        cost_estimate=pl.CostEstimate(
            flops=90 * extent * width * CHUNK, bytes_accessed=40 * extent * width, transcendentals=0
        ),
        name="mix_backward",
    )(first, second, first, second, dy, core, states, inverses, taps, gain)


def heads_of(ctx, ctxs, heads, row_part):
    blocks = HD // row_part
    groups = ctxs // blocks
    return [((ctx % blocks) * heads + slot) * groups + ctx // blocks for slot in range(heads)]


def pack_mix_kernel(
    qkv_ref, gate_ref, beta_ref, again_ref, fgain_ref, ogain_ref, taps_ref, first_ref, second_ref
):
    ctxs = first_ref.shape[0]
    rows, total = gate_ref.shape
    width = total // ctxs
    heads = beta_ref.shape[1] // ctxs
    row_ids = lax.broadcasted_iota(jnp.int32, (rows, SMALL), 0)

    def lanes(values):
        values = values.astype(F32)
        missing = SMALL - values.shape[1]
        if missing:
            values = jnp.concatenate([values, jnp.zeros((1, missing), F32)], axis=1)
        return values

    lines = [again_ref[...], fgain_ref[...], ogain_ref[...]]
    taps = taps_ref[...].astype(F32)
    for tap in range(CONV):
        for start in range(0, taps.shape[1], SMALL):
            lines.append(taps[tap : tap + 1, start : start + SMALL])
    small = jnp.zeros((rows, SMALL), F32)
    for row, line in enumerate(lines):
        small = jnp.where(row_ids == row, lanes(line), small)
    betas = beta_ref[...].astype(F32)
    for ctx in range(ctxs):
        own = []
        for slot, head in enumerate(heads_of(ctx, ctxs, heads, rows)):
            to, cols = slot * HD, slice(head * HD, (head + 1) * HD)
            for part in range(3):
                out_ref = second_ref if part == 2 else first_ref
                start = to + (width if part == 1 else 0)
                out_ref[ctx, :, start : start + HD] = qkv_ref[
                    :, part * total + head * HD : part * total + (head + 1) * HD
                ]
            second_ref[ctx, :, width + to : width + to + HD] = gate_ref[:, cols]
            own.append(betas[:, head : head + 1])
        own.append(jnp.zeros((rows, 128 - SMALL - heads), F32))
        first_ref[ctx, :, 2 * width :] = jnp.concatenate(own + [small], axis=1).astype(
            first_ref.dtype
        )


def pack_mix(w_qkv, w_gate_o, w_beta, attn_gain, ffn_gain, norm_gain_o, conv_weight, ctxs):
    rows, total = w_gate_o.shape
    width = total // ctxs
    return pl.pallas_call(
        pack_mix_kernel,
        out_shape=[
            jax.ShapeDtypeStruct((ctxs, rows, 2 * width + 128), w_qkv.dtype),
            jax.ShapeDtypeStruct((ctxs, rows, 2 * width), w_qkv.dtype),
        ],
        compiler_params=pltpu.CompilerParams(vmem_limit_bytes=48 * 1024 * 1024),
        name="pack_mix",
    )(
        w_qkv, w_gate_o, w_beta, attn_gain[None, :], ffn_gain[None, :], norm_gain_o[None, :],
        conv_weight,
    )


def read_small_kernel(
    in_ref, again_ref, fgain_ref, ogain_ref, taps_ref, all_taps, *, row_part, taps_part, gain_part
):
    values = in_ref[...].astype(F32)
    devices = values.shape[0] // row_part
    lines = -(-taps_part // SMALL)

    def line(row, size):
        starts = [device * row_part + row for device in range(devices)]
        return jnp.concatenate(
            [values[at : at + 1, 128 - SMALL : 128 - SMALL + size] for at in starts], axis=1
        )

    again_ref[...] = line(0, row_part)
    fgain_ref[...] = line(1, row_part)
    ogain_ref[...] = line(2, gain_part)
    for tap in range(CONV):
        pieces = []
        for device in range(devices):
            for index in range(lines):
                at = device * row_part + 3 + tap * lines + index
                size = min(SMALL, taps_part - index * SMALL)
                pieces.append(values[at : at + 1, 128 - SMALL : 128 - SMALL + size])
        all_taps[tap : tap + 1] = jnp.concatenate(pieces, axis=1)
    taps_ref[...] = jnp.zeros_like(taps_ref)
    total = all_taps.shape[1] // 3
    width = taps_ref.shape[1] // 3
    heads = width // HD
    ctxs = total // width
    ctx = lax.axis_index("ctx")
    blocks = HD // row_part
    for slot in range(heads):
        head = ((ctx % blocks) * heads + slot) * (ctxs // blocks) + ctx // blocks
        for part in range(3):
            start = pl.multiple_of(part * total + head * HD, HD)
            to = part * width + slot * HD
            taps_ref[0:CONV, to : to + HD] = all_taps[0:CONV, pl.ds(start, HD)]


def read_small(w_small, row_part, taps_part, gain_part, width):
    rows = w_small.shape[0]
    total = 3 * rows
    return pl.pallas_call(
        functools.partial(
            read_small_kernel, row_part=row_part, taps_part=taps_part, gain_part=gain_part
        ),
        out_shape=[
            jax.ShapeDtypeStruct((1, rows), F32),
            jax.ShapeDtypeStruct((1, rows), F32),
            jax.ShapeDtypeStruct((1, HD), F32),
            jax.ShapeDtypeStruct((8, 3 * width), F32),
        ],
        scratch_shapes=[pltpu.VMEM((8, total), F32)],
        compiler_params=pltpu.CompilerParams(vmem_limit_bytes=48 * 1024 * 1024),
        name="read_small",
    )(w_small)


def unpack_mix_kernel(
    in_ref, qkv_ref, gate_ref, beta_ref, gqkv_ref, ggate_ref, gbeta_ref, small_ref,
    rows_ref
):
    ctxs = in_ref.shape[0]
    rows, total = gate_ref.shape
    width = total // ctxs
    heads = gbeta_ref.shape[1] // ctxs
    row_sum = jnp.zeros(rows_ref.shape, F32)
    small_sum = jnp.zeros(small_ref.shape, F32)
    betas = [None] * (heads * ctxs)
    for ctx in range(ctxs):
        small = in_ref[ctx, :, 4 * width :].astype(F32)
        small_sum += small
        for slot, head in enumerate(heads_of(ctx, ctxs, heads, rows)):
            betas[head] = small[:, slot : slot + 1]
            for part in range(4):
                start = part * width + slot * HD
                grad = in_ref[ctx, :, start : start + HD].astype(F32)
                if part == 3:
                    cols = slice(head * HD, (head + 1) * HD)
                    ggate_ref[:, cols] = grad
                    weight = gate_ref[:, cols].astype(F32)
                else:
                    cols = slice(part * total + head * HD, part * total + (head + 1) * HD)
                    gqkv_ref[:, cols] = grad
                    weight = qkv_ref[:, cols].astype(F32)
                row_sum += jnp.sum(grad * weight, axis=1, keepdims=True)
    grad = jnp.concatenate(betas, axis=1)
    gbeta_ref[...] = grad
    small_ref[...] = small_sum
    rows_ref[...] = row_sum + jnp.sum(grad * beta_ref[...].astype(F32), axis=1, keepdims=True)


def unpack_mix(received, w_qkv, w_gate_o, w_beta):
    rows = w_qkv.shape[0]
    return pl.pallas_call(
        unpack_mix_kernel,
        out_shape=[
            jax.ShapeDtypeStruct(w_qkv.shape, F32),
            jax.ShapeDtypeStruct(w_gate_o.shape, F32),
            jax.ShapeDtypeStruct(w_beta.shape, F32),
            jax.ShapeDtypeStruct((rows, 128), F32),
            jax.ShapeDtypeStruct((rows, 1), F32),
        ],
        compiler_params=pltpu.CompilerParams(vmem_limit_bytes=48 * 1024 * 1024),
        name="unpack_mix",
    )(received, w_qkv, w_gate_o, w_beta)


def pack_ff_kernel(in_ref, out_ref, *, dps):
    ctxs = out_ref.shape[0]
    part = out_ref.shape[2] // (2 * dps)
    hidden = in_ref.shape[1] // 2
    for ctx in range(ctxs):
        starts = [
            side * hidden + (place * ctxs + ctx) * part for side in range(2) for place in range(dps)
        ]
        out_ref[ctx] = jnp.concatenate([in_ref[:, s : s + part] for s in starts], axis=1)


def pack_ff(w_gate_up, ctxs, dps):
    rows, total = w_gate_up.shape
    return pl.pallas_call(
        functools.partial(pack_ff_kernel, dps=dps),
        out_shape=jax.ShapeDtypeStruct((ctxs, rows, total // ctxs), w_gate_up.dtype),
        compiler_params=pltpu.CompilerParams(vmem_limit_bytes=48 * 1024 * 1024),
        name="pack_ff",
    )(w_gate_up)


def unpack_ff_kernel(in_ref, w_ref, out_ref, rows_ref, *, dps):
    ctxs = in_ref.shape[0]
    part = in_ref.shape[2] // (2 * dps)
    hidden = out_ref.shape[1] // 2
    row_sum = jnp.zeros(rows_ref.shape, F32)
    for side in range(2):
        pieces = []
        for place in range(dps):
            start = (side * dps + place) * part
            pieces.extend(in_ref[ctx, :, start : start + part] for ctx in range(ctxs))
        grad = jnp.concatenate(pieces, axis=1).astype(F32)
        cols = slice(side * hidden, (side + 1) * hidden)
        out_ref[:, cols] = grad
        row_sum += jnp.sum(grad * w_ref[:, cols].astype(F32), axis=1, keepdims=True)
    rows_ref[...] = row_sum


def unpack_ff(received, w_gate_up, dps):
    return pl.pallas_call(
        functools.partial(unpack_ff_kernel, dps=dps),
        out_shape=[
            jax.ShapeDtypeStruct(w_gate_up.shape, F32),
            jax.ShapeDtypeStruct((w_gate_up.shape[0], 1), F32),
        ],
        compiler_params=pltpu.CompilerParams(vmem_limit_bytes=48 * 1024 * 1024),
        name="unpack_ff",
    )(received, w_gate_up)


def gate_up_kernel(h2_ref, dhidden_ref, weight_ref, hidden_ref, dgate_up_ref, dh2_ref):
    half = hidden_ref.shape[1]
    weight = weight_ref[...]
    gate_up = lax.dot_general(h2_ref[...], weight, (NN, ((), ())), preferred_element_type=F32)
    gate, up = gate_up[:, :half], gate_up[:, half:]
    gate_sig = sigmoid(gate)
    gate_act = gate * gate_sig
    dhidden = dhidden_ref[...].astype(F32)
    hidden_ref[...] = (gate_act * up).astype(BF)
    dgate = dhidden * up * (gate_sig * (1.0 + gate * (1.0 - gate_sig)))
    dgate_up = jnp.concatenate([dgate, dhidden * gate_act], axis=1).astype(BF)
    dgate_up_ref[...] = dgate_up
    dh2_ref[...] = lax.dot_general(
        dgate_up, weight, (NT, ((), ())), preferred_element_type=F32
    ).astype(BF)


def gate_up_both_ways(h2_low, d_hidden, w_gu):
    extent, width = h2_low.shape
    cols = w_gu.shape[1]
    half = cols // 2
    step = min(FF_STEP, extent)

    def rows(size):
        return pl.BlockSpec((step, size), lambda i: (i, 0))

    return pl.pallas_call(
        gate_up_kernel,
        grid=(extent // step,),
        in_specs=[
            rows(width),
            rows(half),
            pl.BlockSpec((width, cols), lambda i: (0, 0), pipeline_mode=pl.Buffered(1)),
        ],
        out_specs=[rows(half), rows(cols), rows(width)],
        out_shape=[
            jax.ShapeDtypeStruct((extent, half), BF),
            jax.ShapeDtypeStruct((extent, cols), BF),
            jax.ShapeDtypeStruct((extent, width), BF),
        ],
        compiler_params=pltpu.CompilerParams(
            dimension_semantics=("arbitrary",), vmem_limit_bytes=52 * 1024 * 1024
        ),
        cost_estimate=pl.CostEstimate(
            flops=4 * extent * width * cols, bytes_accessed=6 * extent * width, transcendentals=0
        ),
        name="gate_up_both_ways",
    )(h2_low, d_hidden, w_gu)


def dot(left, right, dims=NN):
    return lax.dot_general(left, right, (dims, ((), ())), preferred_element_type=F32)


def after(value, *others):
    return lax.optimization_barrier((value,) + others)[0]


def swapped(value, axis, distance):
    count = lax.axis_size(axis)
    return lax.ppermute(value, axis, [(i, i ^ distance) for i in range(count)])


def row_major(value):
    return with_layout_constraint(value, Layout(major_to_minor=tuple(range(value.ndim))))


def placed(parts, order):
    whole = row_major(jnp.zeros((len(parts),) + parts[0].shape, parts[0].dtype))
    for part, place in zip(parts, order):
        whole = lax.dynamic_update_index_in_dim(whole, part, place, 0)
    return row_major(lax.optimization_barrier(whole))


def shards_of(shard, axis):
    count = lax.axis_size(axis)
    return [shard] + [swapped(shard, axis, distance) for distance in range(1, count)]


def placed_shards(parts, axis):
    place = lax.axis_index(axis)
    return placed(parts, [place ^ distance for distance in range(len(parts))])


def gather_start(shard, axis):
    if lax.axis_size(axis) != 4:
        return shards_of(shard, axis)[1:]
    half = shard.shape[0] // 2
    return [swapped(shard[:half], axis, 1), swapped(shard[half:], axis, 2)]


def gather_end(shard, moved, axis):
    count, place = lax.axis_size(axis), lax.axis_index(axis)
    if count != 4:
        return placed_shards([shard] + moved, axis)
    half = shard.shape[0] // 2
    tops = swapped(jnp.stack([shard[:half], moved[0]]), axis, 2)
    ends = swapped(jnp.stack([shard[half:], moved[1]]), axis, 1)
    parts = [shard[:half], shard[half:], moved[0], moved[1], tops[0], ends[0], tops[1], ends[1]]
    order = [(0, 0), (0, 1), (1, 0), (2, 1), (2, 0), (1, 1), (3, 0), (3, 1)]
    whole = placed(parts, [2 * (place ^ distance) + side for distance, side in order])
    return whole.reshape((count,) + shard.shape)


def reduce_parts(part_of, axis):
    count, place = lax.axis_size(axis), lax.axis_index(axis)
    parts = [part_of(place ^ distance) for distance in range(count)]
    if count != 4:
        return parts[1:], parts[:1]
    half = parts[0].shape[0] // 2
    sent = [
        jnp.stack([parts[1][:half], parts[3][:half]]), jnp.stack([parts[2][half:], parts[3][half:]])
    ]
    return sent, [parts[0], parts[2][:half], parts[1][half:]]


def reduce_start(sent, axis):
    if lax.axis_size(axis) != 4:
        return [swapped(part, axis, index + 1) for index, part in enumerate(sent)]
    return [swapped(sent[0], axis, 1), swapped(sent[1], axis, 2)]


def reduce_end(moved, kept, axis):
    if lax.axis_size(axis) != 4:
        return total_of(moved + kept)
    own, top, end = kept
    half = own.shape[0] // 2
    top = swapped((top.astype(F32) + moved[0][1].astype(F32)).astype(BF), axis, 2)
    end = swapped((end.astype(F32) + moved[1][1].astype(F32)).astype(BF), axis, 1)
    top = total_of([moved[0][0], top, own[:half]])
    end = total_of([moved[1][0], end, own[half:]])
    return jnp.concatenate([top, end], axis=0)


def shard_parts(part_of, axis):
    count, place = lax.axis_size(axis), lax.axis_index(axis)
    sent = [part_of(place ^ distance) for distance in range(1, count)]
    return sent + [part_of(place)]


def swapped_parts(parts, axis):
    return [swapped(part, axis, index + 1) for index, part in enumerate(parts[:-1])] + parts[-1:]


def total_of(parts):
    total = parts[-1].astype(F32)
    for part in parts[:-1]:
        total = total + part.astype(F32)
    return total


def head_routes(row_part, turn):
    dps, ctxs = lax.axis_size("dp"), lax.axis_size("ctx")
    blocks = HD // row_part
    heads = dps // blocks
    routes = []
    for dp in range(dps):
        for ctx in range(ctxs):
            place = (dp % heads) * blocks + ctx % blocks
            user = (ctx // blocks) * blocks + dp // heads
            routes.append((dp * ctxs + ctx, (place ^ turn) * ctxs + user))
    return routes


def head_owner_parts(rows):
    turns = range(lax.axis_size("dp"))
    return [lax.ppermute(rows, ("dp", "ctx"), head_routes(rows.shape[0], turn)) for turn in turns]


def row_owner_parts(blocks):
    place = lax.axis_index("dp")
    parts = []
    for turn in range(lax.axis_size("dp")):
        routes = [(user, owner) for owner, user in head_routes(blocks.shape[1], turn)]
        block = lax.dynamic_index_in_dim(blocks, place ^ turn, 0, False)
        parts.append(lax.ppermute(block, ("dp", "ctx"), routes))
    return parts


def spread(value, axis):
    return lax.all_to_all(value, axis, 0, 0, tiled=True)


def rms_scale(values):
    return lax.rsqrt(jnp.mean(values * values, axis=-1, keepdims=True) + EPS)


def norm_pull(values, scale, gain, grad):
    weighted = grad * gain
    return scale * weighted - values * (
        scale * scale * scale * jnp.mean(weighted * values, axis=-1, keepdims=True)
    )


def per_device(
    tokens,
    cotangent,
    group_ids,
    group_scale,
    attn_gain,
    w_qkv,
    conv_weight,
    w_beta,
    w_gate_o,
    norm_gain_o,
    w_out,
    ffn_gain,
    w_gate_up,
    w_down,
):
    seg_len, width = tokens.shape[1:]
    dps, ctxs = lax.axis_size("dp"), lax.axis_size("ctx")
    devices = dps * ctxs
    ctx_place = lax.axis_index("ctx")
    head_count = w_beta.shape[1]
    heads = head_count // ctxs
    mix_width = heads * HD
    row_part = w_qkv.shape[0]
    dp_rows = ctxs * row_part
    ff_part = w_down.shape[0]
    ff_local = dps * ff_part
    taps_part = conv_weight.shape[1]
    taps_cols = CONV * taps_part // row_part
    gain_part = norm_gain_o.shape[0]
    head_dims = (HD // row_part, heads, ctxs * row_part // HD)

    x_full = lax.all_gather(tokens[0], "ctx", axis=0, tiled=True)
    first_rows, second_rows = pack_mix(
        w_qkv, w_gate_o, w_beta, attn_gain, ffn_gain, norm_gain_o, conv_weight, ctxs
    )
    matches = group_ids[:, None] == lax.broadcasted_iota(
        jnp.int32, (group_ids.shape[0], group_scale.shape[0]), 1
    )
    seq_scale = jnp.sum(jnp.where(matches, group_scale[None, :], 0.0), axis=1)
    d_out = after(cotangent[0], first_rows).astype(F32) * seq_scale[0]
    d_out_full = lax.all_gather(after(d_out.astype(BF), x_full), "ctx", axis=0, tiled=True)
    first_half = spread(first_rows, "ctx").reshape(dp_rows, first_rows.shape[2])
    down_parts = shards_of(w_down, "dp")
    out_parts = head_owner_parts(after(w_out, *down_parts[1:3]))
    first_half, *down_parts = lax.optimization_barrier((first_half, *down_parts))
    second_half = spread(after(second_rows, first_half), "ctx").reshape(dp_rows, 2 * mix_width)
    first_parts = shards_of(first_half, "dp")
    second_half, *parts = lax.optimization_barrier((second_half, *first_parts[1:3], *out_parts))
    first_parts[1:3], out_parts = parts[:2], parts[2:]
    second_parts = shards_of(second_half, "dp")
    gate_up_rows = pack_ff(w_gate_up, ctxs, dps)
    gate_up_half = spread(after(gate_up_rows, second_half), "ctx").reshape(dp_rows, 2 * ff_local)

    x_rows = x_full.astype(F32)
    x_scale = rms_scale(x_rows)
    w_out_own = placed_shards(out_parts, "dp").reshape(mix_width, width)
    x_scale, w_out_own, *first_parts = lax.optimization_barrier(
        (x_scale, w_out_own, *first_parts)
    )
    w_first = placed_shards(first_parts, "dp").reshape(width, first_rows.shape[2])
    w_small = lax.optimization_barrier(w_first[:, 2 * mix_width :])
    attn_full, ffn_full, norm_o_full, taps = read_small(
        w_small, row_part, taps_part, gain_part, mix_width
    )

    h1_low = (x_rows * x_scale * attn_full).astype(BF)
    first = dot(h1_low, w_first)
    first, taps, *second_parts = lax.optimization_barrier((first, taps, *second_parts))
    w_second = placed_shards(second_parts, "dp").reshape(width, 2 * mix_width)
    second = dot(h1_low, w_second)
    y_local, core, states, inverses = mix_forward(first, second, taps, norm_o_full)
    y_local, d_out_full, gate_up_half = lax.optimization_barrier(
        (y_local, d_out_full, gate_up_half)
    )
    gate_up_moved = gather_start(gate_up_half, "dp")
    w_dn = placed_shards(down_parts, "dp").reshape(ff_local, width)
    attn_part = dot(y_local, w_out_own).astype(BF)
    attn_sum = lax.psum_scatter(attn_part, "ctx", scatter_dimension=0, tiled=True)

    x_own = tokens[0].astype(F32)
    w_mix = jnp.concatenate([w_first[:, : 2 * mix_width], w_second, w_small], axis=1)
    attn_sum, gate_up_moved, w_dn, w_mix = lax.optimization_barrier(
        (attn_sum, gate_up_moved, w_dn, w_mix)
    )
    resid = x_own + attn_sum.astype(F32)
    resid_scale = rms_scale(resid)
    h2_own = (resid * resid_scale * ffn_full).astype(BF)
    h2_low = lax.all_gather(h2_own, "ctx", axis=0, tiled=True)

    w_gu = gather_end(gate_up_half, gate_up_moved, "dp").reshape(width, 2 * ff_local)
    d_hidden = dot(d_out_full, w_dn, NT).astype(BF)
    h2_low, d_hidden = lax.optimization_barrier((h2_low, d_hidden))
    hidden_low, d_gate_up, d_h2_part = gate_up_both_ways(h2_low, d_hidden, w_gu)
    d_h2 = lax.psum_scatter(d_h2_part, "ctx", scatter_dimension=0, tiled=True)
    hidden_later, d_gate_up_later = lax.optimization_barrier((hidden_low, d_gate_up, d_h2_part))[:2]
    out_part = dot(hidden_later, w_dn).astype(BF)

    def down_part(place):
        hidden_cols = lax.dynamic_slice_in_dim(hidden_later, place * ff_part, ff_part, 1)
        return dot(hidden_cols, d_out_full, TN).astype(BF)

    def gate_up_part(place):
        h2_cols = lax.dynamic_slice_in_dim(h2_low, place * dp_rows, dp_rows, 1)
        return dot(h2_cols, d_gate_up_later, TN).astype(BF)

    g_gate_up_sent, g_gate_up_kept = reduce_parts(gate_up_part, "dp")
    g_down_parts = shard_parts(down_part, "dp")
    g_gate_up_moved = reduce_start(g_gate_up_sent, "dp")
    d_h2, g_gate_up_moved = lax.optimization_barrier((d_h2, g_gate_up_moved))

    d_resid = d_out + norm_pull(resid, resid_scale, ffn_full, d_h2.astype(F32))
    d_attn = lax.all_gather(d_resid.astype(BF), "ctx", axis=0, tiled=True)
    g_gate_up = reduce_end(g_gate_up_moved, g_gate_up_kept, "dp").astype(BF)
    g_down_moved = swapped_parts(g_down_parts, "dp")
    d_attn, g_gate_up, out_part, *g_down_moved[:2] = lax.optimization_barrier(
        (d_attn, g_gate_up, out_part, *g_down_moved[:2])
    )
    out_sum = lax.psum_scatter(after(out_part, d_attn), "ctx", scatter_dimension=0, tiled=True)
    d_y = dot(d_attn, w_out_own, NT).astype(BF)
    g_gate_up = spread(g_gate_up.reshape(ctxs, row_part, 2 * ff_local), "ctx")

    d_proj, d_beta, g_taps, g_gain_o = mix_backward(
        first, second, d_y, core, states, inverses, taps, norm_o_full
    )

    def mix_part(place):
        h1_cols = lax.dynamic_slice_in_dim(h1_low, place * dp_rows, dp_rows, 1)
        return dot(h1_cols, d_proj, TN).astype(BF)

    g_mix_sent, g_mix_kept = reduce_parts(mix_part, "dp")
    d_proj_later, g_mix_sent, d_beta, g_taps, g_gain_o, d_attn_later = lax.optimization_barrier(
        (d_proj, g_mix_sent, d_beta, g_taps, g_gain_o, d_attn)
    )
    g_mix_moved = reduce_start(g_mix_sent, "dp")
    d_beta_low = jnp.pad(d_beta.astype(BF), ((0, 0), (0, 128 - heads)))
    d_h1_part = dot(jnp.concatenate([d_proj_later, d_beta_low], axis=1), w_mix, NT).astype(BF)
    taps_grad = jnp.zeros((ctxs, CONV, 3 * mix_width), F32)
    taps_grad = lax.dynamic_update_index_in_dim(taps_grad, g_taps[:CONV], ctx_place, 0)
    taps_grad = (
        taps_grad.reshape(head_dims[2], head_dims[0], CONV, 3, heads, HD)
        .transpose(2, 3, 1, 4, 0, 5)
        .reshape(CONV, devices, taps_part)
        .transpose(1, 0, 2)
        .reshape(width, taps_cols)
    )
    gain_grad = jnp.pad(g_gain_o[0].reshape(devices, gain_part), ((0, 0), (0, row_part - gain_part)))
    small_grad = jnp.concatenate(
        [jnp.zeros((width, heads), F32), gain_grad.reshape(width, 1), taps_grad], axis=1
    )
    small_grad = jnp.pad(small_grad, ((0, 0), (0, 128 - small_grad.shape[1])))
    small_grad = (small_grad + dot(h1_low, d_beta_low, TN)).astype(BF)
    small_grad = small_grad.reshape(dps, dp_rows, 128)

    g_out = dot(y_local, d_attn_later, TN).astype(BF)
    g_out_parts = row_owner_parts(g_out.reshape(dps, row_part, width))
    d_h1_part, out_sum, g_gate_up, g_mix_moved, *g_out_parts = lax.optimization_barrier(
        (d_h1_part, out_sum, g_gate_up, g_mix_moved, *g_out_parts)
    )
    block_out = (resid + out_sum.astype(F32)).astype(BF)[None]
    d_h1 = lax.psum_scatter(d_h1_part, "ctx", scatter_dimension=0, tiled=True).astype(F32)
    d_tokens = (d_resid + norm_pull(x_own, rms_scale(x_own), attn_full, d_h1))[None]

    def small_part(place):
        return lax.dynamic_index_in_dim(small_grad, place, 0, False)

    g_small = total_of(swapped_parts(shard_parts(small_part, "dp"), "dp")).astype(BF)
    g_mix = reduce_end(g_mix_moved, g_mix_kept, "dp").astype(BF)
    g_mix = jnp.concatenate([g_mix, g_small], axis=1)
    g_w_out = total_of(g_out_parts)
    g_w_down = total_of(g_down_moved)

    g_w_gate_up, ffn_sum = unpack_ff(g_gate_up, w_gate_up, dps)
    g_ffn_gain = ffn_sum[:, 0] / ffn_gain.astype(F32)
    g_mix = spread(g_mix.reshape(ctxs, row_part, g_mix.shape[1]), "ctx")
    g_mix, d_tokens, g_w_gate_up, g_w_down, g_w_out = lax.optimization_barrier(
        (g_mix, d_tokens, g_w_gate_up, g_w_down, g_w_out)
    )
    g_w_qkv, g_w_gate_o, g_w_beta, small_sum, attn_row_sum = unpack_mix(
        g_mix, w_qkv, w_gate_o, w_beta
    )
    g_attn_gain = attn_row_sum[:, 0] / attn_gain.astype(F32)
    g_norm_gain_o = small_sum[:gain_part, heads]
    g_conv = small_sum[:, heads + 1 : heads + 1 + taps_cols].reshape(CONV, taps_part)
    return (
        block_out,
        d_tokens,
        g_attn_gain,
        g_w_qkv,
        g_conv,
        g_w_beta,
        g_w_gate_o,
        g_norm_gain_o,
        g_w_out,
        g_ffn_gain,
        g_w_gate_up,
        g_w_down,
    )


def solution(mesh):
    rows = P(("dp", "ctx"), None)
    flat = P(("dp", "ctx"))
    taps = P(None, ("dp", "ctx"))
    acts = P("dp", "ctx", None)
    return jax.shard_map(
        per_device,
        mesh=mesh,
        in_specs=(
            acts, acts, P("dp"), P(), flat, rows, taps, rows, rows, flat, rows, flat, rows, rows
        ),
        out_specs=(acts, acts, flat, rows, taps, rows, rows, flat, rows, flat, rows, rows),
        check_vma=False,
    )
```
